768 devices in a mesh: row: 24 (over z_lo, y), col: 32 (over x, z_hi, core).
Axes of the slice: x: 4, y: 8, z: 12 (z_hi: 4, z_lo: 3; z = z_hi * 3 + z_lo), core: 2. Of those that a mesh axis runs over, the one named last changes fastest.
Arguments:
- features: bfloat16 [98304, 256], P(('row', 'col')), may hold values from -6 to 6
- weight: bfloat16 [256, 256], replicated, may hold values from -0.375 to 0.375
- tiles: bfloat16 [9216, 128, 128], P(('row', 'col')), may hold values from 0 to 0.0099487305
- tile_pos: int32 [9216], P(('row', 'col')), may hold values from -1 to 767, as said below
- edge_keep: int32 [2, 9216], P(None, ('row', 'col')), may hold values 0 or 1
- feature_keep: int32 [2, 256], replicated, may hold values 0 or 1
- negatives: int32 [98304, 1024], P(('row', 'col')), may hold values from 0 to 3071, as said below
Outputs:
- node_loss: float32 [98304], P(('row', 'col'))
- weight_grad: float32 [256, 256], replicated
The draws below stay inside these ranges and needn't reach their ends.
Inputs may be any that keep to these rules, and one draw needn't show every extreme that they name: `tile_pos`: on each device the first count slots hold distinct positions and the rest are -1; every device has at least one tile, at least one device has all 12 slots filled. `negatives`: indices into the node's column group, each node's list in ascending order; an index may repeat within a node's list.
All inputs are finite; a program needn't handle non-finite values. No bound on the sum of `edge_keep` on one device may be relied on, other than what follows from the above.
Results may differ from the reference program's by a relative error of at most 0.0035.
Values may be sent and summed in bfloat16 or wider, within the bound.
No kernel may reach another device: no remote copies, remote signals or barrier semaphores. Data moves between devices by JAX's collectives and lax.ppermute only.
A program may use at most 64 MiB of HBM per device.

```python
import jax
import jax.numpy as jnp
from jax import lax

FEAT = 256
NODE_DEV = 128
NEG = 1024
TR = 24
TC = 32
KT = 12
GROUP = 3072
NODES = 98304
N_ROW = 24
N_COL = 32


def draw_tile_pos(key, part):
    key = jax.random.fold_in(key, 11)
    devcount = N_ROW * N_COL
    first, second, third, fourth = jax.random.split(key, 4)
    upper = jax.random.randint(first, (devcount,), 1, KT + 1)
    lower = jax.random.randint(second, (devcount,), 1, KT + 1)
    filled = jnp.maximum(1, upper * lower // KT)
    busiest = jax.random.randint(third, (), 0, devcount)
    filled = jnp.where(jnp.arange(devcount) == busiest, KT, filled)
    orders = jax.vmap(lambda k: jax.random.permutation(k, TR * TC))(jax.random.split(fourth, devcount))[:, :KT]
    slots = jnp.arange(KT)
    chosen = jnp.where(slots[None, :] < filled[:, None], orders, -1)
    return chosen.reshape(-1).astype(jnp.int32)


def draw_negatives(key, part):
    key = jax.random.fold_in(key, 23)
    span = min(16, NODE_DEV)
    hot_count = NEG * 3 // 4
    cold_count = NEG - hot_count
    first, second, third, fourth, fifth = jax.random.split(key, 5)
    node = jnp.arange(NODES)
    own_block = node // NODE_DEV // N_COL
    side = jax.random.randint(first, (NODES,), 0, 2)
    other = (own_block + jax.random.randint(second, (NODES,), 1, max(N_ROW, 2))) % N_ROW
    block = jnp.where(side == 1, own_block, other)
    start = block * NODE_DEV + jax.random.randint(third, (NODES,), 0, NODE_DEV - span + 1)
    hot = start[:, None] + jax.random.randint(fourth, (NODES, hot_count), 0, span)
    cold = jax.random.randint(fifth, (NODES, cold_count), 0, GROUP)
    merged = jnp.concatenate([hot, cold], axis=1)
    return jnp.sort(merged, axis=1).astype(jnp.int32)


def touch_ends(array, stream_key, low, high):
    shape = array.shape
    index_at = [jax.random.randint(jax.random.fold_in(stream_key, axis), (), 0, shape[axis]) for axis in range(len(shape))]
    array = array.at[tuple(index_at)].set(low)
    longest = shape.index(max(shape))
    index_at[longest] = (index_at[longest] + 1) % shape[longest]
    return array.at[tuple(index_at)].set(high)


def levels(own_key, extent, cuts, least, largest):
    def one(axis_at, parts):
        heights = jax.random.uniform(jax.random.fold_in(jax.random.fold_in(own_key, 6), axis_at), (parts,), jnp.float32, least / len(cuts), largest / len(cuts))
        return jnp.repeat(jnp.exp(heights), extent[axis_at] // parts).reshape((-1,) + (1,) * (len(extent) - axis_at - 1))

    factor_of = one(*cuts[0])
    for cut in cuts[1:]:
        factor_of = factor_of * one(*cut)
    return factor_of


def gaussian(stream_key, dims, deviation, most, shards=(), held_as=jnp.bfloat16):
    factor_of = levels(stream_key, dims, shards, -0.22, 0.18) if shards else 1.0
    result = jax.random.normal(stream_key, dims, jnp.float32) * deviation * factor_of
    return jnp.minimum(jnp.maximum(result, -most), most).astype(held_as)


def setup_inputs(seed: int = 0) -> dict:
    streams_of = jax.random.split(jax.random.key(seed), 8)
    return {
        "features": gaussian(streams_of[0], (NODES, FEAT), 1.0, 6.0, ((0, 768),)),
        "weight": gaussian(streams_of[1], (FEAT, FEAT), FEAT ** -0.5, 0.375),
        "tiles": jnp.clip(0.0099487305 * jax.random.uniform(streams_of[2], (N_ROW * N_COL * KT, 128, 128), jnp.float32) ** levels(streams_of[2], (N_ROW * N_COL * KT, 128, 128), ((0, 768),), -0.2, 0.2), 0.0, 0.0099487305).astype(jnp.bfloat16),
        "tile_pos": draw_tile_pos(jax.random.fold_in(streams_of[7], 71), 0),
        "edge_keep": touch_ends((jax.random.randint(streams_of[4], (2, N_ROW * N_COL * KT), 0, 10) < 7).astype(jnp.int32), jax.random.fold_in(streams_of[4], 1), 0, 1),
        "feature_keep": touch_ends((jax.random.randint(streams_of[5], (2, FEAT), 0, 10) < 7).astype(jnp.int32), jax.random.fold_in(streams_of[5], 1), 0, 1),
        "negatives": draw_negatives(jax.random.fold_in(streams_of[7], 71), 0),
    }


tau = 0.5
eps = 1e-06

def reference(features, weight, tiles, tile_pos, edge_keep, feature_keep, negatives):
    xrows = features.reshape(N_ROW, TC, 128, FEAT)
    tiles_grid = tiles.reshape(N_ROW, N_COL, KT, 128, 128)
    pos_grid = tile_pos.reshape(N_ROW, N_COL, KT)
    keep_grid = edge_keep.astype(jnp.float32).reshape(2, N_ROW, N_COL, KT)
    fkeep = feature_keep.astype(jnp.float32)

    def group_agg(colidx):

        def add_device(total, rowidx):
            xr = xrows[rowidx]
            pos = pos_grid[rowidx, colidx]
            valid = (pos >= 0).astype(jnp.float32)
            clamped = jnp.maximum(pos, 0)
            trow = clamped // TC
            tcol = clamped % TC
            xt = xr[tcol].astype(jnp.float32)
            prod = jnp.einsum('kab,kbf->kaf', tiles_grid[rowidx, colidx].astype(jnp.float32), xt, precision=lax.Precision.HIGHEST)
            wts = keep_grid[:, rowidx, colidx] * valid[None, :]
            onehot = (trow[None, :] == jnp.arange(TR)[:, None]).astype(jnp.float32)
            term = jnp.einsum('vk,tk,kaf->vtaf', wts, onehot, prod, precision=lax.Precision.HIGHEST)
            rounded = lax.optimization_barrier(term.astype(jnp.bfloat16)).astype(jnp.float32)
            return (total + rounded, None)
        total = lax.scan(add_device, jnp.zeros((2, TR, 128, FEAT), jnp.float32), jnp.arange(N_ROW))[0]
        return total.reshape(2, GROUP, FEAT) * fkeep[:, None, :]
    agg = lax.map(group_agg, jnp.arange(N_COL))
    agg_b = agg.astype(jnp.bfloat16)
    neg_groups = negatives.reshape(N_ROW, N_COL, NODE_DEV, NEG).transpose(1, 0, 2, 3).reshape(N_COL, GROUP, NEG)
    coef = 1.0 / (2.0 * tau * jnp.sqrt(jnp.float32(NODES)))

    def group_loss(items):
        pb, negs = items
        z = jnp.einsum('vnf,fg->vng', pb.astype(jnp.float32), weight.astype(jnp.float32), precision=lax.Precision.HIGHEST)
        rinv = lax.rsqrt(lax.optimization_barrier(jnp.sum(z * z, -1, keepdims=True)) + eps)
        emb = z * rinv
        emb_b = emb.astype(jnp.bfloat16)
        hb1, hb2 = (emb_b[0], emb_b[1])
        h1f, h2f = (hb1.astype(jnp.float32), hb2.astype(jnp.float32))
        counts = jnp.zeros((GROUP, GROUP), jnp.float32).at[jnp.arange(GROUP)[:, None], negs].add(1.0)
        pos = lax.optimization_barrier(jnp.sum(h1f * h2f, -1)) / tau
        s12 = jnp.dot(hb1, hb2.T, preferred_element_type=jnp.float32) / tau
        s21 = jnp.dot(hb2, hb1.T, preferred_element_type=jnp.float32) / tau
        e12 = counts * jnp.exp(s12)
        e21 = counts * jnp.exp(s21)
        tot1 = jnp.exp(pos) + lax.optimization_barrier(jnp.sum(e12, 1))
        tot2 = jnp.exp(pos) + lax.optimization_barrier(jnp.sum(e21, 1))
        loss = 0.5 * (jnp.log(tot1) - pos + (jnp.log(tot2) - pos))
        p1 = jnp.exp(pos) / tot1
        p2 = jnp.exp(pos) / tot2
        q1 = (e12 / tot1[:, None]).astype(jnp.bfloat16)
        q2 = (e21 / tot2[:, None]).astype(jnp.bfloat16)
        both = (p1 + p2 - 2.0)[:, None]
        d1 = coef * (both * h2f + jnp.dot(q1, hb2, preferred_element_type=jnp.float32) + jnp.dot(q2.T, hb2, preferred_element_type=jnp.float32))
        d2 = coef * (both * h1f + jnp.dot(q2, hb1, preferred_element_type=jnp.float32) + jnp.dot(q1.T, hb1, preferred_element_type=jnp.float32))
        dh = jnp.stack([d1, d2])
        dz = (dh - emb * lax.optimization_barrier(jnp.sum(emb * dh, -1, keepdims=True))) * rinv
        grad = jnp.einsum('vnf,vng->fg', pb.astype(jnp.float32), dz, precision=lax.Precision.HIGHEST)
        return (loss, grad)
    losses, grads = lax.map(group_loss, (agg_b, neg_groups))
    node_loss = losses.reshape(N_COL, N_ROW, NODE_DEV).transpose(1, 0, 2).reshape(NODES)
    return (node_loss, lax.optimization_barrier(jnp.sum(grads, 0)))
```

```python
import functools

import jax
import jax.numpy as jnp
from jax import lax
from jax.experimental import pallas as pl
from jax.experimental.pallas import tpu as pltpu
from jax.sharding import Mesh
from jax.sharding import PartitionSpec as P

tau = 0.5
eps = 1e-06
T = 128
ZL = 3
FS = 96
f32 = jnp.float32
bf16 = jnp.bfloat16
NT = (((1,), (1,)), ((), ()))
NN = (((1,), (0,)), ((), ()))
ROW = ("zl", "y")
COL = ("x", "zh", "core")
PARAMS = dict(vmem_limit_bytes=48 * 1024 * 1024)


def dot(a, b, dims):
    return lax.dot_general(a, b, dims, preferred_element_type=f32)


def counts_kernel(blocks, neg_ref, out_ref, acc_ref):
    nodes, negs = neg_ref.shape
    rows = 8 * ((blocks + 7) // 8)
    low_iota = lax.broadcasted_iota(jnp.int32, (T, negs), 0)
    high_iota = lax.broadcasted_iota(jnp.int32, (rows, negs), 0)

    def step(i, carry):
        base = pl.multiple_of(i * 8, 8)
        index = neg_ref[pl.ds(base, 8), :]
        low = index & (T - 1)
        high = index >> 7
        for j in range(8):
            low_hot = jnp.where(low[j : j + 1, :] == low_iota, 1.0, 0.0).astype(bf16)
            high_hot = jnp.where(high[j : j + 1, :] == high_iota, 1.0, 0.0).astype(bf16)
            found = dot(high_hot, low_hot, NT)
            acc_ref[pl.ds(base + j, rows, stride=nodes), :] = found
        return carry

    lax.fori_loop(0, nodes // 8, step, 0)

    def turn(h, carry):
        block = acc_ref[pl.ds(pl.multiple_of(h * nodes, nodes), nodes), :]
        out_ref[h] = block.T.astype(jnp.int32).astype(jnp.int16)
        return carry

    lax.fori_loop(0, blocks, turn, 0)


def count_negatives(negatives, blocks):
    nodes = negatives.shape[0]
    rows = 8 * ((blocks + 7) // 8)
    return pl.pallas_call(
        functools.partial(counts_kernel, blocks),
        out_shape=jax.ShapeDtypeStruct((blocks, T, nodes), jnp.int16),
        scratch_shapes=[pltpu.VMEM((rows * nodes, T), f32)],
        compiler_params=pltpu.CompilerParams(**PARAMS),
        cost_estimate=pl.CostEstimate(
            flops=2 * 16 * nodes * T * T * 64, bytes_accessed=2 << 20, transcendentals=0
        ),
        name="counts",
    )(negatives)


def tiles_kernel(cols, ysize, meta_ref, core_ref, own_ref, other_ref, *refs):
    tile_refs, (out_ref, acc_ref) = refs[:ZL], refs[ZL:]
    acc_ref[...] = jnp.zeros_like(acc_ref)
    core = core_ref[0]
    for s in range(ZL):

        def slot(k, carry, s=s):
            place = meta_ref[s, 0, k]

            @pl.when(place >= 0)
            def _():
                tcol = lax.rem(place, cols)
                trow = lax.div(place, cols)
                at = lax.div(tcol, 2)
                mine = lax.rem(tcol, 2) == core
                rows = jnp.where(mine, own_ref[at, s], other_ref[at, s])
                product = dot(rows, tile_refs[s][k], NT)
                yy, zz = lax.rem(trow, ysize), lax.div(trow, ysize)
                for v in range(2):
                    kept = meta_ref[s, 1 + v, k].astype(f32)
                    acc_ref[yy, zz, v] += kept * product

            return carry

        lax.fori_loop(0, tile_refs[s].shape[0], slot, 0)
    out_ref[...] = acc_ref[...].astype(bf16)


def tile_sums(meta, core, own, other, tiles, cols, ysize):
    shape = (ysize, ZL, 2, FS, T)
    return pl.pallas_call(
        functools.partial(tiles_kernel, cols, ysize),
        out_shape=jax.ShapeDtypeStruct(shape, bf16),
        in_specs=[pl.BlockSpec(memory_space=pltpu.SMEM)] * 2
        + [pl.BlockSpec(memory_space=pltpu.VMEM)] * (2 + ZL),
        scratch_shapes=[pltpu.VMEM(shape, f32)],
        compiler_params=pltpu.CompilerParams(**PARAMS),
        name="tile_sums",
    )(meta, core, own, other, *tiles)


def anchors_of(n_ref, v):
    return jnp.concatenate(
        [jnp.concatenate([n_ref[s, z, v] for s in range(ZL)], 0) for z in range(ZL)], 1
    )


def embed(weight_t, agg):
    z = dot(weight_t, agg, NN)
    rinv = lax.rsqrt(jnp.sum(z * z, 0, keepdims=True) + eps)
    return z * rinv, rinv


def scores_kernel(n_ref, a_ref, w_ref, c_ref, tot_ref, e_ref):
    weight_t = w_ref[...]
    width = a_ref.shape[2]
    anchors = [embed(weight_t, anchors_of(n_ref, v))[0].astype(bf16) for v in range(2)]
    tot_ref[...] = jnp.zeros_like(tot_ref)

    def member(y, carry):
        base = pl.multiple_of(y * T, T)
        count = jnp.concatenate(
            [c_ref[z, y].astype(jnp.int32).astype(f32) for z in range(ZL)], 1
        )
        for v in range(2):
            emb = embed(weight_t[:, :width], a_ref[y, 1 - v])[0]
            score = dot(emb.T.astype(bf16), anchors[v], NN)
            term = count * jnp.exp(score * (1.0 / tau))
            e_ref[v, pl.ds(base, T), :] = term
            tot_ref[v : v + 1, :] += jnp.sum(term, 0, keepdims=True)
        return carry

    lax.fori_loop(0, a_ref.shape[0], member, 0)


def split_dot(agg, dz):
    high = dz.astype(bf16)
    low = (dz - high.astype(f32)).astype(bf16)
    return dot(agg, high, NT) + dot(agg, low, NT)


def grads_kernel(coef, n_ref, a_ref, w_ref, e_ref, tot_ref, mask_ref, loss_ref, grad_ref):
    weight_t = w_ref[...]
    ysize, _, width, _ = a_ref.shape
    agg_n = [anchors_of(n_ref, v) for v in range(2)]
    emb_n, rinv_n = zip(*[embed(weight_t, agg) for agg in agg_n])
    low_n = [emb.astype(bf16) for emb in emb_n]
    full_n = [emb.astype(f32) for emb in low_n]
    pos = jnp.sum(full_n[0] * full_n[1], 0, keepdims=True) * (1.0 / tau)
    own = jnp.exp(pos)
    tot = [own + sum(tot_ref[z, v : v + 1, :] for z in range(ZL)) for v in range(2)]
    loss = 0.5 * ((jnp.log(tot[0]) - pos) + (jnp.log(tot[1]) - pos))
    loss_ref[...] = jnp.broadcast_to(loss, loss_ref.shape)
    inverse = [1.0 / t for t in tot]
    both = (own * inverse[0] + own * inverse[1] - 2.0) * mask_ref[0:1, :]

    def back(emb, rinv, d):
        return (d - emb * jnp.sum(emb * d, 0, keepdims=True)) * rinv

    grad_ref[...] = jnp.zeros_like(grad_ref)

    def member(y, carry):
        base = pl.multiple_of(y * T, T)
        parts = [embed(weight_t[:, :width], a_ref[y, v]) for v in range(2)]
        low = [emb.astype(bf16) for emb, _ in parts]
        q = [(e_ref[v, pl.ds(base, T), :] * inverse[v]).astype(bf16) for v in range(2)]
        d_one = coef * dot(low_n[1], q[1], NT)
        d_two = coef * dot(low_n[0], q[0], NT)
        for v, d in ((0, d_one), (1, d_two)):
            dz = back(parts[v][0], parts[v][1], d)
            grad_ref[...] += split_dot(a_ref[y, v], dz)
        return carry[0] + dot(low[1], q[0], NN), carry[1] + dot(low[0], q[1], NN)

    sums = (jnp.zeros_like(pos) + jnp.zeros((weight_t.shape[0], 1), f32),) * 2
    sums = lax.fori_loop(0, ysize, member, sums)
    for v in range(2):
        d = coef * (both * full_n[1 - v] + sums[v])
        dz = back(emb_n[v], rinv_n[v], d)
        grad_ref[...] += split_dot(agg_n[v], dz)[:width]


def vmem_call(kernel, out_shape, name):
    return pl.pallas_call(
        kernel,
        out_shape=out_shape,
        compiler_params=pltpu.CompilerParams(**PARAMS),
        name=name,
    )


def swap(x, axis):
    return lax.all_to_all(x, axis, 0, 0, tiled=True)


def share(x, axis):
    return swap(jnp.broadcast_to(x[None], (lax.axis_size(axis),) + x.shape), axis)


def shift(x, axis, by):
    size = lax.axis_size(axis)
    return lax.ppermute(x, axis, [(i, (i + by) % size) for i in range(size)])


def reduce_all(grad):
    rows, width = grad.shape
    plane = ("y", "x", "core")
    size = lax.axis_size(plane)
    part = jnp.sum(swap(grad.reshape(size, -1, T), plane), 0)
    part = jnp.sum(share(part, ("zl", "zh")), 0)
    return share(part, plane).reshape(rows, width)


def shards(features, weight, tiles, tile_pos, edge_keep, feature_keep, negatives):
    nodes, width = features.shape
    ysize, xsize = lax.axis_size("y"), lax.axis_size("x")
    zsize = lax.axis_size("zh")
    cols = xsize * zsize * lax.axis_size("core")
    zl, core = lax.axis_index("zl"), lax.axis_index("core")
    total = lax.axis_size(ROW) * cols * nodes
    pad = ZL * FS - width

    meta = jnp.concatenate([tile_pos[None], edge_keep], 0)
    metas = jnp.stack([meta] + [shift(meta, "zl", s) for s in range(1, ZL)])
    all_tiles = [tiles] + [shift(tiles, "zl", s) for s in range(1, ZL)]

    turned = jnp.pad(features.T, ((0, pad), (0, 0))).reshape(ZL, FS, nodes)

    def slice_for(s):
        return lax.dynamic_index_in_dim(turned, lax.rem(zl + s, ZL), 0, keepdims=False)

    mine = jnp.stack([slice_for(0)] + [shift(slice_for(s), "zl", s) for s in range(1, ZL)])
    own = share(mine, ("x", "zh"))
    other = shift(own, "core", 1)

    counts = count_negatives(negatives, ZL * ysize)
    counts = swap(counts, "zl").reshape(ZL, ysize, nodes, nodes)

    part = tile_sums(metas, core.reshape(1), own, other, all_tiles, cols, ysize)
    got = swap(part, "y")
    keep = jnp.pad(feature_keep, ((0, 0), (0, pad))).reshape(2, ZL, FS)
    keep = lax.dynamic_index_in_dim(keep, zl, 1, keepdims=False).astype(f32)
    agg = (jnp.sum(got.astype(f32), 0) * keep[None, :, :, None]).astype(bf16)
    anchors = share(agg, "zl")
    one = lax.dynamic_index_in_dim(anchors, zl, 1, keepdims=False)
    one = one.transpose(1, 0, 2, 3).reshape(2, ZL * FS, nodes)[:, :width]
    members = share(one, "y")

    weight_t = jnp.pad(weight.T, ((0, 0), (0, pad)))
    group = ZL * nodes
    tot, terms = vmem_call(
        scores_kernel,
        (
            jax.ShapeDtypeStruct((8, group), f32),
            jax.ShapeDtypeStruct((2, ysize * nodes, group), f32),
        ),
        "scores",
    )(anchors, members, weight_t, counts)
    tots = share(tot, "zl")
    mask = (jnp.arange(group) // nodes == zl).astype(f32)
    coef = 1.0 / (2.0 * tau * float(total) ** 0.5)
    loss, grad = vmem_call(
        functools.partial(grads_kernel, coef),
        (
            jax.ShapeDtypeStruct((8, group), f32),
            jax.ShapeDtypeStruct((width, width), f32),
        ),
        "grads",
    )(anchors, members, weight_t, terms, tots, jnp.broadcast_to(mask, (8, group)))
    node_loss = lax.dynamic_slice_in_dim(loss[0], zl * nodes, nodes)
    return node_loss, reduce_all(grad)


def solution(mesh):
    rows, cols = mesh.devices.shape
    fine = Mesh(mesh.devices.reshape(ZL, rows // ZL, cols // 8, 4, 2), ROW + COL)
    every = ROW + COL
    in_specs = (
        P(every, None),
        P(),
        P(every, None, None),
        P(every),
        P(None, every),
        P(),
        P(every, None),
    )
    out_specs = (P(every), P())
    return jax.shard_map(shards, mesh=fine, in_specs=in_specs, out_specs=out_specs, check_vma=False)
```

```python
import functools

import jax
import jax.numpy as jnp
from jax import lax
from jax.experimental import pallas as pl
from jax.experimental.pallas import tpu as pltpu
from jax.sharding import Mesh
from jax.sharding import PartitionSpec as P

tau = 0.5
eps = 1e-06
T = 128
ZL = 3
FS = 96
f32 = jnp.float32
bf16 = jnp.bfloat16
NT = (((1,), (1,)), ((), ()))
NN = (((1,), (0,)), ((), ()))
ROW = ("zl", "y")
COL = ("x", "zh", "core")
PARAMS = dict(vmem_limit_bytes=48 * 1024 * 1024)


def dot(a, b, dims):
    return lax.dot_general(a, b, dims, preferred_element_type=f32)


def counts_kernel(blocks, neg_ref, out_ref, acc_ref):
    nodes, negs = neg_ref.shape
    rows = 8 * ((blocks + 7) // 8)
    low_iota = lax.broadcasted_iota(jnp.int32, (T, negs), 0)
    high_iota = lax.broadcasted_iota(jnp.int32, (rows, negs), 0)

    def step(i, carry):
        base = pl.multiple_of(i * 8, 8)
        index = neg_ref[pl.ds(base, 8), :]
        low = index & (T - 1)
        high = index >> 7
        for j in range(8):
            low_hot = jnp.where(low[j : j + 1, :] == low_iota, 1.0, 0.0).astype(bf16)
            high_hot = jnp.where(high[j : j + 1, :] == high_iota, 1.0, 0.0).astype(bf16)
            found = dot(high_hot, low_hot, NT)
            acc_ref[pl.ds(base + j, rows, stride=nodes), :] = found
        return carry

    lax.fori_loop(0, nodes // 8, step, 0)

    def turn(h, carry):
        block = acc_ref[pl.ds(pl.multiple_of(h * nodes, nodes), nodes), :]
        out_ref[h] = block.T.astype(jnp.int32).astype(jnp.int16)
        return carry

    lax.fori_loop(0, blocks, turn, 0)


def count_negatives(negatives, blocks):
    nodes = negatives.shape[0]
    rows = 8 * ((blocks + 7) // 8)
    return pl.pallas_call(
        functools.partial(counts_kernel, blocks),
        out_shape=jax.ShapeDtypeStruct((blocks, T, nodes), jnp.int16),
        scratch_shapes=[pltpu.VMEM((rows * nodes, T), f32)],
        compiler_params=pltpu.CompilerParams(**PARAMS),
        cost_estimate=pl.CostEstimate(
            flops=2 * 16 * nodes * T * T * 64, bytes_accessed=2 << 20, transcendentals=0
        ),
        name="counts",
    )(negatives)


def behind(zl, s):
    return lax.rem(zl + ZL - s, ZL)


def tiles_kernel(cols, ysize, meta_ref, place_ref, own_ref, other_ref, *refs):
    tile_refs, (out_ref, acc_ref) = refs[:ZL], refs[ZL:]
    zsize = own_ref.shape[1] // ZL
    acc_ref[...] = jnp.zeros_like(acc_ref)
    core, zl = place_ref[0], place_ref[1]
    for s in range(ZL):

        def slot(k, carry, s=s):
            trow, tcol = meta_ref[s, 0, k], meta_ref[s, 1, k]

            @pl.when(trow >= 0)
            def _():
                chip = lax.div(tcol, 2)
                at = lax.div(chip, zsize), behind(zl, s) * zsize + lax.rem(chip, zsize)
                mine = lax.rem(tcol, 2) == core
                rows = jnp.where(mine, own_ref[at], other_ref[at])
                product = dot(rows, tile_refs[s][pl.ds(pl.multiple_of(k * T, T), T), :], NT)
                yy, zz = lax.rem(trow, ysize), lax.div(trow, ysize)
                for v in range(2):
                    kept = meta_ref[s, 2 + v, k].astype(f32)
                    acc_ref[yy, zz, v] += kept * product

            return carry

        lax.fori_loop(0, meta_ref.shape[2], slot, 0)
    out_ref[...] = acc_ref[...].astype(bf16)


def tile_sums(meta, place, own, other, tiles, cols, ysize):
    shape = (ysize, ZL, 2, FS, T)
    return pl.pallas_call(
        functools.partial(tiles_kernel, cols, ysize),
        out_shape=jax.ShapeDtypeStruct(shape, bf16),
        in_specs=[pl.BlockSpec(memory_space=pltpu.SMEM)] * 2
        + [pl.BlockSpec(memory_space=pltpu.VMEM)] * (2 + ZL),
        scratch_shapes=[pltpu.VMEM(shape, f32)],
        compiler_params=pltpu.CompilerParams(**PARAMS),
        name="tile_sums",
    )(meta, place, own, other, *tiles)


def anchors_of(n_ref, zl, v):
    shares = [n_ref.at[behind(zl, s)] for s in range(ZL)]
    return jnp.concatenate(
        [jnp.concatenate([share[z, v] for share in shares], 0) for z in range(ZL)], 1
    )


def embed(weight_t, agg):
    z = dot(weight_t, agg, NN)
    rinv = lax.rsqrt(jnp.sum(z * z, 0, keepdims=True) + eps)
    return z * rinv, rinv


def scores_kernel(place_ref, n_ref, a_ref, w_ref, c_ref, tot_ref, e_ref):
    weight_t = w_ref[...]
    width = a_ref.shape[2]
    zl = place_ref[1]
    anchors = [embed(weight_t, anchors_of(n_ref, zl, v))[0].astype(bf16) for v in range(2)]
    tot_ref[...] = jnp.zeros_like(tot_ref)

    def member(y, carry):
        base = pl.multiple_of(y * T, T)
        count = jnp.concatenate(
            [c_ref[behind(zl, z), y].astype(jnp.int32).astype(f32) for z in range(ZL)], 1
        )
        for v in range(2):
            emb = embed(weight_t[:, :width], a_ref[y, 1 - v])[0]
            score = dot(emb.T.astype(bf16), anchors[v], NN)
            term = count * jnp.exp(score * (1.0 / tau))
            e_ref[v, pl.ds(base, T), :] = term
            tot_ref[v : v + 1, :] += jnp.sum(term, 0, keepdims=True)
        return carry

    lax.fori_loop(0, a_ref.shape[0], member, 0)


def split_dot(agg, dz):
    high = dz.astype(bf16)
    low = (dz - high.astype(f32)).astype(bf16)
    return dot(agg, high, NT) + dot(agg, low, NT)


def grads_kernel(coef, place_ref, n_ref, a_ref, w_ref, e_ref, tot_ref, mask_ref, loss_ref, grad_ref):
    weight_t = w_ref[...]
    ysize, _, width, _ = a_ref.shape
    agg_n = [anchors_of(n_ref, place_ref[1], v) for v in range(2)]
    emb_n, rinv_n = zip(*[embed(weight_t, agg) for agg in agg_n])
    low_n = [emb.astype(bf16) for emb in emb_n]
    full_n = [emb.astype(f32) for emb in low_n]
    pos = jnp.sum(full_n[0] * full_n[1], 0, keepdims=True) * (1.0 / tau)
    own = jnp.exp(pos)
    tot = [own + sum(tot_ref[z, v : v + 1, :] for z in range(ZL)) for v in range(2)]
    loss = 0.5 * ((jnp.log(tot[0]) - pos) + (jnp.log(tot[1]) - pos))
    loss_ref[...] = jnp.broadcast_to(loss, loss_ref.shape)
    inverse = [1.0 / t for t in tot]
    both = (own * inverse[0] + own * inverse[1] - 2.0) * mask_ref[0:1, :]

    def back(emb, rinv, d):
        return (d - emb * jnp.sum(emb * d, 0, keepdims=True)) * rinv

    grad_ref[...] = jnp.zeros_like(grad_ref)

    def member(y, carry):
        base = pl.multiple_of(y * T, T)
        parts = [embed(weight_t[:, :width], a_ref[y, v]) for v in range(2)]
        low = [emb.astype(bf16) for emb, _ in parts]
        q = [(e_ref[v, pl.ds(base, T), :] * inverse[v]).astype(bf16) for v in range(2)]
        d_one = coef * dot(low_n[1], q[1], NT)
        d_two = coef * dot(low_n[0], q[0], NT)
        for v, d in ((0, d_one), (1, d_two)):
            dz = back(parts[v][0], parts[v][1], d)
            grad_ref[...] += split_dot(a_ref[y, v], dz)
        return carry[0] + dot(low[1], q[0], NN), carry[1] + dot(low[0], q[1], NN)

    sums = (jnp.zeros_like(pos) + jnp.zeros((weight_t.shape[0], 1), f32),) * 2
    sums = lax.fori_loop(0, ysize, member, sums)
    for v in range(2):
        d = coef * (both * full_n[1 - v] + sums[v])
        dz = back(emb_n[v], rinv_n[v], d)
        grad_ref[...] += split_dot(agg_n[v], dz)[:width]


def vmem_call(kernel, out_shape, inputs, name):
    return pl.pallas_call(
        kernel,
        out_shape=out_shape,
        in_specs=[pl.BlockSpec(memory_space=pltpu.SMEM)]
        + [pl.BlockSpec(memory_space=pltpu.VMEM)] * (inputs - 1),
        compiler_params=pltpu.CompilerParams(**PARAMS),
        name=name,
    )


def swap(x, axis):
    return lax.all_to_all(x, axis, 0, 0, tiled=True)


def share(x, axis):
    return swap(jnp.broadcast_to(x[None], (lax.axis_size(axis),) + x.shape), axis)


def shift(x, axis, by):
    size = lax.axis_size(axis)
    return lax.ppermute(x, axis, [(i, (i + by) % size) for i in range(size)])


def around(x, pick):
    return [pick(x, 0)] + [shift(pick(x, s), "zl", s) for s in range(1, ZL)]


def reduce_all(grad):
    rows, width = grad.shape
    plane = ("y", "x")
    size = lax.axis_size(plane)
    part = jnp.sum(swap(grad.reshape(size, -1, T), plane), 0)
    part = jnp.sum(share(part, ("zl", "zh", "core")), 0)
    return share(part, plane).reshape(rows, width)


def packed(tiles, tile_pos, edge_keep, cols):
    slots = tile_pos.shape[0]
    held = tile_pos >= 0
    trow = jnp.where(held, tile_pos // cols, -1)
    tcol = jnp.where(held, tile_pos % cols, 0)
    meta = jnp.concatenate([trow[None], tcol[None], edge_keep], 0).astype(bf16)
    meta = jnp.pad(meta, ((0, 16 - meta.shape[0]), (0, T - slots)))
    return jnp.concatenate([tiles.reshape(slots * T, T), meta], 0)


def shards(features, weight, tiles, tile_pos, edge_keep, feature_keep, negatives):
    nodes, width = features.shape
    slots = tiles.shape[0]
    ysize, xsize = lax.axis_size("y"), lax.axis_size("x")
    zsize = lax.axis_size("zh")
    cols = xsize * zsize * lax.axis_size("core")
    zl, core = lax.axis_index("zl"), lax.axis_index("core")
    place = jnp.stack([core, zl])
    total = lax.axis_size(ROW) * cols * nodes
    pad = ZL * FS - width

    turned = jnp.pad(features.T, ((0, pad), (0, 0))).reshape(ZL, 1, FS, nodes)
    sent = jnp.broadcast_to(turned, (ZL, zsize, FS, nodes)).reshape(ZL * zsize, FS, nodes)
    near = swap(sent, ("zl", "zh"))
    counts = count_negatives(negatives, ZL * ysize)
    all_tiles = around(packed(tiles, tile_pos, edge_keep, cols), lambda x, s: x)
    near, counts, all_tiles = lax.optimization_barrier((near, counts, all_tiles))
    own = share(near, "x")
    other = shift(own, "core", 1)
    metas = jnp.stack([x[slots * T : slots * T + 4, :slots] for x in all_tiles]).astype(jnp.int32)

    part = tile_sums(metas, place, own, other, all_tiles, cols, ysize)
    part, counts = lax.optimization_barrier((part, counts))
    got = swap(part, "y")
    counts = counts.reshape(ZL, ysize, nodes, nodes)
    ahead = lambda x, s: lax.dynamic_index_in_dim(x, lax.rem(zl + s, ZL), 0, keepdims=False)
    counts = jnp.stack(around(counts, ahead))
    got, counts = lax.optimization_barrier((got, counts))
    keep = jnp.pad(feature_keep, ((0, 0), (0, pad))).reshape(2, ZL, FS)
    keep = lax.dynamic_index_in_dim(keep, zl, 1, keepdims=False).astype(f32)
    agg = (jnp.sum(got.astype(f32), 0) * keep[None, :, :, None]).astype(bf16)
    one = swap(agg, "zl")
    one, agg = lax.optimization_barrier((one, agg))
    one = one.transpose(1, 0, 2, 3).reshape(2, ZL * FS, nodes)[:, :width]
    members = share(one, "y")
    anchors = jnp.stack(around(agg, lambda x, s: x))

    weight_t = jnp.pad(weight.T, ((0, 0), (0, pad)))
    group = ZL * nodes
    tot, terms = vmem_call(
        scores_kernel,
        (
            jax.ShapeDtypeStruct((8, group), f32),
            jax.ShapeDtypeStruct((2, ysize * nodes, group), f32),
        ),
        5,
        "scores",
    )(place, anchors, members, weight_t, counts)
    tots = share(tot, "zl")
    mask = (jnp.arange(group) // nodes == zl).astype(f32)
    coef = 1.0 / (2.0 * tau * float(total) ** 0.5)
    loss, grad = vmem_call(
        functools.partial(grads_kernel, coef),
        (
            jax.ShapeDtypeStruct((8, group), f32),
            jax.ShapeDtypeStruct((width, width), f32),
        ),
        7,
        "grads",
    )(place, anchors, members, weight_t, terms, tots, jnp.broadcast_to(mask, (8, group)))
    node_loss = lax.dynamic_slice_in_dim(loss[0], zl * nodes, nodes)
    return node_loss, reduce_all(grad)


def solution(mesh):
    rows, cols = mesh.devices.shape
    fine = Mesh(mesh.devices.reshape(ZL, rows // ZL, cols // 8, 4, 2), ROW + COL)
    every = ROW + COL
    in_specs = (
        P(every, None),
        P(),
        P(every, None, None),
        P(every),
        P(None, every),
        P(),
        P(every, None),
    )
    out_specs = (P(every), P())
    return jax.shard_map(shards, mesh=fine, in_specs=in_specs, out_specs=out_specs, check_vma=False)
```

```python
import functools

import jax
import jax.numpy as jnp
from jax import lax
from jax.experimental import pallas as pl
from jax.experimental.pallas import tpu as pltpu
from jax.sharding import Mesh
from jax.sharding import PartitionSpec as P

tau = 0.5
eps = 1e-06
T = 128
ZL = 3
YL = 4
f32 = jnp.float32
bf16 = jnp.bfloat16
NT = (((1,), (1,)), ((), ()))
NN = (((1,), (0,)), ((), ()))
Y = ("yh", "yl")
ROW = ("zl",) + Y
COL = ("x", "zh", "core")
HBM = pl.BlockSpec(memory_space=pltpu.HBM)
PARAMS = dict(vmem_limit_bytes=24 * 1024 * 1024)


def dot(a, b, dims):
    return lax.dot_general(a, b, dims, preferred_element_type=f32)


def counts_kernel(blocks, neg_ref, out_ref, acc_ref):
    nodes, negs = neg_ref.shape
    rows = 8 * ((blocks + 7) // 8)
    low_iota = lax.broadcasted_iota(jnp.int32, (T, negs), 0)
    high_iota = lax.broadcasted_iota(jnp.int32, (rows, negs), 0)

    def step(i, carry):
        base = pl.multiple_of(i * 8, 8)
        index = neg_ref[pl.ds(base, 8), :]
        low = index & (T - 1)
        high = index >> 7
        for j in range(8):
            low_hot = jnp.where(low[j : j + 1, :] == low_iota, 1.0, 0.0).astype(bf16)
            high_hot = jnp.where(high[j : j + 1, :] == high_iota, 1.0, 0.0).astype(bf16)
            found = dot(high_hot, low_hot, NT)
            acc_ref[pl.ds(base + j, rows, stride=nodes), :] = found
        return carry

    lax.fori_loop(0, nodes // 8, step, 0)

    def turn(h, carry):
        block = acc_ref[pl.ds(pl.multiple_of(h * nodes, nodes), nodes), :]
        out_ref[h] = block.T.astype(jnp.int32).astype(jnp.int16)
        return carry

    lax.fori_loop(0, blocks, turn, 0)


def count_negatives(negatives, blocks):
    nodes = negatives.shape[0]
    rows = 8 * ((blocks + 7) // 8)
    return pl.pallas_call(
        functools.partial(counts_kernel, blocks),
        out_shape=jax.ShapeDtypeStruct((blocks, T, nodes), jnp.int16),
        scratch_shapes=[pltpu.VMEM((rows * nodes, T), f32)],
        compiler_params=pltpu.CompilerParams(**PARAMS),
        cost_estimate=pl.CostEstimate(
            flops=2 * 16 * nodes * T * T * 64, bytes_accessed=2 << 20, transcendentals=0
        ),
        name="counts",
    )(negatives)


def behind(place, s, size):
    return lax.rem(place + size - s, size)


def tiles_kernel(cols, meta_ref, place_ref, own_ref, other_ref, *refs):
    tile_refs, (out_ref, acc_ref) = refs[:YL], refs[YL:]
    zsize = own_ref.shape[1] // YL
    acc_ref[...] = jnp.zeros_like(acc_ref)
    core, yl = place_ref[0], place_ref[2]
    for s in range(YL):

        def slot(k, carry, s=s):
            trow, tcol = meta_ref[s, 0, k], meta_ref[s, 1, k]

            @pl.when(trow >= 0)
            def _():
                chip = lax.div(tcol, 2)
                at = lax.div(chip, zsize), behind(yl, s, YL) * zsize + lax.rem(chip, zsize)
                mine = lax.rem(tcol, 2) == core
                rows = jnp.where(mine, own_ref[at], other_ref[at])
                product = dot(rows, tile_refs[s][pl.ds(pl.multiple_of(k * T, T), T), :], NT)
                for v in range(2):
                    kept = meta_ref[s, 2 + v, k].astype(f32)
                    acc_ref[trow, v] += kept * product

            return carry

        lax.fori_loop(0, meta_ref.shape[2], slot, 0)
    out_ref[...] = acc_ref[...].astype(bf16)


def tile_sums(meta, place, own, other, tiles, cols, blocks):
    shape = (blocks, 2, own.shape[2], T)
    return pl.pallas_call(
        functools.partial(tiles_kernel, cols),
        out_shape=jax.ShapeDtypeStruct(shape, bf16),
        in_specs=[pl.BlockSpec(memory_space=pltpu.SMEM)] * 2
        + [pl.BlockSpec(memory_space=pltpu.VMEM)] * (2 + YL),
        scratch_shapes=[pltpu.VMEM(shape, f32)],
        compiler_params=pltpu.CompilerParams(**PARAMS),
        name="tile_sums",
    )(meta, place, own, other, *tiles)


def anchors_of(n_ref, zl, v):
    return jnp.concatenate([n_ref[behind(zl, z, ZL), v] for z in range(ZL)], 1)


def embed(weight_t, agg):
    z = dot(weight_t, agg, NN)
    rinv = lax.rsqrt(jnp.sum(z * z, 0, keepdims=True) + eps)
    return z * rinv, rinv


def scores_kernel(place_ref, n_ref, a_ref, w_ref, c_ref, tot_ref, e_ref, terms, sems):
    weight_t = w_ref[...]
    ysize = a_ref.shape[0]
    zl = place_ref[1]
    anchors = [embed(weight_t, anchors_of(n_ref, zl, v))[0].astype(bf16) for v in range(2)]
    tot_ref[...] = jnp.zeros_like(tot_ref)

    def keep(y):
        return pltpu.make_async_copy(terms.at[y], e_ref.at[y], sems.at[y])

    def member(y, carry):
        count = jnp.concatenate(
            [c_ref[behind(zl, z, ZL), y].astype(jnp.int32).astype(f32) for z in range(ZL)], 1
        )
        for v in range(2):
            emb = embed(weight_t, a_ref[y, 1 - v])[0]
            score = dot(emb.T.astype(bf16), anchors[v], NN)
            term = count * jnp.exp(score * (1.0 / tau))
            terms[y, v] = term
            tot_ref[v : v + 1, :] += jnp.sum(term, 0, keepdims=True)
        keep(y).start()
        return carry

    lax.fori_loop(0, ysize, member, 0)
    for y in range(ysize):
        keep(y).wait()


def split_dot(agg, dz):
    high = dz.astype(bf16)
    low = (dz - high.astype(f32)).astype(bf16)
    return dot(agg, high, NT) + dot(agg, low, NT)


def grads_kernel(coef, place_ref, n_ref, a_ref, w_ref, e_ref, tot_ref, mask_ref, loss_ref, grad_ref, terms, sems):
    weight_t = w_ref[...]
    ysize = a_ref.shape[0]

    def fetch(y):
        return pltpu.make_async_copy(e_ref.at[y], terms.at[y], sems.at[y])

    for y in range(ysize):
        fetch(y).start()
    agg_n = [anchors_of(n_ref, place_ref[1], v) for v in range(2)]
    emb_n, rinv_n = zip(*[embed(weight_t, agg) for agg in agg_n])
    low_n = [emb.astype(bf16) for emb in emb_n]
    full_n = [emb.astype(f32) for emb in low_n]
    pos = jnp.sum(full_n[0] * full_n[1], 0, keepdims=True) * (1.0 / tau)
    own = jnp.exp(pos)
    tot = [own + sum(tot_ref[z, v : v + 1, :] for z in range(ZL)) for v in range(2)]
    loss = 0.5 * ((jnp.log(tot[0]) - pos) + (jnp.log(tot[1]) - pos))
    loss_ref[...] = jnp.broadcast_to(loss, loss_ref.shape)
    inverse = [1.0 / t for t in tot]
    both = (own * inverse[0] + own * inverse[1] - 2.0) * mask_ref[0:1, :]

    def back(emb, rinv, d):
        return (d - emb * jnp.sum(emb * d, 0, keepdims=True)) * rinv

    grad_ref[...] = jnp.zeros_like(grad_ref)

    def member(y, carry):
        parts = [embed(weight_t, a_ref[y, v]) for v in range(2)]
        low = [emb.astype(bf16) for emb, _ in parts]
        fetch(y).wait()
        q = [(terms[y, v] * inverse[v]).astype(bf16) for v in range(2)]
        d_one = coef * dot(low_n[1], q[1], NT)
        d_two = coef * dot(low_n[0], q[0], NT)
        for v, d in ((0, d_one), (1, d_two)):
            dz = back(parts[v][0], parts[v][1], d)
            grad_ref[...] += split_dot(a_ref[y, v], dz)
        return carry[0] + dot(low[1], q[0], NN), carry[1] + dot(low[0], q[1], NN)

    sums = (jnp.zeros_like(pos) + jnp.zeros((weight_t.shape[0], 1), f32),) * 2
    sums = lax.fori_loop(0, ysize, member, sums)
    for v in range(2):
        d = coef * (both * full_n[1 - v] + sums[v])
        dz = back(emb_n[v], rinv_n[v], d)
        grad_ref[...] += split_dot(agg_n[v], dz)


def group_call(kernel, out_shape, in_specs, out_specs, terms, name):
    return pl.pallas_call(
        kernel,
        out_shape=out_shape,
        in_specs=in_specs,
        out_specs=out_specs,
        scratch_shapes=[pltpu.VMEM(terms, f32), pltpu.SemaphoreType.DMA((terms[0],))],
        compiler_params=pltpu.CompilerParams(**PARAMS),
        name=name,
    )


def swap(x, axis):
    return lax.all_to_all(x, axis, 0, 0, tiled=True)


def share(x, axis):
    return swap(jnp.broadcast_to(x[None], (lax.axis_size(axis),) + x.shape), axis)


def shift(x, axis, by):
    size = lax.axis_size(axis)
    return lax.ppermute(x, axis, [(i, (i + by) % size) for i in range(size)])


def around(x, pick, axis):
    return [pick(x, 0)] + [shift(pick(x, s), axis, s) for s in range(1, lax.axis_size(axis))]


def reduce_all(grad):
    rows, width = grad.shape
    planes = ("core",), Y + ("x",)
    part = grad.reshape(-1, T)
    for axes in planes:
        got = swap(part.reshape(lax.axis_size(axes), -1, T), axes)
        part = jnp.sum(got, 0)
    part = jnp.sum(share(part, ("zl", "zh")), 0)
    for axes in planes[::-1]:
        part = share(part, axes).reshape(-1, T)
    return part.reshape(rows, width)


def packed(tiles, tile_pos, edge_keep, cols):
    slots = tile_pos.shape[0]
    held = tile_pos >= 0
    trow = jnp.where(held, tile_pos // cols, -1)
    tcol = jnp.where(held, tile_pos % cols, 0)
    meta = jnp.concatenate([trow[None], tcol[None], edge_keep], 0).astype(bf16)
    meta = jnp.pad(meta, ((0, 16 - meta.shape[0]), (0, T - slots)))
    return jnp.concatenate([tiles.reshape(slots * T, T), meta], 0)


def shards(features, weight, tiles, tile_pos, edge_keep, feature_keep, negatives):
    nodes, width = features.shape
    slots = tiles.shape[0]
    xsize, zsize = lax.axis_size("x"), lax.axis_size("zh")
    ysize = lax.axis_size(Y)
    cols = xsize * zsize * lax.axis_size("core")
    zl = lax.axis_index("zl")
    place = jnp.stack([lax.axis_index("core"), zl, lax.axis_index("yl")])
    total = lax.axis_size(ROW) * cols * nodes
    part_width = width // YL
    whole = lambda x, s: x

    turned = features.T.reshape(YL, 1, part_width, nodes)
    sent = jnp.broadcast_to(turned, (YL, zsize, part_width, nodes))
    near = swap(sent.reshape(YL * zsize, part_width, nodes), ("yl", "zh"))
    held = packed(tiles, tile_pos, edge_keep, cols)
    first, last = shift(held, "yl", 1), shift(held, "yl", 3)
    near, first, last = lax.optimization_barrier((near, first, last))
    own = share(near, "x")
    across = shift(held, "yl", 2)
    own, across = lax.optimization_barrier((own, across))
    all_tiles = [held, first, across, last]
    other = shift(own, "core", 1)
    metas = jnp.stack([x[slots * T : slots * T + 4, :slots] for x in all_tiles]).astype(jnp.int32)

    part = tile_sums(metas, place, own, other, all_tiles, cols, ZL * ysize)
    part, negatives = lax.optimization_barrier((part, negatives))
    got = swap(part, ROW)
    counts = count_negatives(negatives, ZL * ysize)
    got, counts = lax.optimization_barrier((got, counts))
    got = got.reshape(ZL, ysize // YL, YL, 2, part_width, nodes).astype(f32)
    agg = jnp.sum(got, (0, 1)).transpose(1, 0, 2, 3).reshape(2, width, nodes)
    agg = (agg * feature_keep.astype(f32)[:, :, None]).astype(bf16)
    agg, counts = lax.optimization_barrier((agg, counts))
    members = share(agg, Y)
    anchors = jnp.stack(around(agg, whole, "zl"))
    ahead = lambda x, s: lax.dynamic_index_in_dim(x, lax.rem(zl + s, ZL), 0, keepdims=False)
    counts = jnp.stack(around(counts.reshape(ZL, ysize, nodes, nodes), ahead, "zl"))

    weight_t = weight.T
    group = ZL * nodes
    smem, vmem = pl.BlockSpec(memory_space=pltpu.SMEM), pl.BlockSpec(memory_space=pltpu.VMEM)
    rows = jax.ShapeDtypeStruct((8, group), f32)
    terms_shape = (ysize, 2, nodes, group)
    tot, terms = group_call(
        scores_kernel,
        (rows, jax.ShapeDtypeStruct(terms_shape, f32)),
        [smem] + [vmem] * 4,
        (vmem, HBM),
        terms_shape,
        "scores",
    )(place, anchors, members, weight_t, counts)
    tots = share(tot, "zl")
    mask = (jnp.arange(group) // nodes == zl).astype(f32)
    coef = 1.0 / (2.0 * tau * float(total) ** 0.5)
    loss, grad = group_call(
        functools.partial(grads_kernel, coef),
        (rows, jax.ShapeDtypeStruct((width, width), f32)),
        [smem] + [vmem] * 3 + [HBM] + [vmem] * 2,
        (vmem, vmem),
        terms_shape,
        "grads",
    )(place, anchors, members, weight_t, terms, tots, jnp.broadcast_to(mask, (8, group)))
    node_loss = lax.dynamic_slice_in_dim(loss[0], zl * nodes, nodes)
    return node_loss, reduce_all(grad)


def solution(mesh):
    rows, cols = mesh.devices.shape
    shape = (ZL, rows // (ZL * YL), YL, cols // 8, 4, 2)
    fine = Mesh(mesh.devices.reshape(shape), ROW + COL)
    every = ROW + COL
    in_specs = (
        P(every, None),
        P(),
        P(every, None, None),
        P(every),
        P(None, every),
        P(),
        P(every, None),
    )
    out_specs = (P(every), P())
    return jax.shard_map(shards, mesh=fine, in_specs=in_specs, out_specs=out_specs, check_vma=False)
```

```python
import functools

import jax
import jax.numpy as jnp
from jax import lax
from jax.experimental import pallas as pl
from jax.experimental.pallas import tpu as pltpu
from jax.sharding import Mesh
from jax.sharding import PartitionSpec as P

tau = 0.5
eps = 1e-06
T = 128
ZL = 3
FS = 96
f32 = jnp.float32
bf16 = jnp.bfloat16
NT = (((1,), (1,)), ((), ()))
NN = (((1,), (0,)), ((), ()))
ROW = ("zl", "y")
COL = ("x", "zh", "core")
PARAMS = dict(vmem_limit_bytes=24 * 1024 * 1024)


def dot(a, b, dims):
    return lax.dot_general(a, b, dims, preferred_element_type=f32)


def counts_kernel(blocks, neg_ref, out_ref, acc_ref):
    nodes, negs = neg_ref.shape
    rows = 8 * ((blocks + 7) // 8)
    low_iota = lax.broadcasted_iota(jnp.int32, (T, negs), 0)
    high_iota = lax.broadcasted_iota(jnp.int32, (rows, negs), 0)

    def step(i, carry):
        base = pl.multiple_of(i * 8, 8)
        index = neg_ref[pl.ds(base, 8), :]
        low = index & (T - 1)
        high = index >> 7
        for j in range(8):
            low_hot = jnp.where(low[j : j + 1, :] == low_iota, 1.0, 0.0).astype(bf16)
            high_hot = jnp.where(high[j : j + 1, :] == high_iota, 1.0, 0.0).astype(bf16)
            found = dot(high_hot, low_hot, NT)
            acc_ref[pl.ds(base + j, rows, stride=nodes), :] = found
        return carry

    lax.fori_loop(0, nodes // 8, step, 0)

    def turn(h, carry):
        block = acc_ref[pl.ds(pl.multiple_of(h * nodes, nodes), nodes), :]
        out_ref[h] = block.T.astype(jnp.int32).astype(jnp.int16)
        return carry

    lax.fori_loop(0, blocks, turn, 0)


def count_negatives(negatives, blocks):
    nodes = negatives.shape[0]
    rows = 8 * ((blocks + 7) // 8)
    return pl.pallas_call(
        functools.partial(counts_kernel, blocks),
        out_shape=jax.ShapeDtypeStruct((blocks, T, nodes), jnp.int16),
        scratch_shapes=[pltpu.VMEM((rows * nodes, T), f32)],
        compiler_params=pltpu.CompilerParams(**PARAMS),
        cost_estimate=pl.CostEstimate(
            flops=2 * 16 * nodes * T * T * 64, bytes_accessed=2 << 20, transcendentals=0
        ),
        name="counts",
    )(negatives)


def behind(place, s):
    return lax.rem(place + ZL - s, ZL)


def tiles_kernel(cols, meta_ref, place_ref, own_ref, other_ref, *refs):
    tile_refs, (out_ref, acc_ref) = refs[:ZL], refs[ZL:]
    zsize = own_ref.shape[1] // ZL
    acc_ref[...] = jnp.zeros_like(acc_ref)
    core, zl = place_ref[0], place_ref[1]
    for s in range(ZL):

        def slot(k, carry, s=s):
            trow, tcol = meta_ref[s, 0, k], meta_ref[s, 1, k]

            @pl.when(trow >= 0)
            def _():
                chip = lax.div(tcol, 2)
                at = lax.div(chip, zsize), behind(zl, s) * zsize + lax.rem(chip, zsize)
                mine = lax.rem(tcol, 2) == core
                rows = jnp.where(mine, own_ref[at], other_ref[at])
                product = dot(rows, tile_refs[s][pl.ds(pl.multiple_of(k * T, T), T), :], NT)
                for v in range(2):
                    kept = meta_ref[s, 2 + v, k].astype(f32)
                    acc_ref[trow, v] += kept * product

            return carry

        lax.fori_loop(0, meta_ref.shape[2], slot, 0)
    out_ref[...] = acc_ref[...].astype(bf16)


def tile_sums(meta, place, own, other, tiles, cols, blocks):
    shape = (blocks, 2, own.shape[2], T)
    return pl.pallas_call(
        functools.partial(tiles_kernel, cols),
        out_shape=jax.ShapeDtypeStruct(shape, bf16),
        in_specs=[pl.BlockSpec(memory_space=pltpu.SMEM)] * 2
        + [pl.BlockSpec(memory_space=pltpu.VMEM)] * (2 + ZL),
        scratch_shapes=[pltpu.VMEM(shape, f32)],
        compiler_params=pltpu.CompilerParams(**PARAMS),
        name="tile_sums",
    )(meta, place, own, other, *tiles)


def anchors_of(n_ref, zl, v):
    return jnp.concatenate([n_ref[behind(zl, z), v] for z in range(ZL)], 1)


def embed(weight_t, agg):
    z = dot(weight_t, agg, NN)
    rinv = lax.rsqrt(jnp.sum(z * z, 0, keepdims=True) + eps)
    return z * rinv, rinv


def pair_of(a_ref, p, v):
    return jnp.concatenate([a_ref[2 * p, v], a_ref[2 * p + 1, v]], 1)


def scores_kernel(place_ref, n_ref, a_ref, w_ref, c_ref, tot_ref, e_ref, low_ref):
    weight_t = w_ref[...]
    zl = place_ref[1]
    anchors = [embed(weight_t, anchors_of(n_ref, zl, v))[0].astype(bf16) for v in range(2)]
    tot_ref[...] = jnp.zeros_like(tot_ref)

    def pair(p, carry):
        count = jnp.concatenate(
            [
                jnp.concatenate([c_ref[behind(zl, z), 2 * p + i] for z in range(ZL)], 1)
                for i in range(2)
            ],
            0,
        )
        count = count.astype(jnp.int32).astype(f32)
        for v in range(2):
            emb = embed(weight_t, pair_of(a_ref, p, 1 - v))[0]
            low_ref[p, 1 - v] = emb.astype(bf16)
            score = dot(emb.T.astype(bf16), anchors[v], NN)
            term = count * jnp.exp(score * (1.0 / tau))
            e_ref[p, v] = term.astype(bf16)
            tot_ref[v : v + 1, :] += jnp.sum(term, 0, keepdims=True)
        return carry

    lax.fori_loop(0, e_ref.shape[0], pair, 0)


def pull_kernel(e_ref, low_ref, sums_ref):
    sums_ref[...] = jnp.zeros_like(sums_ref)

    def pair(p, carry):
        for v in range(2):
            sums_ref[v] += dot(low_ref[p, 1 - v], e_ref[p, v], NN)
        return carry

    lax.fori_loop(0, e_ref.shape[0], pair, 0)


def split_dot(agg, dz):
    high = dz.astype(bf16)
    low = (dz - high.astype(f32)).astype(bf16)
    return dot(agg, high, NT) + dot(agg, low, NT)


def grads_kernel(
    coef, place_ref, n_ref, a_ref, w_ref, e_ref, sums_ref, tot_ref, mask_ref, loss_ref, grad_ref
):
    weight_t = w_ref[...]
    agg_n = [anchors_of(n_ref, place_ref[1], v) for v in range(2)]
    emb_n, rinv_n = zip(*[embed(weight_t, agg) for agg in agg_n])
    full_n = [emb.astype(bf16).astype(f32) for emb in emb_n]
    pos = jnp.sum(full_n[0] * full_n[1], 0, keepdims=True) * (1.0 / tau)
    own = jnp.exp(pos)
    tot = [own + sum(tot_ref[z, v : v + 1, :] for z in range(ZL)) for v in range(2)]
    loss = 0.5 * ((jnp.log(tot[0]) - pos) + (jnp.log(tot[1]) - pos))
    loss_ref[...] = jnp.broadcast_to(loss, loss_ref.shape)
    inverse = [1.0 / t for t in tot]
    both = (own * inverse[0] + own * inverse[1] - 2.0) * mask_ref[0:1, :]
    scaled = [(full_n[v] * inverse[v]).astype(bf16) for v in range(2)]

    def back(emb, rinv, d):
        return (d - emb * jnp.sum(emb * d, 0, keepdims=True)) * rinv

    grad_ref[...] = jnp.zeros_like(grad_ref)

    def pair(p, carry):
        for v in range(2):
            agg = pair_of(a_ref, p, v)
            emb, rinv = embed(weight_t, agg)
            d = coef * dot(scaled[1 - v], e_ref[p, 1 - v], NT)
            grad_ref[...] += split_dot(agg, back(emb, rinv, d))
        return carry

    lax.fori_loop(0, e_ref.shape[0], pair, 0)
    for v in range(2):
        d = coef * (both * full_n[1 - v] + sums_ref[v] * inverse[v])
        grad_ref[...] += split_dot(agg_n[v], back(emb_n[v], rinv_n[v], d))


def group_call(kernel, out_shape, inputs, scalars, name):
    return pl.pallas_call(
        kernel,
        out_shape=out_shape,
        in_specs=[pl.BlockSpec(memory_space=pltpu.SMEM)] * scalars
        + [pl.BlockSpec(memory_space=pltpu.VMEM)] * (inputs - scalars),
        compiler_params=pltpu.CompilerParams(**PARAMS),
        cost_estimate=pl.CostEstimate(flops=1 << 31, bytes_accessed=4 << 20, transcendentals=0),
        name=name,
    )


def swap(x, axis):
    return lax.all_to_all(x, axis, 0, 0, tiled=True)


def share(x, axis):
    return swap(jnp.broadcast_to(x[None], (lax.axis_size(axis),) + x.shape), axis)


def shift(x, axis, by):
    size = lax.axis_size(axis)
    return lax.ppermute(x, axis, [(i, (i + by) % size) for i in range(size)])


def around(x, pick, axis):
    return [pick(x, 0)] + [shift(pick(x, s), axis, s) for s in range(1, lax.axis_size(axis))]


def reduce_all(grad):
    rows, width = grad.shape
    planes = ("core",), ("y", "x")
    part = grad.reshape(-1, T)
    for axes in planes:
        got = swap(part.reshape(lax.axis_size(axes), -1, T), axes)
        part = jnp.sum(got, 0)
    part = jnp.sum(share(part, ("zl", "zh")), 0)
    for axes in planes[::-1]:
        part = share(part, axes).reshape(-1, T)
    return part.reshape(rows, width)


def packed(tiles, tile_pos, edge_keep, cols):
    slots = tile_pos.shape[0]
    held = tile_pos >= 0
    trow = jnp.where(held, tile_pos // cols, -1)
    tcol = jnp.where(held, tile_pos % cols, 0)
    meta = jnp.concatenate([trow[None], tcol[None], edge_keep], 0).astype(bf16)
    meta = jnp.pad(meta, ((0, 16 - meta.shape[0]), (0, T - slots)))
    return jnp.concatenate([tiles.reshape(slots * T, T), meta], 0)


def shards(features, weight, tiles, tile_pos, edge_keep, feature_keep, negatives):
    nodes, width = features.shape
    slots = tiles.shape[0]
    xsize, zsize = lax.axis_size("x"), lax.axis_size("zh")
    ysize = lax.axis_size("y")
    cols = xsize * zsize * lax.axis_size("core")
    zl = lax.axis_index("zl")
    place = jnp.stack([lax.axis_index("core"), zl])
    total = lax.axis_size(ROW) * cols * nodes
    pad = ZL * FS - width
    whole = lambda x, s: x

    turned = jnp.pad(features.T, ((0, pad), (0, 0))).reshape(ZL, 1, FS, nodes)
    sent = jnp.broadcast_to(turned, (ZL, zsize, FS, nodes)).reshape(ZL * zsize, FS, nodes)
    near = swap(sent, ("zl", "zh"))
    all_tiles = around(packed(tiles, tile_pos, edge_keep, cols), whole, "zl")
    own = share(near, "x")
    own, all_tiles = lax.optimization_barrier((own, all_tiles))
    other = shift(own, "core", 1)
    metas = jnp.stack([x[slots * T : slots * T + 4, :slots] for x in all_tiles]).astype(jnp.int32)

    part = tile_sums(metas, place, own, other, all_tiles, cols, ZL * ysize)
    part, negatives = lax.optimization_barrier((part, negatives))
    got = swap(part, ROW)
    counts = count_negatives(negatives, ZL * ysize)
    got, counts = lax.optimization_barrier((got, counts))
    agg = jnp.sum(got.reshape(ZL, ysize, 2, FS, nodes).astype(f32), 1)
    agg = agg.transpose(1, 0, 2, 3).reshape(2, ZL * FS, nodes)[:, :width]
    agg = (agg * feature_keep.astype(f32)[:, :, None]).astype(bf16)
    agg, counts = lax.optimization_barrier((agg, counts))
    members = share(agg, "y")
    anchors = jnp.stack(around(agg, whole, "zl"))
    ahead = lambda x, s: lax.dynamic_index_in_dim(x, lax.rem(zl + s, ZL), 0, keepdims=False)
    counts = jnp.stack(around(counts.reshape(ZL, ysize, nodes, nodes), ahead, "zl"))

    weight_t = weight.T
    group = ZL * nodes
    rows = jax.ShapeDtypeStruct((8, group), f32)
    tot, terms, low = group_call(
        scores_kernel,
        (
            rows,
            jax.ShapeDtypeStruct((ysize // 2, 2, 2 * nodes, group), bf16),
            jax.ShapeDtypeStruct((ysize // 2, 2, width, 2 * nodes), bf16),
        ),
        5,
        1,
        "scores",
    )(place, anchors, members, weight_t, counts)
    tots = share(tot, "zl")
    sums = group_call(
        pull_kernel, jax.ShapeDtypeStruct((2, width, group), f32), 2, 0, "pull"
    )(terms, low)
    mask = (jnp.arange(group) // nodes == zl).astype(f32)
    mask = jnp.broadcast_to(mask, (8, group))
    coef = 1.0 / (2.0 * tau * float(total) ** 0.5)
    loss, grad = group_call(
        functools.partial(grads_kernel, coef),
        (rows, jax.ShapeDtypeStruct((width, width), f32)),
        8,
        1,
        "grads",
    )(place, anchors, members, weight_t, terms, sums, tots, mask)
    node_loss = lax.dynamic_slice_in_dim(loss[0], zl * nodes, nodes)
    return node_loss, reduce_all(grad)


def solution(mesh):
    rows, cols = mesh.devices.shape
    fine = Mesh(mesh.devices.reshape(ZL, rows // ZL, cols // 8, 4, 2), ROW + COL)
    every = ROW + COL
    in_specs = (
        P(every, None),
        P(),
        P(every, None, None),
        P(every),
        P(None, every),
        P(),
        P(every, None),
    )
    out_specs = (P(every), P())
    return jax.shard_map(shards, mesh=fine, in_specs=in_specs, out_specs=out_specs, check_vma=False)
```

```python
import functools

import jax
import jax.numpy as jnp
from jax import lax
from jax.experimental import pallas as pl
from jax.experimental.pallas import tpu as pltpu
from jax.sharding import Mesh
from jax.sharding import PartitionSpec as P

tau = 0.5
eps = 1e-06
T = 128
ZL = 3
FS = 88
f32 = jnp.float32
bf16 = jnp.bfloat16
NT = (((1,), (1,)), ((), ()))
NN = (((1,), (0,)), ((), ()))
ROW = ("zl", "y")
COL = ("x", "zh", "core")
PARAMS = dict(vmem_limit_bytes=24 * 1024 * 1024)


def dot(a, b, dims):
    return lax.dot_general(a, b, dims, preferred_element_type=f32)


def counts_kernel(blocks, neg_ref, out_ref, acc_ref):
    nodes, negs = neg_ref.shape
    rows = 8 * ((blocks + 7) // 8)
    low_iota = lax.broadcasted_iota(jnp.int32, (T, negs), 0)
    high_iota = lax.broadcasted_iota(jnp.int32, (rows, negs), 0)

    def step(i, carry):
        base = pl.multiple_of(i * 8, 8)
        index = neg_ref[pl.ds(base, 8), :]
        low = index & (T - 1)
        high = index >> 7
        for j in range(8):
            low_hot = jnp.where(low[j : j + 1, :] == low_iota, 1.0, 0.0).astype(bf16)
            high_hot = jnp.where(high[j : j + 1, :] == high_iota, 1.0, 0.0).astype(bf16)
            found = dot(high_hot, low_hot, NT)
            acc_ref[pl.ds(base + j, rows, stride=nodes), :] = found
        return carry

    lax.fori_loop(0, nodes // 8, step, 0)

    def turn(h, carry):
        block = acc_ref[pl.ds(pl.multiple_of(h * nodes, nodes), nodes), :]
        out_ref[h] = block.T.astype(jnp.int32).astype(jnp.int16)
        return carry

    lax.fori_loop(0, blocks, turn, 0)


def count_negatives(negatives, blocks):
    nodes = negatives.shape[0]
    rows = 8 * ((blocks + 7) // 8)
    return pl.pallas_call(
        functools.partial(counts_kernel, blocks),
        out_shape=jax.ShapeDtypeStruct((blocks, T, nodes), jnp.int16),
        scratch_shapes=[pltpu.VMEM((rows * nodes, T), f32)],
        compiler_params=pltpu.CompilerParams(**PARAMS),
        cost_estimate=pl.CostEstimate(
            flops=2 * 16 * nodes * T * T * 64, bytes_accessed=2 << 20, transcendentals=0
        ),
        name="counts",
    )(negatives)


def behind(place, s):
    return lax.rem(place + ZL - s, ZL)


def tiles_kernel(cols, meta_ref, place_ref, own_ref, other_ref, *refs):
    tile_refs, (out_ref, acc_ref) = refs[:ZL], refs[ZL:]
    zsize = own_ref.shape[1] // ZL
    acc_ref[...] = jnp.zeros_like(acc_ref)
    core, zl = place_ref[0], place_ref[1]
    for s in range(ZL):

        def slot(k, carry, s=s):
            trow, tcol = meta_ref[s, 0, k], meta_ref[s, 1, k]

            @pl.when(trow >= 0)
            def _():
                chip = lax.div(tcol, 2)
                at = lax.div(chip, zsize), behind(zl, s) * zsize + lax.rem(chip, zsize)
                mine = lax.rem(tcol, 2) == core
                rows = jnp.where(mine, own_ref[at], other_ref[at])
                product = dot(rows, tile_refs[s][pl.ds(pl.multiple_of(k * T, T), T), :], NT)
                for v in range(2):
                    kept = meta_ref[s, 2 + v, k].astype(f32)
                    acc_ref[trow, v] += kept * product

            return carry

        lax.fori_loop(0, meta_ref.shape[2], slot, 0)
    out_ref[...] = acc_ref[...].astype(bf16)


def tile_sums(meta, place, own, other, tiles, cols, blocks):
    shape = (blocks, 2, own.shape[2], T)
    return pl.pallas_call(
        functools.partial(tiles_kernel, cols),
        out_shape=jax.ShapeDtypeStruct(shape, bf16),
        in_specs=[pl.BlockSpec(memory_space=pltpu.SMEM)] * 2
        + [pl.BlockSpec(memory_space=pltpu.VMEM)] * (2 + ZL),
        scratch_shapes=[pltpu.VMEM(shape, f32)],
        compiler_params=pltpu.CompilerParams(**PARAMS),
        name="tile_sums",
    )(meta, place, own, other, *tiles)


def anchors_of(n_ref, zl, v):
    return jnp.concatenate([n_ref[behind(zl, z), v] for z in range(ZL)], 1)


def embed(weight_t, agg):
    z = dot(weight_t, agg, NN)
    rinv = lax.rsqrt(jnp.sum(z * z, 0, keepdims=True) + eps)
    return z * rinv, rinv


def pair_of(a_ref, p, v):
    return jnp.concatenate([a_ref[2 * p, v], a_ref[2 * p + 1, v]], 1)


def scores_kernel(place_ref, n_ref, a_ref, w_ref, c_ref, tot_ref, e_ref, low_ref):
    weight_t = w_ref[...]
    zl = place_ref[1]
    anchors = [embed(weight_t, anchors_of(n_ref, zl, v))[0].astype(bf16) for v in range(2)]
    tot_ref[...] = jnp.zeros_like(tot_ref)

    def pair(p, carry):
        count = jnp.concatenate(
            [
                jnp.concatenate([c_ref[behind(zl, z), 2 * p + i] for z in range(ZL)], 1)
                for i in range(2)
            ],
            0,
        )
        count = count.astype(jnp.int32).astype(f32)
        for v in range(2):
            emb = embed(weight_t, pair_of(a_ref, p, 1 - v))[0]
            low_ref[p, 1 - v] = emb.astype(bf16)
            score = dot(emb.T.astype(bf16), anchors[v], NN)
            term = count * jnp.exp(score * (1.0 / tau))
            e_ref[p, v] = term.astype(bf16)
            tot_ref[v : v + 1, :] += jnp.sum(term, 0, keepdims=True)
        return carry

    lax.fori_loop(0, e_ref.shape[0], pair, 0)


def pull_kernel(e_ref, low_ref, sums_ref):
    sums_ref[...] = jnp.zeros_like(sums_ref)

    def pair(p, carry):
        for v in range(2):
            sums_ref[v] += dot(low_ref[p, 1 - v], e_ref[p, v], NN)
        return carry

    lax.fori_loop(0, e_ref.shape[0], pair, 0)


def split_dot(agg, dz):
    high = dz.astype(bf16)
    low = (dz - high.astype(f32)).astype(bf16)
    return dot(agg, high, NT) + dot(agg, low, NT)


def grads_kernel(
    coef, place_ref, n_ref, a_ref, w_ref, e_ref, sums_ref, mask_ref, *refs
):
    *tot_refs, loss_ref, grad_ref = refs
    weight_t = w_ref[...]
    agg_n = [anchors_of(n_ref, place_ref[1], v) for v in range(2)]
    emb_n, rinv_n = zip(*[embed(weight_t, agg) for agg in agg_n])
    full_n = [emb.astype(bf16).astype(f32) for emb in emb_n]
    pos = jnp.sum(full_n[0] * full_n[1], 0, keepdims=True) * (1.0 / tau)
    own = jnp.exp(pos)
    tot = [own + sum(t[v : v + 1, :] for t in tot_refs) for v in range(2)]
    loss = 0.5 * ((jnp.log(tot[0]) - pos) + (jnp.log(tot[1]) - pos))
    loss_ref[...] = jnp.broadcast_to(loss, loss_ref.shape)
    inverse = [1.0 / t for t in tot]
    both = (own * inverse[0] + own * inverse[1] - 2.0) * mask_ref[0:1, :]
    scaled = [(full_n[v] * inverse[v]).astype(bf16) for v in range(2)]

    def back(emb, rinv, d):
        return (d - emb * jnp.sum(emb * d, 0, keepdims=True)) * rinv

    grad_ref[...] = jnp.zeros_like(grad_ref)

    def pair(p, carry):
        for v in range(2):
            agg = pair_of(a_ref, p, v)
            emb, rinv = embed(weight_t, agg)
            d = coef * dot(scaled[1 - v], e_ref[p, 1 - v], NT)
            grad_ref[...] += split_dot(agg, back(emb, rinv, d))
        return carry

    lax.fori_loop(0, e_ref.shape[0], pair, 0)
    for v in range(2):
        d = coef * (both * full_n[1 - v] + sums_ref[v] * inverse[v])
        grad_ref[...] += split_dot(agg_n[v], back(emb_n[v], rinv_n[v], d))


def group_call(kernel, out_shape, inputs, scalars, name):
    return pl.pallas_call(
        kernel,
        out_shape=out_shape,
        in_specs=[pl.BlockSpec(memory_space=pltpu.SMEM)] * scalars
        + [pl.BlockSpec(memory_space=pltpu.VMEM)] * (inputs - scalars),
        compiler_params=pltpu.CompilerParams(**PARAMS),
        cost_estimate=pl.CostEstimate(flops=1 << 31, bytes_accessed=4 << 20, transcendentals=0),
        name=name,
    )


def swap(x, axis):
    return lax.all_to_all(x, axis, 0, 0, tiled=True)


def share(x, axis):
    return swap(jnp.broadcast_to(x[None], (lax.axis_size(axis),) + x.shape), axis)


def shift(x, axis, by):
    size = lax.axis_size(axis)
    return lax.ppermute(x, axis, [(i, (i + by) % size) for i in range(size)])


def around(x, pick, axis):
    return [pick(x, 0)] + [shift(pick(x, s), axis, s) for s in range(1, lax.axis_size(axis))]


def reduce_all(grad):
    rows, width = grad.shape
    planes = ("core",), ("y", "x")
    part = grad.reshape(-1, T)
    for axes in planes:
        got = swap(part.reshape(lax.axis_size(axes), -1, T), axes)
        part = jnp.sum(got, 0)
    part = jnp.sum(share(part, ("zl", "zh")), 0)
    for axes in planes[::-1]:
        part = share(part, axes).reshape(-1, T)
    return part.reshape(rows, width)


def packed(tiles, tile_pos, edge_keep, cols):
    slots = tile_pos.shape[0]
    held = tile_pos >= 0
    trow = jnp.where(held, tile_pos // cols, -1)
    tcol = jnp.where(held, tile_pos % cols, 0)
    meta = jnp.concatenate([trow[None], tcol[None], edge_keep], 0).astype(bf16)
    meta = jnp.pad(meta, ((0, 16 - meta.shape[0]), (0, T - slots)))
    return jnp.concatenate([tiles.reshape(slots * T, T), meta], 0)


def shards(features, weight, tiles, tile_pos, edge_keep, feature_keep, negatives):
    nodes, width = features.shape
    slots = tiles.shape[0]
    xsize, zsize = lax.axis_size("x"), lax.axis_size("zh")
    ysize = lax.axis_size("y")
    cols = xsize * zsize * lax.axis_size("core")
    zl = lax.axis_index("zl")
    place = jnp.stack([lax.axis_index("core"), zl])
    total = lax.axis_size(ROW) * cols * nodes
    pad = ZL * FS - width
    whole = lambda x, s: x

    turned = jnp.pad(features.T, ((0, pad), (0, 0))).reshape(ZL, 1, FS, nodes)
    sent = jnp.broadcast_to(turned, (ZL, zsize, FS, nodes)).reshape(ZL * zsize, FS, nodes)
    near = swap(sent, ("zl", "zh"))
    held = packed(tiles, tile_pos, edge_keep, cols)
    next_tiles = shift(held, "zl", 1)
    near, next_tiles = lax.optimization_barrier((near, next_tiles))
    own = share(near, "x")
    last_tiles = shift(held, "zl", 2)
    own, last_tiles = lax.optimization_barrier((own, last_tiles))
    all_tiles = [held, next_tiles, last_tiles]
    other = shift(own, "core", 1)
    metas = jnp.stack([x[slots * T : slots * T + 4, :slots] for x in all_tiles]).astype(jnp.int32)

    part = tile_sums(metas, place, own, other, all_tiles, cols, ZL * ysize)
    part, negatives = lax.optimization_barrier((part, negatives))
    got = swap(part, ROW)
    counts = count_negatives(negatives, ZL * ysize)
    got, counts = lax.optimization_barrier((got, counts))
    agg = jnp.sum(got.reshape(ZL, ysize, 2, FS, nodes).astype(f32), 1)
    agg = agg.transpose(1, 0, 2, 3).reshape(2, ZL * FS, nodes)[:, :width]
    agg = (agg * feature_keep.astype(f32)[:, :, None]).astype(bf16)
    agg, counts = lax.optimization_barrier((agg, counts))
    members = share(agg, "y")
    anchors = jnp.stack(around(agg, whole, "zl"))
    ahead = lambda x, s: lax.dynamic_index_in_dim(x, lax.rem(zl + s, ZL), 0, keepdims=False)
    counts = jnp.stack(around(counts.reshape(ZL, ysize, nodes, nodes), ahead, "zl"))

    weight_t = weight.T
    group = ZL * nodes
    rows = jax.ShapeDtypeStruct((8, group), f32)
    tot, terms, low = group_call(
        scores_kernel,
        (
            rows,
            jax.ShapeDtypeStruct((ysize // 2, 2, 2 * nodes, group), bf16),
            jax.ShapeDtypeStruct((ysize // 2, 2, width, 2 * nodes), bf16),
        ),
        5,
        1,
        "scores",
    )(place, anchors, members, weight_t, counts)
    tots = around(tot, whole, "zl")
    sums = group_call(
        pull_kernel, jax.ShapeDtypeStruct((2, width, group), f32), 2, 0, "pull"
    )(terms, low)
    mask = (jnp.arange(group) // nodes == zl).astype(f32)
    mask = jnp.broadcast_to(mask, (8, group))
    coef = 1.0 / (2.0 * tau * float(total) ** 0.5)
    loss, grad = group_call(
        functools.partial(grads_kernel, coef),
        (rows, jax.ShapeDtypeStruct((width, width), f32)),
        7 + ZL,
        1,
        "grads",
    )(place, anchors, members, weight_t, terms, sums, mask, *tots)
    node_loss = lax.dynamic_slice_in_dim(loss[0], zl * nodes, nodes)
    return node_loss, reduce_all(grad)


def solution(mesh):
    rows, cols = mesh.devices.shape
    fine = Mesh(mesh.devices.reshape(ZL, rows // ZL, cols // 8, 4, 2), ROW + COL)
    every = ROW + COL
    in_specs = (
        P(every, None),
        P(),
        P(every, None, None),
        P(every),
        P(None, every),
        P(),
        P(every, None),
    )
    out_specs = (P(every), P())
    return jax.shard_map(shards, mesh=fine, in_specs=in_specs, out_specs=out_specs, check_vma=False)
```

```python
import functools

import jax
import jax.numpy as jnp
from jax import lax
from jax.experimental import pallas as pl
from jax.experimental.pallas import tpu as pltpu
from jax.sharding import Mesh
from jax.sharding import PartitionSpec as P

tau = 0.5
eps = 1e-06
T = 128
ZL = 3
YQ = 4
FS = 88
f32 = jnp.float32
bf16 = jnp.bfloat16
NT = (((1,), (1,)), ((), ()))
NN = (((1,), (0,)), ((), ()))
Y = ("yq", "yp")
ROW = ("zl",) + Y
MEMBERS = ("zl", "yp")
COL = ("x", "zh", "core")
PARAMS = dict(vmem_limit_bytes=24 * 1024 * 1024)


def dot(a, b, dims):
    return lax.dot_general(a, b, dims, preferred_element_type=f32)


def counts_kernel(blocks, neg_ref, out_ref, acc_ref):
    nodes, negs = neg_ref.shape
    rows = 8 * ((blocks + 7) // 8)
    low_iota = lax.broadcasted_iota(jnp.int32, (T, negs), 0)
    high_iota = lax.broadcasted_iota(jnp.int32, (rows, negs), 0)

    def step(i, carry):
        base = pl.multiple_of(i * 8, 8)
        index = neg_ref[pl.ds(base, 8), :]
        low = index & (T - 1)
        high = index >> 7
        for j in range(0, 8, 2):
            low_hot, high_hot = (
                jnp.concatenate(
                    [jnp.where(part[j + i : j + i + 1, :] == iota, 1.0, 0.0) for i in range(2)], 0
                ).astype(bf16)
                for part, iota in ((low, low_iota), (high, high_iota))
            )
            found = dot(high_hot, low_hot, NT)
            for i in range(2):
                own = found[i * rows : (i + 1) * rows, i * T : (i + 1) * T]
                acc_ref[pl.ds(base + j + i, rows, stride=nodes), :] = own
        return carry

    lax.fori_loop(0, nodes // 8, step, 0)

    def turn(h, carry):
        block = acc_ref[pl.ds(pl.multiple_of(h * nodes, nodes), nodes), :]
        out_ref[h] = block.T.astype(jnp.int32).astype(jnp.int16)
        return carry

    lax.fori_loop(0, blocks, turn, 0)


def count_negatives(negatives, blocks):
    nodes = negatives.shape[0]
    rows = 8 * ((blocks + 7) // 8)
    return pl.pallas_call(
        functools.partial(counts_kernel, blocks),
        out_shape=jax.ShapeDtypeStruct((blocks, T, nodes), jnp.int16),
        scratch_shapes=[pltpu.VMEM((rows * nodes, T), f32)],
        compiler_params=pltpu.CompilerParams(**PARAMS),
        cost_estimate=pl.CostEstimate(
            flops=2 * 16 * nodes * T * T * 64, bytes_accessed=2 << 20, transcendentals=0
        ),
        name="counts",
    )(negatives)


def behind(place, s, size):
    return lax.rem(place + size - s, size)


def tiles_kernel(cols, meta_ref, place_ref, own_ref, other_ref, *refs):
    tile_refs, (out_ref, acc_ref) = refs[:ZL], refs[ZL:]
    zsize = own_ref.shape[1] // ZL
    slots = meta_ref.shape[2]
    acc_ref[...] = jnp.zeros_like(acc_ref)
    core, zl = place_ref[0], place_ref[1]
    for s in range(ZL):

        def few(i, carry, s=s):
            @pl.when(meta_ref[s, 0, i * 4] >= 0)
            def _():
                products = []
                for j in range(4):
                    k = i * 4 + j
                    tcol = meta_ref[s, 1, k]
                    chip = lax.div(tcol, 2)
                    at = lax.div(chip, zsize), behind(zl, s, ZL) * zsize + lax.rem(chip, zsize)
                    mine = lax.rem(tcol, 2) == core
                    rows = jnp.where(mine, own_ref[at], other_ref[at])
                    tile = tile_refs[s][pl.ds(pl.multiple_of(k * T, T), T), :]
                    products.append(dot(rows, tile, NT))
                for j in range(4):
                    k = i * 4 + j
                    trow = meta_ref[s, 0, k]
                    held = jnp.where(trow >= 0, 1, 0)
                    at = jnp.maximum(trow, 0)
                    for v in range(2):
                        kept = (held * meta_ref[s, 2 + v, k]).astype(f32)
                        acc_ref[at, v] += kept * products[j]

            return carry

        lax.fori_loop(0, slots // 4, few, 0)
    out_ref[...] = acc_ref[...].astype(bf16)


def tile_sums(meta, place, own, other, tiles, cols, blocks):
    shape = (blocks, 2, own.shape[2], T)
    return pl.pallas_call(
        functools.partial(tiles_kernel, cols),
        out_shape=jax.ShapeDtypeStruct(shape, bf16),
        in_specs=[pl.BlockSpec(memory_space=pltpu.SMEM)] * 2
        + [pl.BlockSpec(memory_space=pltpu.VMEM)] * (2 + ZL),
        scratch_shapes=[pltpu.VMEM(shape, f32)],
        compiler_params=pltpu.CompilerParams(**PARAMS),
        name="tile_sums",
    )(meta, place, own, other, *tiles)


def anchors_of(n_ref, yq, v):
    return jnp.concatenate([n_ref[behind(yq, q, YQ), v] for q in range(YQ)], 1)


def embed(weight_t, agg):
    z = dot(weight_t, agg, NN)
    rinv = lax.rsqrt(jnp.sum(z * z, 0, keepdims=True) + eps)
    return z * rinv, rinv


def pair_of(a_ref, p, v):
    return jnp.concatenate([a_ref[2 * p, v], a_ref[2 * p + 1, v]], 1)


def scores_kernel(place_ref, n_ref, a_ref, w_ref, c_ref, tot_ref, e_ref, low_ref):
    weight_t = w_ref[...]
    yq = place_ref[2]
    anchors = [embed(weight_t, anchors_of(n_ref, yq, v))[0].astype(bf16) for v in range(2)]
    tot_ref[...] = jnp.zeros_like(tot_ref)

    def pair(p, carry):
        count = jnp.concatenate(
            [
                jnp.concatenate([c_ref[behind(yq, q, YQ), 2 * p + i] for q in range(YQ)], 1)
                for i in range(2)
            ],
            0,
        )
        count = count.astype(jnp.int32).astype(f32)
        for v in range(2):
            emb = embed(weight_t, pair_of(a_ref, p, 1 - v))[0]
            low_ref[p, 1 - v] = emb.astype(bf16)
            score = dot(emb.T.astype(bf16), anchors[v], NN)
            term = count * jnp.exp(score * (1.0 / tau))
            e_ref[p, v] = term.astype(bf16)
            tot_ref[v : v + 1, :] += jnp.sum(term, 0, keepdims=True)
        return carry

    lax.fori_loop(0, e_ref.shape[0], pair, 0)


def pull_kernel(e_ref, low_ref, sums_ref):
    sums_ref[...] = jnp.zeros_like(sums_ref)

    def pair(p, carry):
        for v in range(2):
            sums_ref[v] += dot(low_ref[p, 1 - v], e_ref[p, v], NN)
        return carry

    lax.fori_loop(0, e_ref.shape[0], pair, 0)


def split_dot(agg, dz):
    high = dz.astype(bf16)
    low = (dz - high.astype(f32)).astype(bf16)
    return dot(agg, high, NT) + dot(agg, low, NT)


def grads_kernel(
    coef, place_ref, n_ref, a_ref, w_ref, e_ref, sums_ref, mask_ref, *refs
):
    *tot_refs, loss_ref, grad_ref = refs
    weight_t = w_ref[...]
    agg_n = [anchors_of(n_ref, place_ref[2], v) for v in range(2)]
    emb_n, rinv_n = zip(*[embed(weight_t, agg) for agg in agg_n])
    full_n = [emb.astype(bf16).astype(f32) for emb in emb_n]
    pos = jnp.sum(full_n[0] * full_n[1], 0, keepdims=True) * (1.0 / tau)
    own = jnp.exp(pos)
    tot = [own + sum(t[v : v + 1, :] for t in tot_refs) for v in range(2)]
    loss = 0.5 * ((jnp.log(tot[0]) - pos) + (jnp.log(tot[1]) - pos))
    loss_ref[...] = jnp.broadcast_to(loss, loss_ref.shape)
    inverse = [1.0 / t for t in tot]
    both = (own * inverse[0] + own * inverse[1] - 2.0) * mask_ref[0:1, :]
    scaled = [(full_n[v] * inverse[v]).astype(bf16) for v in range(2)]

    def back(emb, rinv, d):
        return (d - emb * jnp.sum(emb * d, 0, keepdims=True)) * rinv

    grad_ref[...] = jnp.zeros_like(grad_ref)

    def pair(p, carry):
        for v in range(2):
            agg = pair_of(a_ref, p, v)
            emb, rinv = embed(weight_t, agg)
            d = coef * dot(scaled[1 - v], e_ref[p, 1 - v], NT)
            grad_ref[...] += split_dot(agg, back(emb, rinv, d))
        return carry

    lax.fori_loop(0, e_ref.shape[0], pair, 0)
    for v in range(2):
        d = coef * (both * full_n[1 - v] + sums_ref[v] * inverse[v])
        grad_ref[...] += split_dot(agg_n[v], back(emb_n[v], rinv_n[v], d))


def group_call(kernel, out_shape, inputs, scalars, name):
    return pl.pallas_call(
        kernel,
        out_shape=out_shape,
        in_specs=[pl.BlockSpec(memory_space=pltpu.SMEM)] * scalars
        + [pl.BlockSpec(memory_space=pltpu.VMEM)] * (inputs - scalars),
        compiler_params=pltpu.CompilerParams(**PARAMS),
        cost_estimate=pl.CostEstimate(flops=1 << 31, bytes_accessed=4 << 20, transcendentals=0),
        name=name,
    )


def swap(x, axis):
    return lax.all_to_all(x, axis, 0, 0, tiled=True)


def share(x, axis):
    return swap(jnp.broadcast_to(x[None], (lax.axis_size(axis),) + x.shape), axis)


def shift(x, axis, by):
    size = lax.axis_size(axis)
    return lax.ppermute(x, axis, [(i, (i + by) % size) for i in range(size)])


def around(x, pick, axis):
    return [pick(x, 0)] + [shift(pick(x, s), axis, s) for s in range(1, lax.axis_size(axis))]


def reduce_all(grad):
    rows, width = grad.shape
    planes = ("core",), Y + ("x",)
    part = grad.reshape(-1, T)
    for axes in planes:
        got = swap(part.reshape(lax.axis_size(axes), -1, T), axes)
        part = jnp.sum(got, 0)
    part = jnp.sum(share(part, ("zl", "zh")), 0)
    for axes in planes[::-1]:
        part = share(part, axes).reshape(-1, T)
    return part.reshape(rows, width)


def packed(tiles, tile_pos, edge_keep, cols):
    slots = tile_pos.shape[0]
    held = tile_pos >= 0
    trow = jnp.where(held, tile_pos // cols, -1)
    tcol = jnp.where(held, tile_pos % cols, 0)
    meta = jnp.concatenate([trow[None], tcol[None], edge_keep], 0).astype(bf16)
    meta = jnp.pad(meta, ((0, 16 - meta.shape[0]), (0, T - slots)))
    return jnp.concatenate([tiles.reshape(slots * T, T), meta], 0)


def shards(features, weight, tiles, tile_pos, edge_keep, feature_keep, negatives):
    nodes, width = features.shape
    slots = tiles.shape[0]
    xsize, zsize = lax.axis_size("x"), lax.axis_size("zh")
    ysize, psize = lax.axis_size(Y), lax.axis_size("yp")
    cols = xsize * zsize * lax.axis_size("core")
    zl, yq = lax.axis_index("zl"), lax.axis_index("yq")
    place = jnp.stack([lax.axis_index("core"), zl, yq])
    total = lax.axis_size(ROW) * cols * nodes
    pad = ZL * FS - width
    whole = lambda x, s: x

    turned = jnp.pad(features.T, ((0, pad), (0, 0))).reshape(ZL, 1, FS, nodes)
    sent = jnp.broadcast_to(turned, (ZL, zsize, FS, nodes)).reshape(ZL * zsize, FS, nodes)
    near = swap(sent, ("zl", "zh"))
    held = packed(tiles, tile_pos, edge_keep, cols)
    next_tiles = shift(held, "zl", 1)
    counts = count_negatives(negatives, ZL * ysize)
    near, next_tiles, counts = lax.optimization_barrier((near, next_tiles, counts))
    own = share(near, "x")
    last_tiles = shift(held, "zl", 2)
    counts = counts.reshape(ZL, YQ, psize, nodes, nodes)
    ahead = lambda x, s: lax.dynamic_index_in_dim(x, lax.rem(yq + s, YQ), 1, keepdims=False)
    counts = around(counts, ahead, "yq")
    own, last_tiles, counts = lax.optimization_barrier((own, last_tiles, counts))
    all_tiles = [held, next_tiles, last_tiles]
    other = shift(own, "core", 1)
    metas = jnp.stack([x[slots * T : slots * T + 4, :slots] for x in all_tiles]).astype(jnp.int32)

    part = tile_sums(metas, place, own, other, all_tiles, cols, ZL * ysize)
    part, counts = lax.optimization_barrier((part, counts))
    got = swap(part, ROW)
    counts = jnp.stack(counts).reshape(YQ, ZL * psize, nodes, nodes)
    agg = jnp.sum(got.reshape(ZL, ysize, 2, FS, nodes).astype(f32), 1)
    agg = agg.transpose(1, 0, 2, 3).reshape(2, ZL * FS, nodes)[:, :width]
    agg = (agg * feature_keep.astype(f32)[:, :, None]).astype(bf16)
    members = share(agg, MEMBERS)
    anchors = jnp.stack(around(agg, whole, "yq"))

    weight_t = weight.T
    group, pairs = YQ * nodes, ZL * psize // 2
    rows = jax.ShapeDtypeStruct((8, group), f32)
    tot, terms, low = group_call(
        scores_kernel,
        (
            rows,
            jax.ShapeDtypeStruct((pairs, 2, 2 * nodes, group), bf16),
            jax.ShapeDtypeStruct((pairs, 2, width, 2 * nodes), bf16),
        ),
        5,
        1,
        "scores",
    )(place, anchors, members, weight_t, counts)
    tots = around(tot, whole, "yq")
    sums = group_call(
        pull_kernel, jax.ShapeDtypeStruct((2, width, group), f32), 2, 0, "pull"
    )(terms, low)
    mask = (jnp.arange(group) // nodes == yq).astype(f32)
    mask = jnp.broadcast_to(mask, (8, group))
    coef = 1.0 / (2.0 * tau * float(total) ** 0.5)
    loss, grad = group_call(
        functools.partial(grads_kernel, coef),
        (rows, jax.ShapeDtypeStruct((width, width), f32)),
        7 + YQ,
        1,
        "grads",
    )(place, anchors, members, weight_t, terms, sums, mask, *tots)
    node_loss = lax.dynamic_slice_in_dim(loss[0], yq * nodes, nodes)
    return node_loss, reduce_all(grad)


def solution(mesh):
    rows, cols = mesh.devices.shape
    fine = Mesh(mesh.devices.reshape(ZL, YQ, rows // (ZL * YQ), cols // 8, 4, 2), ROW + COL)
    every = ROW + COL
    in_specs = (
        P(every, None),
        P(),
        P(every, None, None),
        P(every),
        P(None, every),
        P(),
        P(every, None),
    )
    out_specs = (P(every), P())
    return jax.shard_map(shards, mesh=fine, in_specs=in_specs, out_specs=out_specs, check_vma=False)
```

```python
import functools

import jax
import jax.numpy as jnp
from jax import lax
from jax.experimental import pallas as pl
from jax.experimental.pallas import tpu as pltpu
from jax.sharding import Mesh
from jax.sharding import PartitionSpec as P

tau = 0.5
eps = 1e-06
T = 128
ZL = 3
FS = 88
f32 = jnp.float32
bf16 = jnp.bfloat16
NT = (((1,), (1,)), ((), ()))
NN = (((1,), (0,)), ((), ()))
ROW = ("zl", "y")
COL = ("x", "zh", "core")
PARAMS = dict(vmem_limit_bytes=24 * 1024 * 1024)


def dot(a, b, dims):
    return lax.dot_general(a, b, dims, preferred_element_type=f32)


def counts_kernel(blocks, neg_ref, out_ref, acc_ref):
    nodes, negs = neg_ref.shape
    rows = 8 * ((blocks + 7) // 8)
    low_iota = lax.broadcasted_iota(jnp.int32, (T, negs), 0)
    high_iota = lax.broadcasted_iota(jnp.int32, (rows, negs), 0)

    def step(i, carry):
        base = pl.multiple_of(i * 8, 8)
        index = neg_ref[pl.ds(base, 8), :]
        low = index & (T - 1)
        high = index >> 7
        for j in range(0, 8, 2):
            low_hot, high_hot = (
                jnp.concatenate(
                    [jnp.where(part[j + i : j + i + 1, :] == iota, 1.0, 0.0) for i in range(2)], 0
                ).astype(bf16)
                for part, iota in ((low, low_iota), (high, high_iota))
            )
            found = dot(high_hot, low_hot, NT)
            for i in range(2):
                own = found[i * rows : (i + 1) * rows, i * T : (i + 1) * T]
                acc_ref[pl.ds(base + j + i, rows, stride=nodes), :] = own
        return carry

    lax.fori_loop(0, nodes // 8, step, 0)

    def turn(h, carry):
        block = acc_ref[pl.ds(pl.multiple_of(h * nodes, nodes), nodes), :]
        out_ref[h] = block.T.astype(jnp.int32).astype(jnp.int16)
        return carry

    lax.fori_loop(0, blocks, turn, 0)


def count_negatives(negatives, blocks):
    nodes = negatives.shape[0]
    rows = 8 * ((blocks + 7) // 8)
    return pl.pallas_call(
        functools.partial(counts_kernel, blocks),
        out_shape=jax.ShapeDtypeStruct((blocks, T, nodes), jnp.int16),
        scratch_shapes=[pltpu.VMEM((rows * nodes, T), f32)],
        compiler_params=pltpu.CompilerParams(**PARAMS),
        cost_estimate=pl.CostEstimate(
            flops=2 * 16 * nodes * T * T * 64, bytes_accessed=2 << 20, transcendentals=0
        ),
        name="counts",
    )(negatives)


def behind(place, s):
    return lax.rem(place + ZL - s, ZL)


def tiles_kernel(cols, meta_ref, place_ref, own_ref, other_ref, *refs):
    tile_refs, (out_ref, acc_ref) = refs[:ZL], refs[ZL:]
    zsize = own_ref.shape[1] // ZL
    slots = meta_ref.shape[2]
    acc_ref[...] = jnp.zeros_like(acc_ref)
    core, zl = place_ref[0], place_ref[1]
    for s in range(ZL):

        def few(i, carry, s=s):
            @pl.when(meta_ref[s, 0, i * 4] >= 0)
            def _():
                products = []
                for j in range(4):
                    k = i * 4 + j
                    tcol = meta_ref[s, 1, k]
                    chip = lax.div(tcol, 2)
                    at = lax.div(chip, zsize), behind(zl, s) * zsize + lax.rem(chip, zsize)
                    mine = lax.rem(tcol, 2) == core
                    rows = jnp.where(mine, own_ref[at], other_ref[at])
                    tile = tile_refs[s][pl.ds(pl.multiple_of(k * T, T), T), :]
                    products.append(dot(rows, tile, NT))
                for j in range(4):
                    k = i * 4 + j
                    trow = meta_ref[s, 0, k]
                    held = jnp.where(trow >= 0, 1, 0)
                    at = jnp.maximum(trow, 0)
                    for v in range(2):
                        kept = (held * meta_ref[s, 2 + v, k]).astype(f32)
                        acc_ref[at, v] += kept * products[j]

            return carry

        lax.fori_loop(0, slots // 4, few, 0)
    out_ref[...] = acc_ref[...].astype(bf16)


def tile_sums(meta, place, own, other, tiles, cols, blocks):
    shape = (blocks, 2, own.shape[2], T)
    return pl.pallas_call(
        functools.partial(tiles_kernel, cols),
        out_shape=jax.ShapeDtypeStruct(shape, bf16),
        in_specs=[pl.BlockSpec(memory_space=pltpu.SMEM)] * 2
        + [pl.BlockSpec(memory_space=pltpu.VMEM)] * (2 + ZL),
        scratch_shapes=[pltpu.VMEM(shape, f32)],
        compiler_params=pltpu.CompilerParams(**PARAMS),
        name="tile_sums",
    )(meta, place, own, other, *tiles)


def anchors_of(n_ref, zl, v):
    return jnp.concatenate([n_ref[behind(zl, z), v] for z in range(ZL)], 1)


def embed(weight_t, agg):
    z = dot(weight_t, agg, NN)
    rinv = lax.rsqrt(jnp.sum(z * z, 0, keepdims=True) + eps)
    return z * rinv, rinv


def pair_of(a_ref, p, v):
    return jnp.concatenate([a_ref[2 * p, v], a_ref[2 * p + 1, v]], 1)


def scores_kernel(place_ref, n_ref, a_ref, w_ref, c_ref, tot_ref, e_ref, low_ref):
    weight_t = w_ref[...]
    zl = place_ref[1]
    anchors = [embed(weight_t, anchors_of(n_ref, zl, v))[0].astype(bf16) for v in range(2)]
    tot_ref[...] = jnp.zeros_like(tot_ref)

    def pair(p, carry):
        count = jnp.concatenate(
            [
                jnp.concatenate([c_ref[behind(zl, z), 2 * p + i] for z in range(ZL)], 1)
                for i in range(2)
            ],
            0,
        )
        count = count.astype(jnp.int32).astype(f32)
        for v in range(2):
            emb = embed(weight_t, pair_of(a_ref, p, 1 - v))[0]
            low_ref[p, 1 - v] = emb.astype(bf16)
            score = dot(emb.T.astype(bf16), anchors[v], NN)
            term = count * jnp.exp(score * (1.0 / tau))
            e_ref[p, v] = term.astype(bf16)
            tot_ref[v : v + 1, :] += jnp.sum(term, 0, keepdims=True)
        return carry

    lax.fori_loop(0, e_ref.shape[0], pair, 0, unroll=True)


def pull_kernel(e_ref, low_ref, sums_ref):
    sums_ref[...] = jnp.zeros_like(sums_ref)

    def pair(p, carry):
        for v in range(2):
            sums_ref[v] += dot(low_ref[p, 1 - v], e_ref[p, v], NN)
        return carry

    lax.fori_loop(0, e_ref.shape[0], pair, 0, unroll=True)


def split_dot(agg, dz):
    high = dz.astype(bf16)
    low = (dz - high.astype(f32)).astype(bf16)
    return dot(agg, high, NT) + dot(agg, low, NT)


def grads_kernel(
    coef, place_ref, n_ref, a_ref, w_ref, e_ref, sums_ref, mask_ref, *refs
):
    *tot_refs, loss_ref, grad_ref = refs
    weight_t = w_ref[...]
    agg_n = [anchors_of(n_ref, place_ref[1], v) for v in range(2)]
    emb_n, rinv_n = zip(*[embed(weight_t, agg) for agg in agg_n])
    full_n = [emb.astype(bf16).astype(f32) for emb in emb_n]
    pos = jnp.sum(full_n[0] * full_n[1], 0, keepdims=True) * (1.0 / tau)
    own = jnp.exp(pos)
    tot = [own + sum(t[v : v + 1, :] for t in tot_refs) for v in range(2)]
    loss = 0.5 * ((jnp.log(tot[0]) - pos) + (jnp.log(tot[1]) - pos))
    loss_ref[...] = jnp.broadcast_to(loss, loss_ref.shape)
    inverse = [1.0 / t for t in tot]
    both = (own * inverse[0] + own * inverse[1] - 2.0) * mask_ref[0:1, :]
    scaled = [(full_n[v] * inverse[v]).astype(bf16) for v in range(2)]

    def back(emb, rinv, d):
        return (d - emb * jnp.sum(emb * d, 0, keepdims=True)) * rinv

    grad_ref[...] = jnp.zeros_like(grad_ref)

    def pair(p, carry):
        for v in range(2):
            agg = pair_of(a_ref, p, v)
            emb, rinv = embed(weight_t, agg)
            d = coef * dot(scaled[1 - v], e_ref[p, 1 - v], NT)
            grad_ref[...] += split_dot(agg, back(emb, rinv, d))
        return carry

    lax.fori_loop(0, e_ref.shape[0], pair, 0, unroll=True)
    for v in range(2):
        d = coef * (both * full_n[1 - v] + sums_ref[v] * inverse[v])
        grad_ref[...] += split_dot(agg_n[v], back(emb_n[v], rinv_n[v], d))


def group_call(kernel, out_shape, inputs, scalars, name):
    return pl.pallas_call(
        kernel,
        out_shape=out_shape,
        in_specs=[pl.BlockSpec(memory_space=pltpu.SMEM)] * scalars
        + [pl.BlockSpec(memory_space=pltpu.VMEM)] * (inputs - scalars),
        compiler_params=pltpu.CompilerParams(**PARAMS),
        cost_estimate=pl.CostEstimate(flops=1 << 31, bytes_accessed=4 << 20, transcendentals=0),
        name=name,
    )


def swap(x, axis):
    return lax.all_to_all(x, axis, 0, 0, tiled=True)


def share(x, axis):
    return swap(jnp.broadcast_to(x[None], (lax.axis_size(axis),) + x.shape), axis)


def shift(x, axis, by):
    size = lax.axis_size(axis)
    return lax.ppermute(x, axis, [(i, (i + by) % size) for i in range(size)])


def around(x, pick, axis):
    return [pick(x, 0)] + [shift(pick(x, s), axis, s) for s in range(1, lax.axis_size(axis))]


def reduce_all(grad):
    rows, width = grad.shape
    planes = ("core",), ("y", "x")
    part = grad.reshape(-1, T)
    for axes in planes:
        got = swap(part.reshape(lax.axis_size(axes), -1, T), axes)
        part = jnp.sum(got, 0)
    part = jnp.sum(share(part, ("zl", "zh")), 0)
    for axes in planes[::-1]:
        part = share(part, axes).reshape(-1, T)
    return part.reshape(rows, width)


def packed(tiles, tile_pos, edge_keep, cols):
    slots = tile_pos.shape[0]
    held = tile_pos >= 0
    trow = jnp.where(held, tile_pos // cols, -1)
    tcol = jnp.where(held, tile_pos % cols, 0)
    meta = jnp.concatenate([trow[None], tcol[None], edge_keep], 0).astype(bf16)
    meta = jnp.pad(meta, ((0, 16 - meta.shape[0]), (0, T - slots)))
    return jnp.concatenate([tiles.reshape(slots * T, T), meta], 0)


def shards(features, weight, tiles, tile_pos, edge_keep, feature_keep, negatives):
    nodes, width = features.shape
    slots = tiles.shape[0]
    xsize, zsize = lax.axis_size("x"), lax.axis_size("zh")
    ysize = lax.axis_size("y")
    cols = xsize * zsize * lax.axis_size("core")
    zl = lax.axis_index("zl")
    place = jnp.stack([lax.axis_index("core"), zl])
    total = lax.axis_size(ROW) * cols * nodes
    pad = ZL * FS - width
    whole = lambda x, s: x

    turned = jnp.pad(features.T, ((0, pad), (0, 0))).reshape(ZL, 1, FS, nodes)
    sent = jnp.broadcast_to(turned, (ZL, zsize, FS, nodes)).reshape(ZL * zsize, FS, nodes)
    near = swap(sent, ("zl", "zh"))
    held = packed(tiles, tile_pos, edge_keep, cols)
    next_tiles = shift(held, "zl", 1)
    near, next_tiles = lax.optimization_barrier((near, next_tiles))
    own = share(near, "x")
    last_tiles = shift(held, "zl", 2)
    own, last_tiles = lax.optimization_barrier((own, last_tiles))
    all_tiles = [held, next_tiles, last_tiles]
    other = shift(own, "core", 1)
    metas = jnp.stack([x[slots * T : slots * T + 4, :slots] for x in all_tiles]).astype(jnp.int32)

    part = tile_sums(metas, place, own, other, all_tiles, cols, ZL * ysize)
    part, negatives = lax.optimization_barrier((part, negatives))
    got = swap(part, ROW)
    counts = count_negatives(negatives, ZL * ysize)
    got, counts = lax.optimization_barrier((got, counts))
    agg = jnp.sum(got.reshape(ZL, ysize, 2, FS, nodes).astype(f32), 1)
    agg = agg.transpose(1, 0, 2, 3).reshape(2, ZL * FS, nodes)[:, :width]
    agg = (agg * feature_keep.astype(f32)[:, :, None]).astype(bf16)
    agg, counts = lax.optimization_barrier((agg, counts))
    members = share(agg, "y")
    anchors = jnp.stack(around(agg, whole, "zl"))
    ahead = lambda x, s: lax.dynamic_index_in_dim(x, lax.rem(zl + s, ZL), 0, keepdims=False)
    counts = jnp.stack(around(counts.reshape(ZL, ysize, nodes, nodes), ahead, "zl"))

    weight_t = weight.T
    group = ZL * nodes
    rows = jax.ShapeDtypeStruct((8, group), f32)
    tot, terms, low = group_call(
        scores_kernel,
        (
            rows,
            jax.ShapeDtypeStruct((ysize // 2, 2, 2 * nodes, group), bf16),
            jax.ShapeDtypeStruct((ysize // 2, 2, width, 2 * nodes), bf16),
        ),
        5,
        1,
        "scores",
    )(place, anchors, members, weight_t, counts)
    tots = around(tot, whole, "zl")
    sums = group_call(
        pull_kernel, jax.ShapeDtypeStruct((2, width, group), f32), 2, 0, "pull"
    )(terms, low)
    mask = (jnp.arange(group) // nodes == zl).astype(f32)
    mask = jnp.broadcast_to(mask, (8, group))
    coef = 1.0 / (2.0 * tau * float(total) ** 0.5)
    loss, grad = group_call(
        functools.partial(grads_kernel, coef),
        (rows, jax.ShapeDtypeStruct((width, width), f32)),
        7 + ZL,
        1,
        "grads",
    )(place, anchors, members, weight_t, terms, sums, mask, *tots)
    node_loss = lax.dynamic_slice_in_dim(loss[0], zl * nodes, nodes)
    return node_loss, reduce_all(grad)


def solution(mesh):
    rows, cols = mesh.devices.shape
    fine = Mesh(mesh.devices.reshape(ZL, rows // ZL, cols // 8, 4, 2), ROW + COL)
    every = ROW + COL
    in_specs = (
        P(every, None),
        P(),
        P(every, None, None),
        P(every),
        P(None, every),
        P(),
        P(every, None),
    )
    out_specs = (P(every), P())
    return jax.shard_map(shards, mesh=fine, in_specs=in_specs, out_specs=out_specs, check_vma=False)
```

```python
import functools

import jax
import jax.numpy as jnp
from jax import lax
from jax.experimental import pallas as pl
from jax.experimental.pallas import tpu as pltpu
from jax.sharding import Mesh
from jax.sharding import PartitionSpec as P

tau = 0.5
eps = 1e-06
T = 128
ZL = 3
FS = 88
f32 = jnp.float32
bf16 = jnp.bfloat16
NT = (((1,), (1,)), ((), ()))
NN = (((1,), (0,)), ((), ()))
ROW = ("zl", "y")
COL = ("x", "zh", "core")
PARAMS = dict(vmem_limit_bytes=24 * 1024 * 1024)


def dot(a, b, dims):
    return lax.dot_general(a, b, dims, preferred_element_type=f32)


def counts_kernel(blocks, neg_ref, out_ref, acc_ref):
    nodes, negs = neg_ref.shape
    rows = 8 * ((blocks + 7) // 8)
    low_iota = lax.broadcasted_iota(jnp.int32, (T, negs), 0)
    high_iota = lax.broadcasted_iota(jnp.int32, (rows, negs), 0)

    def step(i, carry):
        base = pl.multiple_of(i * 8, 8)
        index = neg_ref[pl.ds(base, 8), :]
        low = index & (T - 1)
        high = index >> 7
        for j in range(0, 8, 2):
            low_hot, high_hot = (
                jnp.concatenate(
                    [jnp.where(part[j + i : j + i + 1, :] == iota, 1.0, 0.0) for i in range(2)], 0
                ).astype(bf16)
                for part, iota in ((low, low_iota), (high, high_iota))
            )
            found = dot(high_hot, low_hot, NT)
            for i in range(2):
                own = found[i * rows : (i + 1) * rows, i * T : (i + 1) * T]
                acc_ref[pl.ds(base + j + i, rows, stride=nodes), :] = own
        return carry

    lax.fori_loop(0, nodes // 8, step, 0)

    def turn(h, carry):
        block = acc_ref[pl.ds(pl.multiple_of(h * nodes, nodes), nodes), :]
        out_ref[h] = block.T.astype(jnp.int32).astype(jnp.int16)
        return carry

    lax.fori_loop(0, blocks, turn, 0)


def count_negatives(negatives, blocks):
    nodes = negatives.shape[0]
    rows = 8 * ((blocks + 7) // 8)
    return pl.pallas_call(
        functools.partial(counts_kernel, blocks),
        out_shape=jax.ShapeDtypeStruct((blocks, T, nodes), jnp.int16),
        scratch_shapes=[pltpu.VMEM((rows * nodes, T), f32)],
        compiler_params=pltpu.CompilerParams(**PARAMS),
        cost_estimate=pl.CostEstimate(
            flops=2 * 16 * nodes * T * T * 64, bytes_accessed=2 << 20, transcendentals=0
        ),
        name="counts",
    )(negatives)


def behind(place, s):
    return lax.rem(place + ZL - s, ZL)


def tiles_kernel(cols, meta_ref, place_ref, own_ref, other_ref, *refs):
    tile_refs, (out_ref, acc_ref) = refs[:ZL], refs[ZL:]
    zsize = own_ref.shape[1] // ZL
    slots = meta_ref.shape[2]
    acc_ref[...] = jnp.zeros_like(acc_ref)
    core, zl = place_ref[0], place_ref[1]
    for s in range(ZL):

        def few(i, carry, s=s):
            @pl.when(meta_ref[s, 0, i * 4] >= 0)
            def _():
                products = []
                for j in range(4):
                    k = i * 4 + j
                    tcol = meta_ref[s, 1, k]
                    chip = lax.div(tcol, 2)
                    at = lax.div(chip, zsize), behind(zl, s) * zsize + lax.rem(chip, zsize)
                    mine = lax.rem(tcol, 2) == core
                    rows = jnp.where(mine, own_ref[at], other_ref[at])
                    tile = tile_refs[s][pl.ds(pl.multiple_of(k * T, T), T), :]
                    products.append(dot(rows, tile, NT))
                for j in range(4):
                    k = i * 4 + j
                    trow = meta_ref[s, 0, k]
                    held = jnp.where(trow >= 0, 1, 0)
                    at = jnp.maximum(trow, 0)
                    for v in range(2):
                        kept = (held * meta_ref[s, 2 + v, k]).astype(f32)
                        acc_ref[at, v] += kept * products[j]

            return carry

        lax.fori_loop(0, slots // 4, few, 0)
    out_ref[...] = acc_ref[...].astype(bf16)


def tile_sums(meta, place, own, other, tiles, cols, blocks):
    shape = (blocks, 2, own.shape[2], T)
    return pl.pallas_call(
        functools.partial(tiles_kernel, cols),
        out_shape=jax.ShapeDtypeStruct(shape, bf16),
        in_specs=[pl.BlockSpec(memory_space=pltpu.SMEM)] * 2
        + [pl.BlockSpec(memory_space=pltpu.VMEM)] * (2 + ZL),
        scratch_shapes=[pltpu.VMEM(shape, f32)],
        compiler_params=pltpu.CompilerParams(**PARAMS),
        name="tile_sums",
    )(meta, place, own, other, *tiles)


def anchors_of(n_ref, zl, v):
    return jnp.concatenate([n_ref[behind(zl, z), v] for z in range(ZL)], 1)


def embed(weight_t, agg):
    z = dot(weight_t, agg, NN)
    rinv = lax.rsqrt(jnp.sum(z * z, 0, keepdims=True) + eps)
    return z * rinv, rinv


def pair_of(a_ref, p, v):
    return jnp.concatenate([a_ref[2 * p, v], a_ref[2 * p + 1, v]], 1)


def scores_kernel(place_ref, n_ref, a_ref, w_ref, c_ref, tot_ref, e_ref, low_ref):
    weight_t = w_ref[...]
    zl = place_ref[1]
    anchors = [embed(weight_t, anchors_of(n_ref, zl, v))[0].astype(bf16) for v in range(2)]
    tot_ref[...] = jnp.zeros_like(tot_ref)

    def pair(p, carry):
        count = jnp.concatenate(
            [
                jnp.concatenate([c_ref[behind(zl, z), 2 * p + i] for z in range(ZL)], 1)
                for i in range(2)
            ],
            0,
        )
        count = count.astype(jnp.int32).astype(f32)
        for v in range(2):
            emb = embed(weight_t, pair_of(a_ref, p, 1 - v))[0]
            low_ref[p, 1 - v] = emb.astype(bf16)
            score = dot(emb.T.astype(bf16), anchors[v], NN)
            term = count * jnp.exp(score * (1.0 / tau))
            e_ref[p, v] = term.astype(bf16)
            tot_ref[v : v + 1, :] += jnp.sum(term, 0, keepdims=True)
        return carry

    lax.fori_loop(0, e_ref.shape[0], pair, 0, unroll=True)


def pull_kernel(e_ref, low_ref, sums_ref):
    sums_ref[...] = jnp.zeros_like(sums_ref)

    def pair(p, carry):
        for v in range(2):
            sums_ref[v] += dot(low_ref[p, 1 - v], e_ref[p, v], NN)
        return carry

    lax.fori_loop(0, e_ref.shape[0], pair, 0, unroll=True)


def split_dot(agg, dz):
    high = dz.astype(bf16)
    low = (dz - high.astype(f32)).astype(bf16)
    return dot(agg, high, NT) + dot(agg, low, NT)


def grads_kernel(
    coef, place_ref, n_ref, a_ref, w_ref, e_ref, sums_ref, mask_ref, *refs
):
    *tot_refs, loss_ref, grad_ref = refs
    weight_t = w_ref[...]
    agg_n = [anchors_of(n_ref, place_ref[1], v) for v in range(2)]
    emb_n, rinv_n = zip(*[embed(weight_t, agg) for agg in agg_n])
    full_n = [emb.astype(bf16).astype(f32) for emb in emb_n]
    pos = jnp.sum(full_n[0] * full_n[1], 0, keepdims=True) * (1.0 / tau)
    own = jnp.exp(pos)
    tot = [own + sum(t[v : v + 1, :] for t in tot_refs) for v in range(2)]
    loss = 0.5 * ((jnp.log(tot[0]) - pos) + (jnp.log(tot[1]) - pos))
    loss_ref[...] = jnp.broadcast_to(loss, loss_ref.shape)
    inverse = [1.0 / t for t in tot]
    both = (own * inverse[0] + own * inverse[1] - 2.0) * mask_ref[0:1, :]
    scaled = [(full_n[v] * inverse[v]).astype(bf16) for v in range(2)]

    def back(emb, rinv, d):
        return (d - emb * jnp.sum(emb * d, 0, keepdims=True)) * rinv

    grad_ref[...] = jnp.zeros_like(grad_ref)

    def pair(p, carry):
        for v in range(2):
            agg = pair_of(a_ref, p, v)
            emb, rinv = embed(weight_t, agg)
            d = coef * dot(scaled[1 - v], e_ref[p, 1 - v], NT)
            grad_ref[...] += split_dot(agg, back(emb, rinv, d))
        return carry

    lax.fori_loop(0, e_ref.shape[0], pair, 0, unroll=True)
    for v in range(2):
        d = coef * (both * full_n[1 - v] + sums_ref[v] * inverse[v])
        grad_ref[...] += split_dot(agg_n[v], back(emb_n[v], rinv_n[v], d))


def group_call(kernel, out_shape, inputs, scalars, name):
    return pl.pallas_call(
        kernel,
        out_shape=out_shape,
        in_specs=[pl.BlockSpec(memory_space=pltpu.SMEM)] * scalars
        + [pl.BlockSpec(memory_space=pltpu.VMEM)] * (inputs - scalars),
        compiler_params=pltpu.CompilerParams(**PARAMS),
        cost_estimate=pl.CostEstimate(flops=1 << 31, bytes_accessed=4 << 20, transcendentals=0),
        name=name,
    )


def swap(x, axis):
    return lax.all_to_all(x, axis, 0, 0, tiled=True)


def share(x, axis):
    return swap(jnp.broadcast_to(x[None], (lax.axis_size(axis),) + x.shape), axis)


def shift(x, axis, by):
    size = lax.axis_size(axis)
    return lax.ppermute(x, axis, [(i, (i + by) % size) for i in range(size)])


def around(x, pick, axis):
    return [pick(x, 0)] + [shift(pick(x, s), axis, s) for s in range(1, lax.axis_size(axis))]


def reduce_all(grad):
    rows, width = grad.shape
    planes = ("core",), ("y", "x")
    part = grad.reshape(-1, T)
    for axes in planes:
        got = swap(part.reshape(lax.axis_size(axes), -1, T), axes)
        part = jnp.sum(got, 0)
    part = jnp.sum(share(part, ("zl", "zh")), 0)
    for axes in planes[::-1]:
        part = share(part, axes).reshape(-1, T)
    return part.reshape(rows, width)


def packed(tiles, tile_pos, edge_keep, cols):
    slots = tile_pos.shape[0]
    held = tile_pos >= 0
    trow = jnp.where(held, tile_pos // cols, -1)
    tcol = jnp.where(held, tile_pos % cols, 0)
    meta = jnp.concatenate([trow[None], tcol[None], edge_keep], 0).astype(bf16)
    meta = jnp.pad(meta, ((0, 16 - meta.shape[0]), (0, T - slots)))
    return jnp.concatenate([tiles.reshape(slots * T, T), meta], 0)


def shards(features, weight, tiles, tile_pos, edge_keep, feature_keep, negatives):
    nodes, width = features.shape
    slots = tiles.shape[0]
    xsize, zsize = lax.axis_size("x"), lax.axis_size("zh")
    ysize = lax.axis_size("y")
    cols = xsize * zsize * lax.axis_size("core")
    zl = lax.axis_index("zl")
    place = jnp.stack([lax.axis_index("core"), zl])
    total = lax.axis_size(ROW) * cols * nodes
    pad = ZL * FS - width
    whole = lambda x, s: x

    turned = jnp.pad(features.T, ((0, pad), (0, 0))).reshape(ZL, 1, FS, nodes)
    sent = jnp.broadcast_to(turned, (ZL, zsize, FS, nodes)).reshape(ZL * zsize, FS, nodes)
    near = swap(sent, ("zl", "zh"))
    held = packed(tiles, tile_pos, edge_keep, cols)
    next_tiles = shift(held, "zl", 1)
    counts = count_negatives(negatives, ZL * ysize)
    near, next_tiles, counts = lax.optimization_barrier((near, next_tiles, counts))
    own = share(near, "x")
    last_tiles = shift(held, "zl", 2)
    own, last_tiles = lax.optimization_barrier((own, last_tiles))
    all_tiles = [held, next_tiles, last_tiles]
    other = shift(own, "core", 1)
    metas = jnp.stack([x[slots * T : slots * T + 4, :slots] for x in all_tiles]).astype(jnp.int32)

    part = tile_sums(metas, place, own, other, all_tiles, cols, ZL * ysize)
    part, counts = lax.optimization_barrier((part, counts))
    got = swap(part, ROW)
    ahead = lambda x, s: lax.dynamic_index_in_dim(x, lax.rem(zl + s, ZL), 0, keepdims=False)
    counts = jnp.stack(around(counts.reshape(ZL, ysize, nodes, nodes), ahead, "zl"))
    got, counts = lax.optimization_barrier((got, counts))
    agg = jnp.sum(got.reshape(ZL, ysize, 2, FS, nodes).astype(f32), 1)
    agg = agg.transpose(1, 0, 2, 3).reshape(2, ZL * FS, nodes)[:, :width]
    agg = (agg * feature_keep.astype(f32)[:, :, None]).astype(bf16)
    members = share(agg, "y")
    anchors = jnp.stack(around(agg, whole, "zl"))

    weight_t = weight.T
    group = ZL * nodes
    rows = jax.ShapeDtypeStruct((8, group), f32)
    tot, terms, low = group_call(
        scores_kernel,
        (
            rows,
            jax.ShapeDtypeStruct((ysize // 2, 2, 2 * nodes, group), bf16),
            jax.ShapeDtypeStruct((ysize // 2, 2, width, 2 * nodes), bf16),
        ),
        5,
        1,
        "scores",
    )(place, anchors, members, weight_t, counts)
    tots = around(tot, whole, "zl")
    sums = group_call(
        pull_kernel, jax.ShapeDtypeStruct((2, width, group), f32), 2, 0, "pull"
    )(terms, low)
    mask = (jnp.arange(group) // nodes == zl).astype(f32)
    mask = jnp.broadcast_to(mask, (8, group))
    coef = 1.0 / (2.0 * tau * float(total) ** 0.5)
    loss, grad = group_call(
        functools.partial(grads_kernel, coef),
        (rows, jax.ShapeDtypeStruct((width, width), f32)),
        7 + ZL,
        1,
        "grads",
    )(place, anchors, members, weight_t, terms, sums, mask, *tots)
    node_loss = lax.dynamic_slice_in_dim(loss[0], zl * nodes, nodes)
    return node_loss, reduce_all(grad)


def solution(mesh):
    rows, cols = mesh.devices.shape
    fine = Mesh(mesh.devices.reshape(ZL, rows // ZL, cols // 8, 4, 2), ROW + COL)
    every = ROW + COL
    in_specs = (
        P(every, None),
        P(),
        P(every, None, None),
        P(every),
        P(None, every),
        P(),
        P(every, None),
    )
    out_specs = (P(every), P())
    return jax.shard_map(shards, mesh=fine, in_specs=in_specs, out_specs=out_specs, check_vma=False)
```

```python
import functools

import jax
import jax.numpy as jnp
from jax import lax
from jax.experimental import pallas as pl
from jax.experimental.pallas import tpu as pltpu
from jax.sharding import Mesh
from jax.sharding import PartitionSpec as P

tau = 0.5
eps = 1e-06
T = 128
ZL = 3
FS = 88
f32 = jnp.float32
bf16 = jnp.bfloat16
NT = (((1,), (1,)), ((), ()))
NN = (((1,), (0,)), ((), ()))
ROW = ("zl", "y")
COL = ("x", "zh", "core")
PARAMS = dict(vmem_limit_bytes=24 * 1024 * 1024)


def dot(a, b, dims):
    return lax.dot_general(a, b, dims, preferred_element_type=f32)


def counts_kernel(blocks, neg_ref, out_ref, acc_ref):
    nodes, negs = neg_ref.shape
    rows = 8 * ((blocks + 7) // 8)
    low_iota = lax.broadcasted_iota(jnp.int32, (T, negs), 0)
    high_iota = lax.broadcasted_iota(jnp.int32, (rows, negs), 0)

    def step(i, carry):
        base = pl.multiple_of(i * 8, 8)
        index = neg_ref[pl.ds(base, 8), :]
        low = index & (T - 1)
        high = index >> 7
        for j in range(0, 8, 2):
            low_hot, high_hot = (
                jnp.concatenate(
                    [jnp.where(part[j + i : j + i + 1, :] == iota, 1.0, 0.0) for i in range(2)], 0
                ).astype(bf16)
                for part, iota in ((low, low_iota), (high, high_iota))
            )
            found = dot(high_hot, low_hot, NT)
            for i in range(2):
                own = found[i * rows : (i + 1) * rows, i * T : (i + 1) * T]
                acc_ref[pl.ds(base + j + i, rows, stride=nodes), :] = own
        return carry

    lax.fori_loop(0, nodes // 8, step, 0)

    def turn(h, carry):
        block = acc_ref[pl.ds(pl.multiple_of(h * nodes, nodes), nodes), :]
        out_ref[h] = block.T.astype(jnp.int32).astype(jnp.int16)
        return carry

    lax.fori_loop(0, blocks, turn, 0)


def count_negatives(negatives, blocks):
    nodes = negatives.shape[0]
    rows = 8 * ((blocks + 7) // 8)
    return pl.pallas_call(
        functools.partial(counts_kernel, blocks),
        out_shape=jax.ShapeDtypeStruct((blocks, T, nodes), jnp.int16),
        scratch_shapes=[pltpu.VMEM((rows * nodes, T), f32)],
        compiler_params=pltpu.CompilerParams(**PARAMS),
        cost_estimate=pl.CostEstimate(
            flops=2 * 16 * nodes * T * T * 64, bytes_accessed=2 << 20, transcendentals=0
        ),
        name="counts",
    )(negatives)


def behind(place, s):
    return lax.rem(place + ZL - s, ZL)


def tiles_kernel(cols, meta_ref, place_ref, own_ref, other_ref, *refs):
    tile_refs, (out_ref, acc_ref) = refs[:ZL], refs[ZL:]
    zsize = own_ref.shape[1] // ZL
    slots = meta_ref.shape[2]
    acc_ref[...] = jnp.zeros_like(acc_ref)
    core, zl = place_ref[0], place_ref[1]
    for s in range(ZL):

        def few(i, carry, s=s):
            @pl.when(meta_ref[s, 0, i * 4] >= 0)
            def _():
                products = []
                for j in range(4):
                    k = i * 4 + j
                    tcol = meta_ref[s, 1, k]
                    chip = lax.div(tcol, 2)
                    at = lax.div(chip, zsize), behind(zl, s) * zsize + lax.rem(chip, zsize)
                    mine = lax.rem(tcol, 2) == core
                    rows = jnp.where(mine, own_ref[at], other_ref[at])
                    tile = tile_refs[s][pl.ds(pl.multiple_of(k * T, T), T), :]
                    products.append(dot(rows, tile, NT))
                for j in range(4):
                    k = i * 4 + j
                    trow = meta_ref[s, 0, k]
                    held = jnp.where(trow >= 0, 1, 0)
                    at = jnp.maximum(trow, 0)
                    for v in range(2):
                        kept = (held * meta_ref[s, 2 + v, k]).astype(f32)
                        acc_ref[at, v] += kept * products[j]

            return carry

        lax.fori_loop(0, slots // 4, few, 0)
    out_ref[...] = acc_ref[...].astype(bf16)


def tile_sums(meta, place, own, other, tiles, cols, blocks):
    shape = (blocks, 2, own.shape[2], T)
    return pl.pallas_call(
        functools.partial(tiles_kernel, cols),
        out_shape=jax.ShapeDtypeStruct(shape, bf16),
        in_specs=[pl.BlockSpec(memory_space=pltpu.SMEM)] * 2
        + [pl.BlockSpec(memory_space=pltpu.VMEM)] * (2 + ZL),
        scratch_shapes=[pltpu.VMEM(shape, f32)],
        compiler_params=pltpu.CompilerParams(**PARAMS),
        name="tile_sums",
    )(meta, place, own, other, *tiles)


def anchors_of(n_ref, zl, v):
    return jnp.concatenate([n_ref[behind(zl, z), v] for z in range(ZL)], 1)


def embed(weight_t, agg):
    z = dot(weight_t, agg, NN)
    rinv = lax.rsqrt(jnp.sum(z * z, 0, keepdims=True) + eps)
    return z * rinv, rinv


def pair_of(a_ref, p, v):
    return jnp.concatenate([a_ref[2 * p, v], a_ref[2 * p + 1, v]], 1)


def scores_kernel(place_ref, n_ref, a_ref, w_ref, c_ref, tot_ref, e_ref, low_ref):
    weight_t = w_ref[...]
    zl = place_ref[1]
    anchors = [embed(weight_t, anchors_of(n_ref, zl, v))[0].astype(bf16) for v in range(2)]
    tot_ref[...] = jnp.zeros_like(tot_ref)

    def pair(p, carry):
        count = jnp.concatenate(
            [
                jnp.concatenate([c_ref[behind(zl, z), 2 * p + i] for z in range(ZL)], 1)
                for i in range(2)
            ],
            0,
        )
        count = count.astype(jnp.int32).astype(f32)
        for v in range(2):
            emb = embed(weight_t, pair_of(a_ref, p, 1 - v))[0]
            low_ref[p, 1 - v] = emb.astype(bf16)
            score = dot(emb.T.astype(bf16), anchors[v], NN)
            term = count * jnp.exp(score * (1.0 / tau))
            e_ref[p, v] = term.astype(bf16)
            tot_ref[v : v + 1, :] += jnp.sum(term, 0, keepdims=True)
        return carry

    lax.fori_loop(0, e_ref.shape[0], pair, 0, unroll=True)


def pull_kernel(e_ref, low_ref, sums_ref):
    sums_ref[...] = jnp.zeros_like(sums_ref)

    def pair(p, carry):
        for v in range(2):
            sums_ref[v] += dot(low_ref[p, 1 - v], e_ref[p, v], NN)
        return carry

    lax.fori_loop(0, e_ref.shape[0], pair, 0, unroll=True)


def split_dot(agg, dz):
    high = dz.astype(bf16)
    low = (dz - high.astype(f32)).astype(bf16)
    return dot(agg, high, NT) + dot(agg, low, NT)


def grads_kernel(
    coef, place_ref, n_ref, a_ref, w_ref, e_ref, sums_ref, mask_ref, *refs
):
    *tot_refs, loss_ref, grad_ref = refs
    weight_t = w_ref[...]
    agg_n = [anchors_of(n_ref, place_ref[1], v) for v in range(2)]
    emb_n, rinv_n = zip(*[embed(weight_t, agg) for agg in agg_n])
    full_n = [emb.astype(bf16).astype(f32) for emb in emb_n]
    pos = jnp.sum(full_n[0] * full_n[1], 0, keepdims=True) * (1.0 / tau)
    own = jnp.exp(pos)
    tot = [own + sum(t[v : v + 1, :] for t in tot_refs) for v in range(2)]
    loss = 0.5 * ((jnp.log(tot[0]) - pos) + (jnp.log(tot[1]) - pos))
    loss_ref[...] = jnp.broadcast_to(loss, loss_ref.shape)
    inverse = [1.0 / t for t in tot]
    both = (own * inverse[0] + own * inverse[1] - 2.0) * mask_ref[0:1, :]
    scaled = [(full_n[v] * inverse[v]).astype(bf16) for v in range(2)]

    def back(emb, rinv, d):
        return (d - emb * jnp.sum(emb * d, 0, keepdims=True)) * rinv

    grad_ref[...] = jnp.zeros_like(grad_ref)

    def pair(p, carry):
        for v in range(2):
            agg = pair_of(a_ref, p, v)
            emb, rinv = embed(weight_t, agg)
            d = coef * dot(scaled[1 - v], e_ref[p, 1 - v], NT)
            grad_ref[...] += split_dot(agg, back(emb, rinv, d))
        return carry

    lax.fori_loop(0, e_ref.shape[0], pair, 0, unroll=True)
    for v in range(2):
        d = coef * (both * full_n[1 - v] + sums_ref[v] * inverse[v])
        grad_ref[...] += split_dot(agg_n[v], back(emb_n[v], rinv_n[v], d))


def group_call(kernel, out_shape, inputs, scalars, name):
    return pl.pallas_call(
        kernel,
        out_shape=out_shape,
        in_specs=[pl.BlockSpec(memory_space=pltpu.SMEM)] * scalars
        + [pl.BlockSpec(memory_space=pltpu.VMEM)] * (inputs - scalars),
        compiler_params=pltpu.CompilerParams(**PARAMS),
        cost_estimate=pl.CostEstimate(flops=1 << 31, bytes_accessed=4 << 20, transcendentals=0),
        name=name,
    )


def swap(x, axis):
    return lax.all_to_all(x, axis, 0, 0, tiled=True)


def share(x, axis):
    return swap(jnp.broadcast_to(x[None], (lax.axis_size(axis),) + x.shape), axis)


def shift(x, axis, by):
    size = lax.axis_size(axis)
    return lax.ppermute(x, axis, [(i, (i + by) % size) for i in range(size)])


def around(x, pick, axis):
    return [pick(x, 0)] + [shift(pick(x, s), axis, s) for s in range(1, lax.axis_size(axis))]


def reduce_all(grad):
    rows, width = grad.shape
    plane = ("y", "x")
    part = jnp.sum(swap(grad.reshape(lax.axis_size(plane), -1, width), plane), 0)
    part = part + shift(part, "core", 1)
    part = jnp.sum(share(part, ("zl", "zh")), 0)
    return share(part, plane).reshape(rows, width)


def packed(tiles, tile_pos, edge_keep, cols):
    slots = tile_pos.shape[0]
    held = tile_pos >= 0
    trow = jnp.where(held, tile_pos // cols, -1)
    tcol = jnp.where(held, tile_pos % cols, 0)
    meta = jnp.concatenate([trow[None], tcol[None], edge_keep], 0).astype(bf16)
    meta = jnp.pad(meta, ((0, 16 - meta.shape[0]), (0, T - slots)))
    return jnp.concatenate([tiles.reshape(slots * T, T), meta], 0)


def shards(features, weight, tiles, tile_pos, edge_keep, feature_keep, negatives):
    nodes, width = features.shape
    slots = tiles.shape[0]
    xsize, zsize = lax.axis_size("x"), lax.axis_size("zh")
    ysize = lax.axis_size("y")
    cols = xsize * zsize * lax.axis_size("core")
    zl = lax.axis_index("zl")
    place = jnp.stack([lax.axis_index("core"), zl])
    total = lax.axis_size(ROW) * cols * nodes
    pad = ZL * FS - width
    whole = lambda x, s: x

    turned = jnp.pad(features.T, ((0, pad), (0, 0))).reshape(ZL, 1, FS, nodes)
    sent = jnp.broadcast_to(turned, (ZL, zsize, FS, nodes)).reshape(ZL * zsize, FS, nodes)
    near = swap(sent, ("zl", "zh"))
    held = packed(tiles, tile_pos, edge_keep, cols)
    next_tiles = shift(held, "zl", 1)
    near, next_tiles = lax.optimization_barrier((near, next_tiles))
    own = share(near, "x")
    last_tiles = shift(held, "zl", 2)
    own, last_tiles = lax.optimization_barrier((own, last_tiles))
    all_tiles = [held, next_tiles, last_tiles]
    other = shift(own, "core", 1)
    metas = jnp.stack([x[slots * T : slots * T + 4, :slots] for x in all_tiles]).astype(jnp.int32)

    part = tile_sums(metas, place, own, other, all_tiles, cols, ZL * ysize)
    part, negatives = lax.optimization_barrier((part, negatives))
    got = swap(part, ROW)
    counts = count_negatives(negatives, ZL * ysize)
    got, counts = lax.optimization_barrier((got, counts))
    agg = jnp.sum(got.reshape(ZL, ysize, 2, FS, nodes).astype(f32), 1)
    agg = agg.transpose(1, 0, 2, 3).reshape(2, ZL * FS, nodes)[:, :width]
    agg = (agg * feature_keep.astype(f32)[:, :, None]).astype(bf16)
    agg, counts = lax.optimization_barrier((agg, counts))
    members = share(agg, "y")
    anchors = jnp.stack(around(agg, whole, "zl"))
    ahead = lambda x, s: lax.dynamic_index_in_dim(x, lax.rem(zl + s, ZL), 0, keepdims=False)
    counts = jnp.stack(around(counts.reshape(ZL, ysize, nodes, nodes), ahead, "zl"))

    weight_t = weight.T
    group = ZL * nodes
    rows = jax.ShapeDtypeStruct((8, group), f32)
    tot, terms, low = group_call(
        scores_kernel,
        (
            rows,
            jax.ShapeDtypeStruct((ysize // 2, 2, 2 * nodes, group), bf16),
            jax.ShapeDtypeStruct((ysize // 2, 2, width, 2 * nodes), bf16),
        ),
        5,
        1,
        "scores",
    )(place, anchors, members, weight_t, counts)
    tots = around(tot, whole, "zl")
    sums = group_call(
        pull_kernel, jax.ShapeDtypeStruct((2, width, group), f32), 2, 0, "pull"
    )(terms, low)
    mask = (jnp.arange(group) // nodes == zl).astype(f32)
    mask = jnp.broadcast_to(mask, (8, group))
    coef = 1.0 / (2.0 * tau * float(total) ** 0.5)
    loss, grad = group_call(
        functools.partial(grads_kernel, coef),
        (rows, jax.ShapeDtypeStruct((width, width), f32)),
        7 + ZL,
        1,
        "grads",
    )(place, anchors, members, weight_t, terms, sums, mask, *tots)
    node_loss = lax.dynamic_slice_in_dim(loss[0], zl * nodes, nodes)
    return node_loss, reduce_all(grad)


def solution(mesh):
    rows, cols = mesh.devices.shape
    fine = Mesh(mesh.devices.reshape(ZL, rows // ZL, cols // 8, 4, 2), ROW + COL)
    every = ROW + COL
    in_specs = (
        P(every, None),
        P(),
        P(every, None, None),
        P(every),
        P(None, every),
        P(),
        P(every, None),
    )
    out_specs = (P(every), P())
    return jax.shard_map(shards, mesh=fine, in_specs=in_specs, out_specs=out_specs, check_vma=False)
```

```python
import functools

import jax
import jax.numpy as jnp
from jax import lax
from jax.experimental import pallas as pl
from jax.experimental.pallas import tpu as pltpu
from jax.sharding import Mesh
from jax.sharding import PartitionSpec as P

tau = 0.5
eps = 1e-06
T = 128
ZL = 3
EARLY = 8
FS = 88
f32 = jnp.float32
bf16 = jnp.bfloat16
NT = (((1,), (1,)), ((), ()))
NN = (((1,), (0,)), ((), ()))
ROW = ("zl", "y")
COL = ("x", "zh", "core")
PARAMS = dict(vmem_limit_bytes=24 * 1024 * 1024)


def dot(a, b, dims):
    return lax.dot_general(a, b, dims, preferred_element_type=f32)


def counts_kernel(blocks, neg_ref, out_ref, acc_ref):
    nodes, negs = neg_ref.shape
    rows = 8 * ((blocks + 7) // 8)
    low_iota = lax.broadcasted_iota(jnp.int32, (T, negs), 0)
    high_iota = lax.broadcasted_iota(jnp.int32, (rows, negs), 0)

    def step(i, carry):
        base = pl.multiple_of(i * 8, 8)
        index = neg_ref[pl.ds(base, 8), :]
        low = index & (T - 1)
        high = index >> 7
        for j in range(0, 8, 2):
            low_hot, high_hot = (
                jnp.concatenate(
                    [jnp.where(part[j + i : j + i + 1, :] == iota, 1.0, 0.0) for i in range(2)], 0
                ).astype(bf16)
                for part, iota in ((low, low_iota), (high, high_iota))
            )
            found = dot(high_hot, low_hot, NT)
            for i in range(2):
                own = found[i * rows : (i + 1) * rows, i * T : (i + 1) * T]
                acc_ref[pl.ds(base + j + i, rows, stride=nodes), :] = own
        return carry

    lax.fori_loop(0, nodes // 8, step, 0)

    def turn(h, carry):
        block = acc_ref[pl.ds(pl.multiple_of(h * nodes, nodes), nodes), :]
        out_ref[h] = block.T.astype(jnp.int32).astype(jnp.int16)
        return carry

    lax.fori_loop(0, blocks, turn, 0)


def count_negatives(negatives, blocks):
    nodes = negatives.shape[0]
    rows = 8 * ((blocks + 7) // 8)
    return pl.pallas_call(
        functools.partial(counts_kernel, blocks),
        out_shape=jax.ShapeDtypeStruct((blocks, T, nodes), jnp.int16),
        scratch_shapes=[pltpu.VMEM((rows * nodes, T), f32)],
        compiler_params=pltpu.CompilerParams(**PARAMS),
        cost_estimate=pl.CostEstimate(
            flops=2 * 16 * nodes * T * T * 64, bytes_accessed=2 << 20, transcendentals=0
        ),
        name="counts",
    )(negatives)


def behind(place, s):
    return lax.rem(place + ZL - s, ZL)


def tiles_kernel(cols, meta_ref, place_ref, own_ref, other_ref, *refs):
    tile_refs, (out_ref, acc_ref) = refs[: 2 * ZL], refs[2 * ZL :]
    zsize = own_ref.shape[1] // ZL
    slots = meta_ref.shape[2]
    acc_ref[...] = jnp.zeros_like(acc_ref)
    core, zl = place_ref[0], place_ref[1]
    for s in range(ZL):
        for i in range(slots // 4):
            late = i * 4 >= EARLY

            @pl.when(meta_ref[s, 0, i * 4] >= 0)
            def _(s=s, i=i, late=late):
                products = []
                for j in range(4):
                    k = i * 4 + j
                    tcol = meta_ref[s, 1, k]
                    chip = lax.div(tcol, 2)
                    at = lax.div(chip, zsize), behind(zl, s) * zsize + lax.rem(chip, zsize)
                    mine = lax.rem(tcol, 2) == core
                    rows = jnp.where(mine, own_ref[at], other_ref[at])
                    start = (k - EARLY if late else k) * T
                    tile = tile_refs[2 * s + late][start : start + T, :]
                    products.append(dot(rows, tile, NT))
                for j in range(4):
                    k = i * 4 + j
                    trow = meta_ref[s, 0, k]
                    held = jnp.where(trow >= 0, 1, 0)
                    at = jnp.maximum(trow, 0)
                    for v in range(2):
                        kept = (held * meta_ref[s, 2 + v, k]).astype(f32)
                        acc_ref[at, v] += kept * products[j]

    out_ref[...] = acc_ref[...].astype(bf16)


def cut_kernel(x_ref, out_ref):
    copies = out_ref.shape[0] // ZL
    turned = x_ref[...].astype(f32).T
    for s in range(ZL):
        rows = turned[s * FS : (s + 1) * FS]
        if rows.shape[0] < FS:
            rows = jnp.concatenate([rows, jnp.zeros((FS - rows.shape[0], T), f32)], 0)
        for i in range(copies):
            out_ref[s * copies + i] = rows.astype(bf16)


def cut_features(features, copies):
    return pl.pallas_call(
        cut_kernel,
        out_shape=jax.ShapeDtypeStruct((ZL * copies, FS, features.shape[0]), bf16),
        name="cut_features",
    )(features)


def tile_sums(meta, place, own, other, tiles, cols, blocks):
    shape = (blocks, 2, own.shape[2], T)
    return pl.pallas_call(
        functools.partial(tiles_kernel, cols),
        out_shape=jax.ShapeDtypeStruct(shape, bf16),
        in_specs=[pl.BlockSpec(memory_space=pltpu.SMEM)] * 2
        + [pl.BlockSpec(memory_space=pltpu.VMEM)] * (2 + 2 * ZL),
        scratch_shapes=[pltpu.VMEM(shape, f32)],
        compiler_params=pltpu.CompilerParams(**PARAMS),
        name="tile_sums",
    )(meta, place, own, other, *tiles)


def anchors_of(n_ref, zl, v):
    return jnp.concatenate([n_ref[behind(zl, z), v] for z in range(ZL)], 1)


def embed(weight_t, agg):
    z = dot(weight_t, agg, NN)
    rinv = lax.rsqrt(jnp.sum(z * z, 0, keepdims=True) + eps)
    return z * rinv, rinv


def pair_of(a_ref, p, v):
    return jnp.concatenate([a_ref[2 * p, v], a_ref[2 * p + 1, v]], 1)


def scores_kernel(place_ref, n_ref, a_ref, w_ref, c_ref, tot_ref, e_ref, low_ref):
    weight_t = w_ref[...]
    zl = place_ref[1]
    anchors = [embed(weight_t, anchors_of(n_ref, zl, v))[0].astype(bf16) for v in range(2)]
    tot_ref[...] = jnp.zeros_like(tot_ref)

    def pair(p, carry):
        count = jnp.concatenate(
            [
                jnp.concatenate([c_ref[behind(zl, z), 2 * p + i] for z in range(ZL)], 1)
                for i in range(2)
            ],
            0,
        )
        count = count.astype(jnp.int32).astype(f32)
        for v in range(2):
            emb = embed(weight_t, pair_of(a_ref, p, 1 - v))[0]
            low_ref[p, 1 - v] = emb.astype(bf16)
            score = dot(emb.T.astype(bf16), anchors[v], NN)
            term = count * jnp.exp(score * (1.0 / tau))
            e_ref[p, v] = term.astype(bf16)
            tot_ref[v : v + 1, :] += jnp.sum(term, 0, keepdims=True)
        return carry

    lax.fori_loop(0, e_ref.shape[0], pair, 0, unroll=True)


def pull_kernel(e_ref, low_ref, sums_ref):
    sums_ref[...] = jnp.zeros_like(sums_ref)

    def pair(p, carry):
        for v in range(2):
            sums_ref[v] += dot(low_ref[p, 1 - v], e_ref[p, v], NN)
        return carry

    lax.fori_loop(0, e_ref.shape[0], pair, 0, unroll=True)


def split_dot(agg, dz):
    high = dz.astype(bf16)
    low = (dz - high.astype(f32)).astype(bf16)
    return dot(agg, high, NT) + dot(agg, low, NT)


def grads_kernel(
    coef, place_ref, n_ref, a_ref, w_ref, e_ref, sums_ref, mask_ref, *refs
):
    *tot_refs, loss_ref, grad_ref = refs
    weight_t = w_ref[...]
    agg_n = [anchors_of(n_ref, place_ref[1], v) for v in range(2)]
    emb_n, rinv_n = zip(*[embed(weight_t, agg) for agg in agg_n])
    full_n = [emb.astype(bf16).astype(f32) for emb in emb_n]
    pos = jnp.sum(full_n[0] * full_n[1], 0, keepdims=True) * (1.0 / tau)
    own = jnp.exp(pos)
    tot = [own + sum(t[v : v + 1, :] for t in tot_refs) for v in range(2)]
    loss = 0.5 * ((jnp.log(tot[0]) - pos) + (jnp.log(tot[1]) - pos))
    loss_ref[...] = jnp.broadcast_to(loss, loss_ref.shape)
    inverse = [1.0 / t for t in tot]
    both = (own * inverse[0] + own * inverse[1] - 2.0) * mask_ref[0:1, :]
    scaled = [(full_n[v] * inverse[v]).astype(bf16) for v in range(2)]

    def back(emb, rinv, d):
        return (d - emb * jnp.sum(emb * d, 0, keepdims=True)) * rinv

    grad_ref[...] = jnp.zeros_like(grad_ref)

    def pair(p, carry):
        for v in range(2):
            agg = pair_of(a_ref, p, v)
            emb, rinv = embed(weight_t, agg)
            d = coef * dot(scaled[1 - v], e_ref[p, 1 - v], NT)
            grad_ref[...] += split_dot(agg, back(emb, rinv, d))
        return carry

    lax.fori_loop(0, e_ref.shape[0], pair, 0, unroll=True)
    for v in range(2):
        d = coef * (both * full_n[1 - v] + sums_ref[v] * inverse[v])
        grad_ref[...] += split_dot(agg_n[v], back(emb_n[v], rinv_n[v], d))


def group_call(kernel, out_shape, inputs, scalars, name):
    return pl.pallas_call(
        kernel,
        out_shape=out_shape,
        in_specs=[pl.BlockSpec(memory_space=pltpu.SMEM)] * scalars
        + [pl.BlockSpec(memory_space=pltpu.VMEM)] * (inputs - scalars),
        compiler_params=pltpu.CompilerParams(**PARAMS),
        cost_estimate=pl.CostEstimate(flops=1 << 31, bytes_accessed=4 << 20, transcendentals=0),
        name=name,
    )


def swap(x, axis):
    return lax.all_to_all(x, axis, 0, 0, tiled=True)


def share(x, axis):
    return swap(jnp.broadcast_to(x[None], (lax.axis_size(axis),) + x.shape), axis)


def shift(x, axis, by):
    size = lax.axis_size(axis)
    return lax.ppermute(x, axis, [(i, (i + by) % size) for i in range(size)])


def around(x, pick, axis):
    return [pick(x, 0)] + [shift(pick(x, s), axis, s) for s in range(1, lax.axis_size(axis))]


def reduce_all(grad):
    rows, width = grad.shape
    plane = ("y", "x")
    part = jnp.sum(swap(grad.reshape(lax.axis_size(plane), -1, width), plane), 0)
    part = part + shift(part, "core", 1)
    part = jnp.sum(share(part, ("zl", "zh")), 0)
    return share(part, plane).reshape(rows, width)


def packed(tiles, tile_pos, edge_keep, cols):
    slots = tile_pos.shape[0]
    held = tile_pos >= 0
    trow = jnp.where(held, tile_pos // cols, -1)
    tcol = jnp.where(held, tile_pos % cols, 0)
    meta = jnp.concatenate([trow[None], tcol[None], edge_keep], 0).astype(bf16)
    meta = jnp.pad(meta, ((0, 16 - meta.shape[0]), (0, T - slots)))
    return jnp.concatenate([tiles[EARLY:].reshape((slots - EARLY) * T, T), meta], 0)


def shards(features, weight, tiles, tile_pos, edge_keep, feature_keep, negatives):
    nodes, width = features.shape
    slots = tiles.shape[0]
    xsize, zsize = lax.axis_size("x"), lax.axis_size("zh")
    ysize = lax.axis_size("y")
    cols = xsize * zsize * lax.axis_size("core")
    zl = lax.axis_index("zl")
    place = jnp.stack([lax.axis_index("core"), zl])
    total = lax.axis_size(ROW) * cols * nodes
    whole = lambda x, s: x

    near = swap(cut_features(features, zsize), ("zl", "zh"))
    some, rest = tiles[:EARLY].reshape(EARLY * T, T), packed(tiles, tile_pos, edge_keep, cols)
    next_some = shift(some, "zl", 1)
    near, next_some = lax.optimization_barrier((near, next_some))
    own = share(near, "x")
    next_rest, last_some, last_rest = (
        shift(rest, "zl", 1),
        shift(some, "zl", 2),
        shift(rest, "zl", 2),
    )
    own, next_rest, last_some, last_rest = lax.optimization_barrier(
        (own, next_rest, last_some, last_rest)
    )
    all_tiles = [some, rest, next_some, next_rest, last_some, last_rest]
    other = shift(own, "core", 1)
    late = (slots - EARLY) * T
    metas = jnp.stack([x[late : late + 4, :slots] for x in all_tiles[1::2]]).astype(jnp.int32)

    part = tile_sums(metas, place, own, other, all_tiles, cols, ZL * ysize)
    part, negatives = lax.optimization_barrier((part, negatives))
    got = swap(part, ROW)
    counts = count_negatives(negatives, ZL * ysize)
    got, counts = lax.optimization_barrier((got, counts))
    agg = jnp.sum(got.reshape(ZL, ysize, 2, FS, nodes).astype(f32), 1)
    agg = agg.transpose(1, 0, 2, 3).reshape(2, ZL * FS, nodes)[:, :width]
    agg = (agg * feature_keep.astype(f32)[:, :, None]).astype(bf16)
    agg, counts = lax.optimization_barrier((agg, counts))
    members = share(agg, "y")
    anchors = jnp.stack(around(agg, whole, "zl"))
    ahead = lambda x, s: lax.dynamic_index_in_dim(x, lax.rem(zl + s, ZL), 0, keepdims=False)
    counts = jnp.stack(around(counts.reshape(ZL, ysize, nodes, nodes), ahead, "zl"))

    weight_t = weight.T
    group = ZL * nodes
    rows = jax.ShapeDtypeStruct((8, group), f32)
    tot, terms, low = group_call(
        scores_kernel,
        (
            rows,
            jax.ShapeDtypeStruct((ysize // 2, 2, 2 * nodes, group), bf16),
            jax.ShapeDtypeStruct((ysize // 2, 2, width, 2 * nodes), bf16),
        ),
        5,
        1,
        "scores",
    )(place, anchors, members, weight_t, counts)
    tots = around(tot, whole, "zl")
    sums = group_call(
        pull_kernel, jax.ShapeDtypeStruct((2, width, group), f32), 2, 0, "pull"
    )(terms, low)
    mask = (jnp.arange(group) // nodes == zl).astype(f32)
    mask = jnp.broadcast_to(mask, (8, group))
    coef = 1.0 / (2.0 * tau * float(total) ** 0.5)
    loss, grad = group_call(
        functools.partial(grads_kernel, coef),
        (rows, jax.ShapeDtypeStruct((width, width), f32)),
        7 + ZL,
        1,
        "grads",
    )(place, anchors, members, weight_t, terms, sums, mask, *tots)
    node_loss = lax.dynamic_slice_in_dim(loss[0], zl * nodes, nodes)
    return node_loss, reduce_all(grad)


def solution(mesh):
    rows, cols = mesh.devices.shape
    fine = Mesh(mesh.devices.reshape(ZL, rows // ZL, cols // 8, 4, 2), ROW + COL)
    every = ROW + COL
    in_specs = (
        P(every, None),
        P(),
        P(every, None, None),
        P(every),
        P(None, every),
        P(),
        P(every, None),
    )
    out_specs = (P(every), P())
    return jax.shard_map(shards, mesh=fine, in_specs=in_specs, out_specs=out_specs, check_vma=False)
```

```python
import functools

import jax
import jax.numpy as jnp
from jax import lax
from jax.experimental import pallas as pl
from jax.experimental.pallas import tpu as pltpu
from jax.sharding import Mesh
from jax.sharding import PartitionSpec as P

tau = 0.5
eps = 1e-06
T = 128
ZL = 3
EARLY = 4
FS = 88
f32 = jnp.float32
bf16 = jnp.bfloat16
NT = (((1,), (1,)), ((), ()))
NN = (((1,), (0,)), ((), ()))
ROW = ("zl", "y")
COL = ("x", "zh", "core")
PARAMS = dict(vmem_limit_bytes=24 * 1024 * 1024)


def dot(a, b, dims):
    return lax.dot_general(a, b, dims, preferred_element_type=f32)


def counts_kernel(blocks, neg_ref, out_ref, acc_ref):
    nodes, negs = neg_ref.shape
    rows = 8 * ((blocks + 7) // 8)
    low_iota = lax.broadcasted_iota(jnp.int32, (T, negs), 0)
    high_iota = lax.broadcasted_iota(jnp.int32, (rows, negs), 0)

    def step(i, carry):
        base = pl.multiple_of(i * 8, 8)
        index = neg_ref[pl.ds(base, 8), :]
        low = index & (T - 1)
        high = index >> 7
        for j in range(0, 8, 2):
            low_hot, high_hot = (
                jnp.concatenate(
                    [jnp.where(part[j + i : j + i + 1, :] == iota, 1.0, 0.0) for i in range(2)], 0
                ).astype(bf16)
                for part, iota in ((low, low_iota), (high, high_iota))
            )
            found = dot(high_hot, low_hot, NT)
            for i in range(2):
                own = found[i * rows : (i + 1) * rows, i * T : (i + 1) * T]
                acc_ref[pl.ds(base + j + i, rows, stride=nodes), :] = own
        return carry

    lax.fori_loop(0, nodes // 8, step, 0)

    def turn(h, carry):
        block = acc_ref[pl.ds(pl.multiple_of(h * nodes, nodes), nodes), :]
        out_ref[h] = block.T.astype(jnp.int32).astype(jnp.int16)
        return carry

    lax.fori_loop(0, blocks, turn, 0)


def count_negatives(negatives, blocks):
    nodes = negatives.shape[0]
    rows = 8 * ((blocks + 7) // 8)
    return pl.pallas_call(
        functools.partial(counts_kernel, blocks),
        out_shape=jax.ShapeDtypeStruct((blocks, T, nodes), jnp.int16),
        scratch_shapes=[pltpu.VMEM((rows * nodes, T), f32)],
        compiler_params=pltpu.CompilerParams(**PARAMS),
        cost_estimate=pl.CostEstimate(
            flops=2 * 16 * nodes * T * T * 64, bytes_accessed=2 << 20, transcendentals=0
        ),
        name="counts",
    )(negatives)


def behind(place, s):
    return lax.rem(place + ZL - s, ZL)


def tiles_kernel(cols, meta_ref, place_ref, own_ref, other_ref, *refs):
    tile_refs, (out_ref, acc_ref) = refs[: 2 * ZL], refs[2 * ZL :]
    zsize = own_ref.shape[1] // ZL
    slots = meta_ref.shape[2]
    acc_ref[...] = jnp.zeros_like(acc_ref)
    core, zl = place_ref[0], place_ref[1]
    for s in range(ZL):
        for i in range(slots // 4):
            late = i * 4 >= EARLY

            @pl.when(meta_ref[s, 0, i * 4] >= 0)
            def _(s=s, i=i, late=late):
                products = []
                for j in range(4):
                    k = i * 4 + j
                    tcol = meta_ref[s, 1, k]
                    chip = lax.div(tcol, 2)
                    at = lax.div(chip, zsize), behind(zl, s) * zsize + lax.rem(chip, zsize)
                    mine = lax.rem(tcol, 2) == core
                    rows = jnp.where(mine, own_ref[at], other_ref[at])
                    start = (k - EARLY if late else k) * T
                    tile = tile_refs[2 * s + late][start : start + T, :]
                    products.append(dot(rows, tile, NT))
                for j in range(4):
                    k = i * 4 + j
                    trow = meta_ref[s, 0, k]
                    held = jnp.where(trow >= 0, 1, 0)
                    at = jnp.maximum(trow, 0)
                    for v in range(2):
                        kept = (held * meta_ref[s, 2 + v, k]).astype(f32)
                        acc_ref[at, v] += kept * products[j]

    out_ref[...] = acc_ref[...].astype(bf16)


def cut_kernel(x_ref, out_ref):
    copies = out_ref.shape[0] // ZL
    turned = x_ref[...].astype(f32).T
    for s in range(ZL):
        rows = turned[s * FS : (s + 1) * FS]
        if rows.shape[0] < FS:
            rows = jnp.concatenate([rows, jnp.zeros((FS - rows.shape[0], T), f32)], 0)
        for i in range(copies):
            out_ref[s * copies + i] = rows.astype(bf16)


def cut_features(features, copies):
    return pl.pallas_call(
        cut_kernel,
        out_shape=jax.ShapeDtypeStruct((ZL * copies, FS, features.shape[0]), bf16),
        name="cut_features",
    )(features)


def tile_sums(meta, place, own, other, tiles, cols, blocks):
    shape = (blocks, 2, own.shape[2], T)
    return pl.pallas_call(
        functools.partial(tiles_kernel, cols),
        out_shape=jax.ShapeDtypeStruct(shape, bf16),
        in_specs=[pl.BlockSpec(memory_space=pltpu.SMEM)] * 2
        + [pl.BlockSpec(memory_space=pltpu.VMEM)] * (2 + 2 * ZL),
        scratch_shapes=[pltpu.VMEM(shape, f32)],
        compiler_params=pltpu.CompilerParams(**PARAMS),
        name="tile_sums",
    )(meta, place, own, other, *tiles)


def anchors_of(n_ref, zl, v):
    return jnp.concatenate([n_ref[behind(zl, z), v] for z in range(ZL)], 1)


def embed(weight_t, agg):
    z = dot(weight_t, agg, NN)
    rinv = lax.rsqrt(jnp.sum(z * z, 0, keepdims=True) + eps)
    return z * rinv, rinv


def pair_of(a_ref, p, v):
    return jnp.concatenate([a_ref[2 * p, v], a_ref[2 * p + 1, v]], 1)


def scores_kernel(place_ref, n_ref, a_ref, w_ref, c_ref, tot_ref, e_ref, low_ref):
    weight_t = w_ref[...]
    zl = place_ref[1]
    anchors = [embed(weight_t, anchors_of(n_ref, zl, v))[0].astype(bf16) for v in range(2)]
    tot_ref[...] = jnp.zeros_like(tot_ref)

    def pair(p, carry):
        count = jnp.concatenate(
            [
                jnp.concatenate([c_ref[behind(zl, z), 2 * p + i] for z in range(ZL)], 1)
                for i in range(2)
            ],
            0,
        )
        count = count.astype(jnp.int32).astype(f32)
        for v in range(2):
            emb = embed(weight_t, pair_of(a_ref, p, 1 - v))[0]
            low_ref[p, 1 - v] = emb.astype(bf16)
            score = dot(emb.T.astype(bf16), anchors[v], NN)
            term = count * jnp.exp(score * (1.0 / tau))
            e_ref[p, v] = term.astype(bf16)
            tot_ref[v : v + 1, :] += jnp.sum(term, 0, keepdims=True)
        return carry

    lax.fori_loop(0, e_ref.shape[0], pair, 0, unroll=True)


def pull_kernel(e_ref, low_ref, sums_ref):
    sums_ref[...] = jnp.zeros_like(sums_ref)

    def pair(p, carry):
        for v in range(2):
            sums_ref[v] += dot(low_ref[p, 1 - v], e_ref[p, v], NN)
        return carry

    lax.fori_loop(0, e_ref.shape[0], pair, 0, unroll=True)


def split_dot(agg, dz):
    high = dz.astype(bf16)
    low = (dz - high.astype(f32)).astype(bf16)
    return dot(agg, high, NT) + dot(agg, low, NT)


def grads_kernel(
    coef, place_ref, n_ref, a_ref, w_ref, e_ref, sums_ref, mask_ref, *refs
):
    *tot_refs, loss_ref, grad_ref = refs
    weight_t = w_ref[...]
    agg_n = [anchors_of(n_ref, place_ref[1], v) for v in range(2)]
    emb_n, rinv_n = zip(*[embed(weight_t, agg) for agg in agg_n])
    full_n = [emb.astype(bf16).astype(f32) for emb in emb_n]
    pos = jnp.sum(full_n[0] * full_n[1], 0, keepdims=True) * (1.0 / tau)
    own = jnp.exp(pos)
    tot = [own + sum(t[v : v + 1, :] for t in tot_refs) for v in range(2)]
    loss = 0.5 * ((jnp.log(tot[0]) - pos) + (jnp.log(tot[1]) - pos))
    loss_ref[...] = jnp.broadcast_to(loss, loss_ref.shape)
    inverse = [1.0 / t for t in tot]
    both = (own * inverse[0] + own * inverse[1] - 2.0) * mask_ref[0:1, :]
    scaled = [(full_n[v] * inverse[v]).astype(bf16) for v in range(2)]

    def back(emb, rinv, d):
        return (d - emb * jnp.sum(emb * d, 0, keepdims=True)) * rinv

    grad_ref[...] = jnp.zeros_like(grad_ref)

    def pair(p, carry):
        for v in range(2):
            agg = pair_of(a_ref, p, v)
            emb, rinv = embed(weight_t, agg)
            d = coef * dot(scaled[1 - v], e_ref[p, 1 - v], NT)
            grad_ref[...] += split_dot(agg, back(emb, rinv, d))
        return carry

    lax.fori_loop(0, e_ref.shape[0], pair, 0, unroll=True)
    for v in range(2):
        d = coef * (both * full_n[1 - v] + sums_ref[v] * inverse[v])
        grad_ref[...] += split_dot(agg_n[v], back(emb_n[v], rinv_n[v], d))


def group_call(kernel, out_shape, inputs, scalars, name):
    return pl.pallas_call(
        kernel,
        out_shape=out_shape,
        in_specs=[pl.BlockSpec(memory_space=pltpu.SMEM)] * scalars
        + [pl.BlockSpec(memory_space=pltpu.VMEM)] * (inputs - scalars),
        compiler_params=pltpu.CompilerParams(**PARAMS),
        cost_estimate=pl.CostEstimate(flops=1 << 31, bytes_accessed=4 << 20, transcendentals=0),
        name=name,
    )


def swap(x, axis):
    return lax.all_to_all(x, axis, 0, 0, tiled=True)


def share(x, axis):
    return swap(jnp.broadcast_to(x[None], (lax.axis_size(axis),) + x.shape), axis)


def shift(x, axis, by):
    size = lax.axis_size(axis)
    return lax.ppermute(x, axis, [(i, (i + by) % size) for i in range(size)])


def around(x, pick, axis):
    return [pick(x, 0)] + [shift(pick(x, s), axis, s) for s in range(1, lax.axis_size(axis))]


def reduce_all(grad):
    rows, width = grad.shape
    plane = ("y", "x")
    part = jnp.sum(swap(grad.reshape(lax.axis_size(plane), -1, width), plane), 0)
    part = part + shift(part, "core", 1)
    part = jnp.sum(share(part, ("zl", "zh")), 0)
    return share(part, plane).reshape(rows, width)


def packed(tiles, tile_pos, edge_keep, cols):
    slots = tile_pos.shape[0]
    held = tile_pos >= 0
    trow = jnp.where(held, tile_pos // cols, -1)
    tcol = jnp.where(held, tile_pos % cols, 0)
    meta = jnp.concatenate([trow[None], tcol[None], edge_keep], 0).astype(bf16)
    meta = jnp.pad(meta, ((0, 16 - meta.shape[0]), (0, T - slots)))
    return jnp.concatenate([tiles[EARLY:].reshape((slots - EARLY) * T, T), meta], 0)


def shards(features, weight, tiles, tile_pos, edge_keep, feature_keep, negatives):
    nodes, width = features.shape
    slots = tiles.shape[0]
    xsize, zsize = lax.axis_size("x"), lax.axis_size("zh")
    ysize = lax.axis_size("y")
    cols = xsize * zsize * lax.axis_size("core")
    zl = lax.axis_index("zl")
    place = jnp.stack([lax.axis_index("core"), zl])
    total = lax.axis_size(ROW) * cols * nodes
    whole = lambda x, s: x

    near = swap(cut_features(features, zsize), ("zl", "zh"))
    some, rest = tiles[:EARLY].reshape(EARLY * T, T), packed(tiles, tile_pos, edge_keep, cols)
    next_some = shift(some, "zl", 1)
    near, next_some = lax.optimization_barrier((near, next_some))
    own = share(near, "x")
    next_rest, last_some, last_rest = (
        shift(rest, "zl", 1),
        shift(some, "zl", 2),
        shift(rest, "zl", 2),
    )
    own, next_rest, last_some, last_rest = lax.optimization_barrier(
        (own, next_rest, last_some, last_rest)
    )
    all_tiles = [some, rest, next_some, next_rest, last_some, last_rest]
    other = shift(own, "core", 1)
    late = (slots - EARLY) * T
    metas = jnp.stack([x[late : late + 4, :slots] for x in all_tiles[1::2]]).astype(jnp.int32)

    part = tile_sums(metas, place, own, other, all_tiles, cols, ZL * ysize)
    part, negatives = lax.optimization_barrier((part, negatives))
    got = swap(part, ROW)
    counts = count_negatives(negatives, ZL * ysize)
    got, counts = lax.optimization_barrier((got, counts))
    agg = jnp.sum(got.reshape(ZL, ysize, 2, FS, nodes).astype(f32), 1)
    agg = agg.transpose(1, 0, 2, 3).reshape(2, ZL * FS, nodes)[:, :width]
    agg = (agg * feature_keep.astype(f32)[:, :, None]).astype(bf16)
    agg, counts = lax.optimization_barrier((agg, counts))
    members = share(agg, "y")
    anchors = jnp.stack(around(agg, whole, "zl"))
    ahead = lambda x, s: lax.dynamic_index_in_dim(x, lax.rem(zl + s, ZL), 0, keepdims=False)
    counts = jnp.stack(around(counts.reshape(ZL, ysize, nodes, nodes), ahead, "zl"))

    weight_t = weight.T
    group = ZL * nodes
    rows = jax.ShapeDtypeStruct((8, group), f32)
    tot, terms, low = group_call(
        scores_kernel,
        (
            rows,
            jax.ShapeDtypeStruct((ysize // 2, 2, 2 * nodes, group), bf16),
            jax.ShapeDtypeStruct((ysize // 2, 2, width, 2 * nodes), bf16),
        ),
        5,
        1,
        "scores",
    )(place, anchors, members, weight_t, counts)
    tots = around(tot, whole, "zl")
    sums = group_call(
        pull_kernel, jax.ShapeDtypeStruct((2, width, group), f32), 2, 0, "pull"
    )(terms, low)
    mask = (jnp.arange(group) // nodes == zl).astype(f32)
    mask = jnp.broadcast_to(mask, (8, group))
    coef = 1.0 / (2.0 * tau * float(total) ** 0.5)
    loss, grad = group_call(
        functools.partial(grads_kernel, coef),
        (rows, jax.ShapeDtypeStruct((width, width), f32)),
        7 + ZL,
        1,
        "grads",
    )(place, anchors, members, weight_t, terms, sums, mask, *tots)
    node_loss = lax.dynamic_slice_in_dim(loss[0], zl * nodes, nodes)
    return node_loss, reduce_all(grad)


def solution(mesh):
    rows, cols = mesh.devices.shape
    fine = Mesh(mesh.devices.reshape(ZL, rows // ZL, cols // 8, 4, 2), ROW + COL)
    every = ROW + COL
    in_specs = (
        P(every, None),
        P(),
        P(every, None, None),
        P(every),
        P(None, every),
        P(),
        P(every, None),
    )
    out_specs = (P(every), P())
    return jax.shard_map(shards, mesh=fine, in_specs=in_specs, out_specs=out_specs, check_vma=False)
```

```python
import functools

import jax
import jax.numpy as jnp
from jax import lax
from jax.experimental import pallas as pl
from jax.experimental.pallas import tpu as pltpu
from jax.sharding import Mesh
from jax.sharding import PartitionSpec as P

tau = 0.5
eps = 1e-06
T = 128
ZL = 3
EARLY = 8
FS = 88
f32 = jnp.float32
bf16 = jnp.bfloat16
NT = (((1,), (1,)), ((), ()))
NN = (((1,), (0,)), ((), ()))
ROW = ("zl", "y")
COL = ("x", "zh", "core")
PARAMS = dict(vmem_limit_bytes=24 * 1024 * 1024)


def dot(a, b, dims):
    return lax.dot_general(a, b, dims, preferred_element_type=f32)


def counts_kernel(blocks, neg_ref, out_ref, acc_ref):
    nodes, negs = neg_ref.shape
    rows = 8 * ((blocks + 7) // 8)
    low_iota = lax.broadcasted_iota(jnp.int32, (T, negs), 0)
    high_iota = lax.broadcasted_iota(jnp.int32, (rows, negs), 0)

    def step(i, carry):
        base = pl.multiple_of(i * 8, 8)
        index = neg_ref[pl.ds(base, 8), :]
        low = index & (T - 1)
        high = index >> 7
        for j in range(0, 8, 2):
            low_hot, high_hot = (
                jnp.concatenate(
                    [jnp.where(part[j + i : j + i + 1, :] == iota, 1.0, 0.0) for i in range(2)], 0
                ).astype(bf16)
                for part, iota in ((low, low_iota), (high, high_iota))
            )
            found = dot(high_hot, low_hot, NT)
            for i in range(2):
                own = found[i * rows : (i + 1) * rows, i * T : (i + 1) * T]
                acc_ref[pl.ds(base + j + i, rows, stride=nodes), :] = own
        return carry

    lax.fori_loop(0, nodes // 8, step, 0)

    def turn(h, carry):
        block = acc_ref[pl.ds(pl.multiple_of(h * nodes, nodes), nodes), :]
        out_ref[h] = block.T.astype(jnp.int32).astype(jnp.int16)
        return carry

    lax.fori_loop(0, blocks, turn, 0)


def count_negatives(negatives, blocks):
    nodes = negatives.shape[0]
    rows = 8 * ((blocks + 7) // 8)
    return pl.pallas_call(
        functools.partial(counts_kernel, blocks),
        out_shape=jax.ShapeDtypeStruct((blocks, T, nodes), jnp.int16),
        scratch_shapes=[pltpu.VMEM((rows * nodes, T), f32)],
        compiler_params=pltpu.CompilerParams(**PARAMS),
        cost_estimate=pl.CostEstimate(
            flops=2 * 16 * nodes * T * T * 64, bytes_accessed=2 << 20, transcendentals=0
        ),
        name="counts",
    )(negatives)


def behind(place, s):
    return lax.rem(place + ZL - s, ZL)


def tiles_kernel(cols, meta_ref, place_ref, own_ref, other_ref, *refs):
    *tile_refs, out_ref, acc_ref = refs
    zsize = own_ref.shape[1] // ZL
    slots = meta_ref.shape[2]
    acc_ref[...] = jnp.zeros_like(acc_ref)
    core, zl = place_ref[0], place_ref[1]
    for s in range(ZL):
        for i in range(slots // 4):
            late = i * 4 >= EARLY

            @pl.when(meta_ref[s, 0, i * 4] >= 0)
            def _(s=s, i=i, late=late):
                products = []
                for j in range(4):
                    k = i * 4 + j
                    tcol = meta_ref[s, 1, k]
                    chip = lax.div(tcol, 2)
                    at = lax.div(chip, zsize), behind(zl, s) * zsize + lax.rem(chip, zsize)
                    mine = lax.rem(tcol, 2) == core
                    rows = jnp.where(mine, own_ref[at], other_ref[at])
                    split = late and s < ZL - 1
                    start = (k - EARLY if split else k) * T
                    tile = tile_refs[2 * s + split][start : start + T, :]
                    products.append(dot(rows, tile, NT))
                for j in range(4):
                    k = i * 4 + j
                    trow = meta_ref[s, 0, k]
                    held = jnp.where(trow >= 0, 1, 0)
                    at = jnp.maximum(trow, 0)
                    for v in range(2):
                        kept = (held * meta_ref[s, 2 + v, k]).astype(f32)
                        acc_ref[at, v] += kept * products[j]

    out_ref[...] = acc_ref[...].astype(bf16)


def cut_kernel(x_ref, out_ref):
    copies = out_ref.shape[0] // ZL
    turned = x_ref[...].astype(f32).T
    for s in range(ZL):
        rows = turned[s * FS : (s + 1) * FS]
        if rows.shape[0] < FS:
            rows = jnp.concatenate([rows, jnp.zeros((FS - rows.shape[0], T), f32)], 0)
        for i in range(copies):
            out_ref[s * copies + i] = rows.astype(bf16)


def cut_features(features, copies):
    return pl.pallas_call(
        cut_kernel,
        out_shape=jax.ShapeDtypeStruct((ZL * copies, FS, features.shape[0]), bf16),
        name="cut_features",
    )(features)


def tile_sums(meta, place, own, other, tiles, cols, blocks):
    shape = (blocks, 2, own.shape[2], T)
    return pl.pallas_call(
        functools.partial(tiles_kernel, cols),
        out_shape=jax.ShapeDtypeStruct(shape, bf16),
        in_specs=[pl.BlockSpec(memory_space=pltpu.SMEM)] * 2
        + [pl.BlockSpec(memory_space=pltpu.VMEM)] * (2 + len(tiles)),
        scratch_shapes=[pltpu.VMEM(shape, f32)],
        compiler_params=pltpu.CompilerParams(**PARAMS),
        name="tile_sums",
    )(meta, place, own, other, *tiles)


def anchors_of(n_ref, zl, v):
    return jnp.concatenate([n_ref[behind(zl, z), v] for z in range(ZL)], 1)


def embed(weight_t, agg):
    z = dot(weight_t, agg, NN)
    rinv = lax.rsqrt(jnp.sum(z * z, 0, keepdims=True) + eps)
    return z * rinv, rinv


def pair_of(a_ref, p, v):
    return jnp.concatenate([a_ref[2 * p, v], a_ref[2 * p + 1, v]], 1)


def scores_kernel(place_ref, n_ref, a_ref, w_ref, c_ref, tot_ref, e_ref, low_ref):
    weight_t = w_ref[...]
    zl = place_ref[1]
    anchors = [embed(weight_t, anchors_of(n_ref, zl, v))[0].astype(bf16) for v in range(2)]
    tot_ref[...] = jnp.zeros_like(tot_ref)

    def pair(p, carry):
        count = jnp.concatenate(
            [
                jnp.concatenate([c_ref[behind(zl, z), 2 * p + i] for z in range(ZL)], 1)
                for i in range(2)
            ],
            0,
        )
        count = count.astype(jnp.int32).astype(f32)
        for v in range(2):
            emb = embed(weight_t, pair_of(a_ref, p, 1 - v))[0]
            low_ref[p, 1 - v] = emb.astype(bf16)
            score = dot(emb.T.astype(bf16), anchors[v], NN)
            term = count * jnp.exp(score * (1.0 / tau))
            e_ref[p, v] = term.astype(bf16)
            tot_ref[v : v + 1, :] += jnp.sum(term, 0, keepdims=True)
        return carry

    lax.fori_loop(0, e_ref.shape[0], pair, 0, unroll=True)


def pull_kernel(e_ref, low_ref, sums_ref):
    sums_ref[...] = jnp.zeros_like(sums_ref)

    def pair(p, carry):
        for v in range(2):
            sums_ref[v] += dot(low_ref[p, 1 - v], e_ref[p, v], NN)
        return carry

    lax.fori_loop(0, e_ref.shape[0], pair, 0, unroll=True)


def split_dot(agg, dz):
    high = dz.astype(bf16)
    low = (dz - high.astype(f32)).astype(bf16)
    return dot(agg, high, NT) + dot(agg, low, NT)


def grads_kernel(
    coef, place_ref, n_ref, a_ref, w_ref, e_ref, sums_ref, mask_ref, *refs
):
    *tot_refs, loss_ref, grad_ref = refs
    weight_t = w_ref[...]
    agg_n = [anchors_of(n_ref, place_ref[1], v) for v in range(2)]
    emb_n, rinv_n = zip(*[embed(weight_t, agg) for agg in agg_n])
    full_n = [emb.astype(bf16).astype(f32) for emb in emb_n]
    pos = jnp.sum(full_n[0] * full_n[1], 0, keepdims=True) * (1.0 / tau)
    own = jnp.exp(pos)
    tot = [own + sum(t[v : v + 1, :] for t in tot_refs) for v in range(2)]
    loss = 0.5 * ((jnp.log(tot[0]) - pos) + (jnp.log(tot[1]) - pos))
    loss_ref[...] = jnp.broadcast_to(loss, loss_ref.shape)
    inverse = [1.0 / t for t in tot]
    both = (own * inverse[0] + own * inverse[1] - 2.0) * mask_ref[0:1, :]
    scaled = [(full_n[v] * inverse[v]).astype(bf16) for v in range(2)]

    def back(emb, rinv, d):
        return (d - emb * jnp.sum(emb * d, 0, keepdims=True)) * rinv

    grad_ref[...] = jnp.zeros_like(grad_ref)

    def pair(p, carry):
        for v in range(2):
            agg = pair_of(a_ref, p, v)
            emb, rinv = embed(weight_t, agg)
            d = coef * dot(scaled[1 - v], e_ref[p, 1 - v], NT)
            grad_ref[...] += split_dot(agg, back(emb, rinv, d))
        return carry

    lax.fori_loop(0, e_ref.shape[0], pair, 0, unroll=True)
    for v in range(2):
        d = coef * (both * full_n[1 - v] + sums_ref[v] * inverse[v])
        grad_ref[...] += split_dot(agg_n[v], back(emb_n[v], rinv_n[v], d))


def group_call(kernel, out_shape, inputs, scalars, name):
    return pl.pallas_call(
        kernel,
        out_shape=out_shape,
        in_specs=[pl.BlockSpec(memory_space=pltpu.SMEM)] * scalars
        + [pl.BlockSpec(memory_space=pltpu.VMEM)] * (inputs - scalars),
        compiler_params=pltpu.CompilerParams(**PARAMS),
        cost_estimate=pl.CostEstimate(flops=1 << 31, bytes_accessed=4 << 20, transcendentals=0),
        name=name,
    )


def swap(x, axis):
    return lax.all_to_all(x, axis, 0, 0, tiled=True)


def share(x, axis):
    return swap(jnp.broadcast_to(x[None], (lax.axis_size(axis),) + x.shape), axis)


def shift(x, axis, by):
    size = lax.axis_size(axis)
    return lax.ppermute(x, axis, [(i, (i + by) % size) for i in range(size)])


def around(x, pick, axis):
    return [pick(x, 0)] + [shift(pick(x, s), axis, s) for s in range(1, lax.axis_size(axis))]


def reduce_all(grad):
    rows, width = grad.shape
    plane = ("y", "x")
    part = jnp.sum(swap(grad.reshape(lax.axis_size(plane), -1, width), plane), 0)
    part = part + shift(part, "core", 1)
    part = jnp.sum(share(part, ("zl", "zh")), 0)
    return share(part, plane).reshape(rows, width)


def packed(tiles, tile_pos, edge_keep, cols):
    slots = tile_pos.shape[0]
    held = tile_pos >= 0
    trow = jnp.where(held, tile_pos // cols, -1)
    tcol = jnp.where(held, tile_pos % cols, 0)
    meta = jnp.concatenate([trow[None], tcol[None], edge_keep], 0).astype(bf16)
    meta = jnp.pad(meta, ((0, 16 - meta.shape[0]), (0, T - slots)))
    return jnp.concatenate([tiles[EARLY:].reshape((slots - EARLY) * T, T), meta], 0)


def shards(features, weight, tiles, tile_pos, edge_keep, feature_keep, negatives):
    nodes, width = features.shape
    slots = tiles.shape[0]
    xsize, zsize = lax.axis_size("x"), lax.axis_size("zh")
    ysize = lax.axis_size("y")
    cols = xsize * zsize * lax.axis_size("core")
    zl = lax.axis_index("zl")
    place = jnp.stack([lax.axis_index("core"), zl])
    total = lax.axis_size(ROW) * cols * nodes
    whole = lambda x, s: x

    near = swap(cut_features(features, zsize), ("zl", "zh"))
    some, rest = tiles[:EARLY].reshape(EARLY * T, T), packed(tiles, tile_pos, edge_keep, cols)
    next_some = shift(some, "zl", 1)
    near, next_some = lax.optimization_barrier((near, next_some))
    own = share(near, "x")
    next_rest = shift(rest, "zl", 1)
    last = shift(jnp.concatenate([some, rest], 0), "zl", 2)
    own, next_rest, last = lax.optimization_barrier((own, next_rest, last))
    all_tiles = [some, rest, next_some, next_rest, last]
    other = shift(own, "core", 1)
    late = (slots - EARLY) * T
    metas = [rest[late : late + 4], next_rest[late : late + 4], last[slots * T : slots * T + 4]]
    metas = jnp.stack(metas)[:, :, :slots].astype(jnp.int32)

    part = tile_sums(metas, place, own, other, all_tiles, cols, ZL * ysize)
    part, negatives = lax.optimization_barrier((part, negatives))
    got = swap(part, ROW)
    counts = count_negatives(negatives, ZL * ysize)
    got, counts = lax.optimization_barrier((got, counts))
    agg = jnp.sum(got.reshape(ZL, ysize, 2, FS, nodes).astype(f32), 1)
    agg = agg.transpose(1, 0, 2, 3).reshape(2, ZL * FS, nodes)[:, :width]
    agg = (agg * feature_keep.astype(f32)[:, :, None]).astype(bf16)
    agg, counts = lax.optimization_barrier((agg, counts))
    members = share(agg, "y")
    anchors = jnp.stack(around(agg, whole, "zl"))
    ahead = lambda x, s: lax.dynamic_index_in_dim(x, lax.rem(zl + s, ZL), 0, keepdims=False)
    counts = jnp.stack(around(counts.reshape(ZL, ysize, nodes, nodes), ahead, "zl"))

    weight_t = weight.T
    group = ZL * nodes
    rows = jax.ShapeDtypeStruct((8, group), f32)
    tot, terms, low = group_call(
        scores_kernel,
        (
            rows,
            jax.ShapeDtypeStruct((ysize // 2, 2, 2 * nodes, group), bf16),
            jax.ShapeDtypeStruct((ysize // 2, 2, width, 2 * nodes), bf16),
        ),
        5,
        1,
        "scores",
    )(place, anchors, members, weight_t, counts)
    tots = around(tot, whole, "zl")
    sums = group_call(
        pull_kernel, jax.ShapeDtypeStruct((2, width, group), f32), 2, 0, "pull"
    )(terms, low)
    mask = (jnp.arange(group) // nodes == zl).astype(f32)
    mask = jnp.broadcast_to(mask, (8, group))
    coef = 1.0 / (2.0 * tau * float(total) ** 0.5)
    loss, grad = group_call(
        functools.partial(grads_kernel, coef),
        (rows, jax.ShapeDtypeStruct((width, width), f32)),
        7 + ZL,
        1,
        "grads",
    )(place, anchors, members, weight_t, terms, sums, mask, *tots)
    node_loss = lax.dynamic_slice_in_dim(loss[0], zl * nodes, nodes)
    return node_loss, reduce_all(grad)


def solution(mesh):
    rows, cols = mesh.devices.shape
    fine = Mesh(mesh.devices.reshape(ZL, rows // ZL, cols // 8, 4, 2), ROW + COL)
    every = ROW + COL
    in_specs = (
        P(every, None),
        P(),
        P(every, None, None),
        P(every),
        P(None, every),
        P(),
        P(every, None),
    )
    out_specs = (P(every), P())
    return jax.shard_map(shards, mesh=fine, in_specs=in_specs, out_specs=out_specs, check_vma=False)
```

```python
import functools

import jax
import jax.numpy as jnp
from jax import lax
from jax.experimental import pallas as pl
from jax.experimental.pallas import tpu as pltpu
from jax.sharding import Mesh
from jax.sharding import PartitionSpec as P

tau = 0.5
eps = 1e-06
T = 128
ZL = 3
EARLY = 8
FS = 88
f32 = jnp.float32
bf16 = jnp.bfloat16
NT = (((1,), (1,)), ((), ()))
NN = (((1,), (0,)), ((), ()))
ROW = ("zl", "y")
COL = ("x", "zh", "core")
PARAMS = dict(vmem_limit_bytes=24 * 1024 * 1024)


def dot(a, b, dims):
    return lax.dot_general(a, b, dims, preferred_element_type=f32)


def counts_kernel(blocks, neg_ref, out_ref, acc_ref):
    nodes, negs = neg_ref.shape
    rows = 8 * ((blocks + 7) // 8)
    low_iota = lax.broadcasted_iota(jnp.int32, (T, negs), 0)
    high_iota = lax.broadcasted_iota(jnp.int32, (rows, negs), 0)

    def step(i, carry):
        base = pl.multiple_of(i * 8, 8)
        index = neg_ref[pl.ds(base, 8), :]
        low = index & (T - 1)
        high = index >> 7
        for j in range(0, 8, 2):
            low_hot, high_hot = (
                jnp.concatenate(
                    [jnp.where(part[j + i : j + i + 1, :] == iota, 1.0, 0.0) for i in range(2)], 0
                ).astype(bf16)
                for part, iota in ((low, low_iota), (high, high_iota))
            )
            found = dot(high_hot, low_hot, NT)
            for i in range(2):
                own = found[i * rows : (i + 1) * rows, i * T : (i + 1) * T]
                acc_ref[pl.ds(base + j + i, rows, stride=nodes), :] = own
        return carry

    lax.fori_loop(0, nodes // 8, step, 0)

    def turn(h, carry):
        block = acc_ref[pl.ds(pl.multiple_of(h * nodes, nodes), nodes), :]
        out_ref[h] = block.T.astype(jnp.int32).astype(jnp.int16)
        return carry

    lax.fori_loop(0, blocks, turn, 0)


def count_negatives(negatives, blocks):
    nodes = negatives.shape[0]
    rows = 8 * ((blocks + 7) // 8)
    return pl.pallas_call(
        functools.partial(counts_kernel, blocks),
        out_shape=jax.ShapeDtypeStruct((blocks, T, nodes), jnp.int16),
        scratch_shapes=[pltpu.VMEM((rows * nodes, T), f32)],
        compiler_params=pltpu.CompilerParams(**PARAMS),
        cost_estimate=pl.CostEstimate(
            flops=2 * 16 * nodes * T * T * 64, bytes_accessed=2 << 20, transcendentals=0
        ),
        name="counts",
    )(negatives)


def behind(place, s):
    return lax.rem(place + ZL - s, ZL)


def tiles_kernel(cols, meta_ref, place_ref, own_ref, other_ref, *refs):
    tile_refs, (out_ref, acc_ref) = refs[: 2 * ZL], refs[2 * ZL :]
    zsize = own_ref.shape[1] // ZL
    slots = meta_ref.shape[2]
    acc_ref[...] = jnp.zeros_like(acc_ref)
    core, zl = place_ref[0], place_ref[1]
    for s in range(ZL):
        for i in range(slots // 4):
            late = i * 4 >= EARLY

            @pl.when(meta_ref[s, 0, i * 4] >= 0)
            def _(s=s, i=i, late=late):
                products = []
                for j in range(4):
                    k = i * 4 + j
                    tcol = meta_ref[s, 1, k]
                    chip = lax.div(tcol, 2)
                    at = lax.div(chip, zsize), behind(zl, s) * zsize + lax.rem(chip, zsize)
                    mine = lax.rem(tcol, 2) == core
                    rows = jnp.where(mine, own_ref[at], other_ref[at])
                    start = (k - EARLY if late else k) * T
                    tile = tile_refs[2 * s + late][start : start + T, :]
                    products.append(dot(rows, tile, NT))
                for j in range(4):
                    k = i * 4 + j
                    trow = meta_ref[s, 0, k]
                    held = jnp.where(trow >= 0, 1, 0)
                    at = jnp.maximum(trow, 0)
                    for v in range(2):
                        kept = (held * meta_ref[s, 2 + v, k]).astype(f32)
                        acc_ref[at, v] += kept * products[j]

    out_ref[...] = acc_ref[...].astype(bf16)


def cut_kernel(x_ref, out_ref):
    copies = out_ref.shape[0] // ZL
    turned = x_ref[...].astype(f32).T
    for s in range(ZL):
        rows = turned[s * FS : (s + 1) * FS]
        if rows.shape[0] < FS:
            rows = jnp.concatenate([rows, jnp.zeros((FS - rows.shape[0], T), f32)], 0)
        for i in range(copies):
            out_ref[s * copies + i] = rows.astype(bf16)


def cut_features(features, copies):
    return pl.pallas_call(
        cut_kernel,
        out_shape=jax.ShapeDtypeStruct((ZL * copies, FS, features.shape[0]), bf16),
        name="cut_features",
    )(features)


def tile_sums(meta, place, own, other, tiles, cols, blocks):
    shape = (blocks, 2, own.shape[2], T)
    return pl.pallas_call(
        functools.partial(tiles_kernel, cols),
        out_shape=jax.ShapeDtypeStruct(shape, bf16),
        in_specs=[pl.BlockSpec(memory_space=pltpu.SMEM)] * 2
        + [pl.BlockSpec(memory_space=pltpu.VMEM)] * (2 + 2 * ZL),
        scratch_shapes=[pltpu.VMEM(shape, f32)],
        compiler_params=pltpu.CompilerParams(**PARAMS),
        name="tile_sums",
    )(meta, place, own, other, *tiles)


def anchors_of(n_ref, zl, v):
    return jnp.concatenate([n_ref[behind(zl, z), v] for z in range(ZL)], 1)


def embed(weight_t, agg):
    z = dot(weight_t, agg, NN)
    rinv = lax.rsqrt(jnp.sum(z * z, 0, keepdims=True) + eps)
    return z * rinv, rinv


def sums_kernel(got_ref, keep_ref, agg_ref, sent_ref):
    copies, _, width, _ = sent_ref.shape
    for v in range(2):
        shares = [
            sum(got_ref[s * copies + y, v].astype(f32) for y in range(copies)) for s in range(ZL)
        ]
        agg = (jnp.concatenate(shares, 0)[:width] * keep_ref[v]).astype(bf16)
        agg_ref[v] = agg
        for y in range(copies):
            sent_ref[y, v] = agg


def own_sums(got, keep, copies):
    return pl.pallas_call(
        sums_kernel,
        out_shape=(
            jax.ShapeDtypeStruct(keep.shape, bf16),
            jax.ShapeDtypeStruct((copies,) + keep.shape, bf16),
        ),
        compiler_params=pltpu.CompilerParams(**PARAMS),
        name="own_sums",
    )(got, keep)


def pair_of(a_ref, p, v):
    return jnp.concatenate([a_ref[2 * p, v], a_ref[2 * p + 1, v]], 1)


def scores_kernel(place_ref, n_ref, a_ref, w_ref, c_ref, tot_ref, e_ref, low_ref):
    weight_t = w_ref[...]
    zl = place_ref[1]
    anchors = [embed(weight_t, anchors_of(n_ref, zl, v))[0].astype(bf16) for v in range(2)]
    tot_ref[...] = jnp.zeros_like(tot_ref)

    def pair(p, carry):
        count = jnp.concatenate(
            [
                jnp.concatenate([c_ref[behind(zl, z), 2 * p + i] for z in range(ZL)], 1)
                for i in range(2)
            ],
            0,
        )
        count = count.astype(jnp.int32).astype(f32)
        for v in range(2):
            emb = embed(weight_t, pair_of(a_ref, p, 1 - v))[0]
            low_ref[p, 1 - v] = emb.astype(bf16)
            score = dot(emb.T.astype(bf16), anchors[v], NN)
            term = count * jnp.exp(score * (1.0 / tau))
            e_ref[p, v] = term.astype(bf16)
            tot_ref[v : v + 1, :] += jnp.sum(term, 0, keepdims=True)
        return carry

    lax.fori_loop(0, e_ref.shape[0], pair, 0, unroll=True)


def pull_kernel(e_ref, low_ref, sums_ref):
    sums_ref[...] = jnp.zeros_like(sums_ref)

    def pair(p, carry):
        for v in range(2):
            sums_ref[v] += dot(low_ref[p, 1 - v], e_ref[p, v], NN)
        return carry

    lax.fori_loop(0, e_ref.shape[0], pair, 0, unroll=True)


def split_dot(agg, dz):
    high = dz.astype(bf16)
    low = (dz - high.astype(f32)).astype(bf16)
    return dot(agg, high, NT) + dot(agg, low, NT)


def grads_kernel(
    coef, place_ref, n_ref, a_ref, w_ref, e_ref, sums_ref, mask_ref, *refs
):
    *tot_refs, loss_ref, grad_ref = refs
    weight_t = w_ref[...]
    agg_n = [anchors_of(n_ref, place_ref[1], v) for v in range(2)]
    emb_n, rinv_n = zip(*[embed(weight_t, agg) for agg in agg_n])
    full_n = [emb.astype(bf16).astype(f32) for emb in emb_n]
    pos = jnp.sum(full_n[0] * full_n[1], 0, keepdims=True) * (1.0 / tau)
    own = jnp.exp(pos)
    tot = [own + sum(t[v : v + 1, :] for t in tot_refs) for v in range(2)]
    loss = 0.5 * ((jnp.log(tot[0]) - pos) + (jnp.log(tot[1]) - pos))
    loss_ref[...] = jnp.broadcast_to(loss, loss_ref.shape)
    inverse = [1.0 / t for t in tot]
    both = (own * inverse[0] + own * inverse[1] - 2.0) * mask_ref[0:1, :]
    scaled = [(full_n[v] * inverse[v]).astype(bf16) for v in range(2)]

    def back(emb, rinv, d):
        return (d - emb * jnp.sum(emb * d, 0, keepdims=True)) * rinv

    grad_ref[...] = jnp.zeros_like(grad_ref)

    def pair(p, carry):
        for v in range(2):
            agg = pair_of(a_ref, p, v)
            emb, rinv = embed(weight_t, agg)
            d = coef * dot(scaled[1 - v], e_ref[p, 1 - v], NT)
            grad_ref[...] += split_dot(agg, back(emb, rinv, d))
        return carry

    lax.fori_loop(0, e_ref.shape[0], pair, 0, unroll=True)
    for v in range(2):
        d = coef * (both * full_n[1 - v] + sums_ref[v] * inverse[v])
        grad_ref[...] += split_dot(agg_n[v], back(emb_n[v], rinv_n[v], d))


def group_call(kernel, out_shape, inputs, scalars, name):
    return pl.pallas_call(
        kernel,
        out_shape=out_shape,
        in_specs=[pl.BlockSpec(memory_space=pltpu.SMEM)] * scalars
        + [pl.BlockSpec(memory_space=pltpu.VMEM)] * (inputs - scalars),
        compiler_params=pltpu.CompilerParams(**PARAMS),
        cost_estimate=pl.CostEstimate(flops=1 << 31, bytes_accessed=4 << 20, transcendentals=0),
        name=name,
    )


def swap(x, axis):
    return lax.all_to_all(x, axis, 0, 0, tiled=True)


def share(x, axis):
    return swap(jnp.broadcast_to(x[None], (lax.axis_size(axis),) + x.shape), axis)


def shift(x, axis, by):
    size = lax.axis_size(axis)
    return lax.ppermute(x, axis, [(i, (i + by) % size) for i in range(size)])


def around(x, pick, axis):
    return [pick(x, 0)] + [shift(pick(x, s), axis, s) for s in range(1, lax.axis_size(axis))]


def reduce_all(grad):
    rows, width = grad.shape
    plane = ("y", "x")
    part = jnp.sum(swap(grad.reshape(lax.axis_size(plane), -1, width), plane), 0)
    part = part + shift(part, "core", 1)
    part = jnp.sum(share(part, ("zl", "zh")), 0)
    return share(part, plane).reshape(rows, width)


def packed(tiles, tile_pos, edge_keep, cols):
    slots = tile_pos.shape[0]
    held = tile_pos >= 0
    trow = jnp.where(held, tile_pos // cols, -1)
    tcol = jnp.where(held, tile_pos % cols, 0)
    meta = jnp.concatenate([trow[None], tcol[None], edge_keep], 0).astype(bf16)
    meta = jnp.pad(meta, ((0, 16 - meta.shape[0]), (0, T - slots)))
    return jnp.concatenate([tiles[EARLY:].reshape((slots - EARLY) * T, T), meta], 0)


def shards(features, weight, tiles, tile_pos, edge_keep, feature_keep, negatives):
    nodes, width = features.shape
    slots = tiles.shape[0]
    xsize, zsize = lax.axis_size("x"), lax.axis_size("zh")
    ysize = lax.axis_size("y")
    cols = xsize * zsize * lax.axis_size("core")
    zl = lax.axis_index("zl")
    place = jnp.stack([lax.axis_index("core"), zl])
    total = lax.axis_size(ROW) * cols * nodes
    whole = lambda x, s: x

    near = swap(cut_features(features, zsize), ("zl", "zh"))
    some, rest = tiles[:EARLY].reshape(EARLY * T, T), packed(tiles, tile_pos, edge_keep, cols)
    next_some = shift(some, "zl", 1)
    near, next_some = lax.optimization_barrier((near, next_some))
    own = share(near, "x")
    next_rest, last_some, last_rest = (
        shift(rest, "zl", 1),
        shift(some, "zl", 2),
        shift(rest, "zl", 2),
    )
    own, next_rest, last_some, last_rest = lax.optimization_barrier(
        (own, next_rest, last_some, last_rest)
    )
    all_tiles = [some, rest, next_some, next_rest, last_some, last_rest]
    other = shift(own, "core", 1)
    late = (slots - EARLY) * T
    metas = jnp.stack([x[late : late + 4, :slots] for x in all_tiles[1::2]]).astype(jnp.int32)

    part = tile_sums(metas, place, own, other, all_tiles, cols, ZL * ysize)
    part, negatives = lax.optimization_barrier((part, negatives))
    got = swap(part, ROW)
    counts = count_negatives(negatives, ZL * ysize)
    got, counts = lax.optimization_barrier((got, counts))
    keep = jnp.broadcast_to(feature_keep.astype(f32)[:, :, None], (2, width, nodes))
    agg, sent = own_sums(got, keep, ysize)
    agg, sent, counts = lax.optimization_barrier((agg, sent, counts))
    members = swap(sent, "y")
    anchors = jnp.stack(around(agg, whole, "zl"))
    ahead = lambda x, s: lax.dynamic_index_in_dim(x, lax.rem(zl + s, ZL), 0, keepdims=False)
    counts = jnp.stack(around(counts.reshape(ZL, ysize, nodes, nodes), ahead, "zl"))

    weight_t = weight.T
    group = ZL * nodes
    rows = jax.ShapeDtypeStruct((8, group), f32)
    tot, terms, low = group_call(
        scores_kernel,
        (
            rows,
            jax.ShapeDtypeStruct((ysize // 2, 2, 2 * nodes, group), bf16),
            jax.ShapeDtypeStruct((ysize // 2, 2, width, 2 * nodes), bf16),
        ),
        5,
        1,
        "scores",
    )(place, anchors, members, weight_t, counts)
    tots = around(tot, whole, "zl")
    sums = group_call(
        pull_kernel, jax.ShapeDtypeStruct((2, width, group), f32), 2, 0, "pull"
    )(terms, low)
    mask = (jnp.arange(group) // nodes == zl).astype(f32)
    mask = jnp.broadcast_to(mask, (8, group))
    coef = 1.0 / (2.0 * tau * float(total) ** 0.5)
    loss, grad = group_call(
        functools.partial(grads_kernel, coef),
        (rows, jax.ShapeDtypeStruct((width, width), f32)),
        7 + ZL,
        1,
        "grads",
    )(place, anchors, members, weight_t, terms, sums, mask, *tots)
    node_loss = lax.dynamic_slice_in_dim(loss[0], zl * nodes, nodes)
    return node_loss, reduce_all(grad)


def solution(mesh):
    rows, cols = mesh.devices.shape
    fine = Mesh(mesh.devices.reshape(ZL, rows // ZL, cols // 8, 4, 2), ROW + COL)
    every = ROW + COL
    in_specs = (
        P(every, None),
        P(),
        P(every, None, None),
        P(every),
        P(None, every),
        P(),
        P(every, None),
    )
    out_specs = (P(every), P())
    return jax.shard_map(shards, mesh=fine, in_specs=in_specs, out_specs=out_specs, check_vma=False)
```
